32 devices in a mesh: rep: 4 (over y, x), seq: 8 (over z, core).
Axes of the slice: x: 2, y: 2, z: 4, core: 2. Of those that a mesh axis runs over, the one named last changes fastest.
Arguments:
- tokens: bfloat16 [32768, 768], P(('rep', 'seq')), may hold values from -6 to 6
- cotangent: bfloat16 [32768, 768], P(('rep', 'seq')), may hold values from -6 to 6
- doc_lengths: int32 [4, 4], P('rep'), may hold values from 0 to 64, as said below
- doc_owners: int32 [4, 4], P('rep'), may hold values from 0 to 7, as said below
- small_params: float32 [67584], replicated
- slot_block: int32 [224], replicated, may hold values from 0 to 223, as said below
- master_blocks: float32 [224, 256, 256], P('seq')
- left_stats: float32 [224, 256, 256], P('seq')
- right_stats: float32 [224, 256, 256], P('seq')
- left_roots: float32 [224, 256, 256], P('seq')
- right_roots: float32 [224, 256, 256], P('seq')
Outputs:
- hidden_out: bfloat16 [32768, 768], P(('rep', 'seq'))
- input_grad: float32 [32768, 768], P(('rep', 'seq'))
- doc_states: bfloat16 [32, 64, 768], P(('rep', 'seq'))
- block_grads: float32 [224, 256, 256], P('seq')
- left_new: float32 [224, 256, 256], P('seq')
- right_new: float32 [224, 256, 256], P('seq')
- new_blocks: float32 [224, 256, 256], P('seq')
- small_grads: float32 [67584], replicated
- new_small: float32 [67584], replicated
The draws below stay inside these ranges and needn't reach their ends.
Inputs may be any that keep to these rules, and one draw needn't show every extreme that they name: `doc_lengths`: each row lists documents of 16 or 64 segments that tile the group's 64 segments in order, then zeros; row 0 holds a document of 64 segments. `doc_owners`: the entries of a row are distinct. `slot_block`: A permutation; values of 216 or more mark empty slots. Slot t lies on the device of seq index t // 28.
All inputs are finite; a program needn't handle non-finite values.
Results may differ from the reference program's by a relative error of at most 0.014.
Values may be sent and summed in bfloat16 or wider, within the bound.
No kernel may reach another device: no remote copies, remote signals or barrier semaphores. Data moves between devices by JAX's collectives and lax.ppermute only.
A program may use at most 384 MiB of HBM per device.

```python
import jax
import jax.numpy as jnp
import numpy as np
from jax import lax

D = 768
HEAD_DIM = 64
FF = 3072
SEG_LEN = 128
SEG_DEV = 8
DOC_SHORT = 16
DOC_LONG = 64
B = 256
GROUP = 64
TOKENS = 32768
DOCS_MAX = 4
NBLK = 216
SLOTS = 224
NSMALL = 67584
N_REP = 4
N_SEQ = 8


def slot_order(key):
    return jax.random.permutation(key, SLOTS).astype(jnp.int32)


def block_tables():
    grad_first = 0.3 * TOKENS ** 0.5
    grad_second = 0.3 * (TOKENS // SEG_LEN) ** 0.5
    spread_list = []
    grad_list = []
    for layer_idx in range(2):
        grad_level = grad_first if layer_idx == 0 else grad_second
        for n_rows, n_cols, fan_in in ((D, 3 * D, D), (D, D, D // 8), (D, FF, D), (FF, D, FF)):
            amount = n_rows // B * (n_cols // B)
            spread_list += [fan_in ** (-0.5)] * amount
            grad_list += [grad_level] * amount
    spread_list += [D ** (-0.5)] * (SLOTS - NBLK)
    grad_list += [grad_second] * (SLOTS - NBLK)
    return (np.array(spread_list, np.float32), np.array(grad_list, np.float32))


def symmetric_noise(noise_key, factor):
    noise = jax.random.normal(noise_key, (SLOTS, B, B), jnp.float32) * factor
    return 0.5 * (noise + jnp.swapaxes(noise, 1, 2))


def statistic(order, salted):
    first_key, second_key = jax.random.split(salted)
    spread_tab, grad_tab = block_tables()
    grad_level = jnp.take(jnp.asarray(grad_tab), order)[:, None, None]
    square = grad_level * grad_level
    diagonal = B * square * jnp.exp(jax.random.uniform(first_key, (SLOTS, B, 1), jnp.float32, 0.0, np.log(4.0)))
    noise = symmetric_noise(second_key, square * (0.5 * B ** 0.5))
    identity = jnp.eye(B, dtype=jnp.float32)[None]
    return noise * (1.0 - identity) + diagonal * identity


def root_matrix(order, salted):
    first_key, second_key = jax.random.split(salted)
    spread_tab, grad_tab = block_tables()
    grad_level = jnp.take(jnp.asarray(grad_tab), order)[:, None, None]
    base = (B * grad_level * grad_level) ** (-0.25)
    diagonal = base * jnp.exp(jax.random.uniform(first_key, (SLOTS, B, 1), jnp.float32, np.log(0.7), np.log(1.4)))
    noise = symmetric_noise(second_key, base * (0.4 / B ** 0.5))
    identity = jnp.eye(B, dtype=jnp.float32)[None]
    return noise * (1.0 - identity) + diagonal * identity


def draw_slot_block(key, part):
    return slot_order(key)


def draw_master_blocks(key, part):
    order = slot_order(key)
    salted = jax.random.fold_in(key, 11)
    spread_tab, grad_tab = block_tables()
    scale_vec = jnp.take(jnp.asarray(spread_tab), order)
    return jax.random.normal(salted, (SLOTS, B, B), jnp.float32) * scale_vec[:, None, None]


def draw_left_stats(key, part):
    order = slot_order(key)
    return statistic(order, jax.random.fold_in(key, 12))


def draw_right_stats(key, part):
    order = slot_order(key)
    return statistic(order, jax.random.fold_in(key, 13))


def draw_left_roots(key, part):
    order = slot_order(key)
    return root_matrix(order, jax.random.fold_in(key, 14))


def draw_right_roots(key, part):
    order = slot_order(key)
    return root_matrix(order, jax.random.fold_in(key, 15))


def draw_small_params(key, part):
    key = jax.random.fold_in(key, 21)
    layer_kinds = [0] * (3 * D) + [1] * D + [0] * D + [0] * FF + [0] * D + [1] * D + [0] * D
    kinds = np.array(layer_kinds * 2 + [2] * (DOC_LONG * D), np.int32)
    normal_key, flat_key = jax.random.split(key)
    gauss = jax.random.normal(normal_key, (NSMALL,), jnp.float32)
    evenly = jax.random.uniform(flat_key, (NSMALL,), jnp.float32, -1.0, 1.0)
    kind_arr = jnp.asarray(kinds)
    return jnp.where(kind_arr == 1, 1.0 + 0.4 * evenly, jnp.where(kind_arr == 2, 0.5 * gauss, 0.2 * gauss))


def draw_doc_lengths(key, part):
    key = jax.random.fold_in(key, 31)
    group_segs = SEG_DEV * N_SEQ
    most_long = group_segs // DOC_LONG

    def one_row(row_key, is_first):
        count_key, order_key = jax.random.split(row_key)
        n_long = jax.random.randint(count_key, (), 0, most_long + 1)
        n_long = jnp.where(is_first, jnp.maximum(n_long, 1), n_long)
        n_docs = n_long + (group_segs - n_long * DOC_LONG) // DOC_SHORT
        ranking = jax.random.permutation(order_key, DOCS_MAX)
        index_vec = jnp.arange(DOCS_MAX, dtype=jnp.int32)
        used = index_vec < n_docs
        lower = (ranking[None, :] < ranking[:, None]) & used[None, :]
        rank_in = jnp.sum(lower.astype(jnp.int32), axis=1)
        is_long = used & (rank_in < n_long)
        return jnp.where(is_long, DOC_LONG, jnp.where(used, DOC_SHORT, 0)).astype(jnp.int32)
    row_keys = jax.random.split(key, N_REP)
    firsts = jnp.arange(N_REP) == 0
    return jax.vmap(one_row)(row_keys, firsts)


def draw_doc_owners(key, part):
    key = jax.random.fold_in(key, 41)

    def one_row(row_key):
        return jax.random.permutation(row_key, N_SEQ)[:DOCS_MAX].astype(jnp.int32)
    return jax.vmap(one_row)(jax.random.split(key, N_REP))


def shard_levels(key, extent, cuts, low, largest):
    loudness = 1.0
    for dim, blocks in cuts:
        draws = jax.random.uniform(jax.random.fold_in(jax.random.fold_in(key, 6), dim), (blocks,), jnp.float32, low / len(cuts), largest / len(cuts))
        loudness = loudness * jnp.repeat(jnp.exp(draws), extent[dim] // blocks).reshape((-1,) + (1,) * (len(extent) - 1 - dim))
    return loudness


def normal_values(rng, extent, width, limit, cuts=(), kind=jnp.bfloat16):
    result = width * jax.random.normal(rng, extent, jnp.float32)
    if cuts:
        result = result * shard_levels(rng, extent, cuts, -0.22, 0.18)
    return jnp.clip(result, -limit, limit).astype(kind)


def setup_inputs(seed: int = 0) -> dict:
    keys = jax.random.split(jax.random.key(seed), 12)
    tokens = normal_values(keys[0], (TOKENS, D), 1.0, 6.0, ((0, 32),))
    cotangent = normal_values(keys[1], (TOKENS, D), 1.0, 6.0, ((0, 32),))
    doc_lengths = draw_doc_lengths(jax.random.fold_in(keys[11], 71), 0)
    doc_owners = draw_doc_owners(jax.random.fold_in(keys[11], 71), 0)
    small_params = draw_small_params(jax.random.fold_in(keys[11], 71), 0)
    slot_block = draw_slot_block(jax.random.fold_in(keys[11], 71), 0)
    master_blocks = draw_master_blocks(jax.random.fold_in(keys[11], 71), 0)
    left_stats = draw_left_stats(jax.random.fold_in(keys[11], 71), 0)
    right_stats = draw_right_stats(jax.random.fold_in(keys[11], 71), 0)
    left_roots = draw_left_roots(jax.random.fold_in(keys[11], 71), 0)
    right_roots = draw_right_roots(jax.random.fold_in(keys[11], 71), 0)
    return {"tokens": tokens, "cotangent": cotangent, "doc_lengths": doc_lengths, "doc_owners": doc_owners, "small_params": small_params, "slot_block": slot_block, "master_blocks": master_blocks, "left_stats": left_stats, "right_stats": right_stats, "left_roots": left_roots, "right_roots": right_roots}


@jax.custom_vjp
def low(v):
    return lax.optimization_barrier(v.astype(jnp.bfloat16)).astype(jnp.float32)

@jax.custom_vjp
def low_back(v):
    return v

def low_keep(v):
    return (low(v), None)

def low_pass(kept, grad):
    return (grad,)

def back_keep(v):
    return (v, None)

def back_low(kept, grad):
    return (low(grad),)
low.defvjp(low_keep, low_pass)
low_back.defvjp(back_keep, back_low)
HIGHEST_PREC = lax.Precision.HIGHEST
NORM_EPS = 1e-05
RMS_EPS = 1e-06
DECAY = 0.5
BLOCK_RATE = 0.02
SMALL_RATE = 0.1
MASKED_SCORE = -1000000000.0

def layer_norm(values, gain_vec, shift_vec):
    center = values - lax.optimization_barrier(jnp.mean(values, axis=-1, keepdims=True))
    spread = lax.optimization_barrier(jnp.mean(center * center, axis=-1, keepdims=True))
    return center * lax.rsqrt(spread + NORM_EPS) * gain_vec + shift_vec

def ref_block(block_in, key_valid, weights, params):
    w_qkv, w_out, w_up, w_down = weights
    bias_q, bias_v, bias_out, gain_one, shift_one, bias_up, bias_down, gain_two, shift_two = params
    n_group, n_rows, feat_dim = block_in.shape
    head_count = feat_dim // HEAD_DIM
    rounded_in = low(block_in)
    bias_qkv = jnp.concatenate([bias_q, jnp.zeros_like(bias_q), bias_v])
    qkv_rows = jnp.einsum('gld,de->gle', rounded_in, w_qkv, precision=HIGHEST_PREC) + bias_qkv
    qkv_rows = low(low_back(qkv_rows))
    shaped = qkv_rows.reshape(n_group, n_rows, 3, head_count, HEAD_DIM)
    query_part, key_part, value_part = (shaped[:, :, 0], shaped[:, :, 1], shaped[:, :, 2])
    raw_scores = low_back(jnp.einsum('gqhe,gkhe->ghqk', query_part, key_part, precision=HIGHEST_PREC))
    scores = raw_scores * HEAD_DIM ** (-0.5) + jnp.where(key_valid, 0.0, MASKED_SCORE)[:, None, None, :]
    attn_probs = low(jax.nn.softmax(scores, axis=-1))
    mixed_rows = jnp.einsum('ghqk,gkhe->gqhe', attn_probs, value_part, precision=HIGHEST_PREC)
    mixed_rows = low(low_back(mixed_rows.reshape(n_group, n_rows, feat_dim)))
    attn_out = low_back(jnp.einsum('gld,de->gle', mixed_rows, w_out, precision=HIGHEST_PREC) + bias_out)
    hidden = layer_norm(block_in + attn_out, gain_one, shift_one)
    up_proj = low_back(jnp.einsum('gld,df->glf', low(hidden), w_up, precision=HIGHEST_PREC) + bias_up)
    active = low(jax.nn.gelu(up_proj, approximate=False))
    down_proj = low_back(jnp.einsum('glf,fd->gld', active, w_down, precision=HIGHEST_PREC) + bias_down)
    return layer_norm(hidden + down_proj, gain_two, shift_two)

def layer_shapes():
    return ((D, 3 * D), (D, D), (D, FF), (FF, D))

def split_blocks(matrix):
    n_rows, n_cols = matrix.shape
    return matrix.reshape(n_rows // B, B, n_cols // B, B).transpose(0, 2, 1, 3).reshape(-1, B, B)

def join_all(blocks):
    mats = []
    offset = 0
    for layer_idx in range(2):
        for n_rows, n_cols in layer_shapes():
            amount = n_rows // B * (n_cols // B)
            piece = blocks[offset:offset + amount].reshape(n_rows // B, n_cols // B, B, B)
            mats.append(piece.transpose(0, 2, 1, 3).reshape(n_rows, n_cols))
            offset += amount
    return tuple(mats)

def unpack_small(small_vec):
    lengths_list = (D, D, D, D, D, FF, D, D, D)
    per_layer = 8 * D + FF
    layers = []
    for layer_idx in range(2):
        offset = layer_idx * per_layer
        parts = []
        for length in lengths_list:
            parts.append(small_vec[offset:offset + length])
            offset += length
        layers.append(tuple(parts))
    position = small_vec[2 * per_layer:].reshape(DOC_LONG, D)
    return (layers[0], layers[1], position)

def shampoo_step(grad_blocks, left_old, right_old, left_root, right_root, master_old):
    left_out = DECAY * left_old + (1.0 - DECAY) * jnp.einsum('bij,bkj->bik', grad_blocks, grad_blocks, precision=HIGHEST_PREC)
    right_out = DECAY * right_old + (1.0 - DECAY) * jnp.einsum('bji,bjk->bik', grad_blocks, grad_blocks, precision=HIGHEST_PREC)
    partial_dir = jnp.einsum('bij,bjk->bik', left_root, grad_blocks, precision=HIGHEST_PREC)
    direction = jnp.einsum('bij,bjk->bik', partial_dir, right_root, precision=HIGHEST_PREC)
    norm_scale = lax.rsqrt(lax.optimization_barrier(jnp.mean(direction * direction, axis=(1, 2), keepdims=True)) + RMS_EPS)
    return (left_out, right_out, master_old - BLOCK_RATE * direction * norm_scale)

def small_step(old_values, grads, split_at):
    head_grad = grads[:split_at]
    tail_grad = grads[split_at:]
    head_new = old_values[:split_at] - SMALL_RATE * head_grad * lax.rsqrt(jnp.mean(head_grad * head_grad) + RMS_EPS)
    tail_new = old_values[split_at:] - SMALL_RATE * tail_grad * lax.rsqrt(jnp.mean(tail_grad * tail_grad) + RMS_EPS)
    return jnp.concatenate([head_new, tail_new])

def forward(tokens_in, mats_flat, small_vec, doc_lengths, doc_owners):
    rounded = tuple((low(matrix) for matrix in mats_flat))
    first_w = rounded[:4]
    second_w = rounded[4:]
    first_p, second_p, position = unpack_small(small_vec)
    seg_valid = jnp.ones((DOC_SHORT, SEG_LEN), dtype=bool)

    def layer_one(block_rows):
        return ref_block(block_rows, seg_valid, first_w, first_p)
    spans = tokens_in.reshape(-1, DOC_SHORT, SEG_LEN, D)
    out_one = lax.map(jax.checkpoint(layer_one), spans).reshape(N_REP, GROUP, SEG_LEN, D)
    cls_rows = low(low_back(out_one[:, :, 0, :]))

    def one_doc(cls_group, start_row, doc_len):
        extended = jnp.concatenate([cls_group, jnp.zeros((DOC_LONG, D), jnp.float32)], axis=0)
        window = lax.dynamic_slice_in_dim(extended, start_row, DOC_LONG, 0)
        row_valid = jnp.arange(DOC_LONG) < doc_len
        doc_res = ref_block((window + position)[None], row_valid[None], second_w, second_p)[0]
        return low(doc_res) * row_valid[:, None].astype(jnp.float32)
    doc_fn = jax.checkpoint(one_doc)

    def place(extended, doc_item):
        doc_rows, start_row = doc_item
        current = lax.dynamic_slice_in_dim(extended, start_row, DOC_LONG, 0)
        return (lax.dynamic_update_slice_in_dim(extended, current + doc_rows, start_row, 0), None)
    new_cls = []
    states = []
    for group_idx in range(N_REP):
        lengths_row = doc_lengths[group_idx].astype(jnp.int32)
        starts_row = (jnp.cumsum(lengths_row) - lengths_row).astype(jnp.int32)
        cls_group = cls_rows[group_idx]
        doc_res = lax.map(lambda doc_item: doc_fn(cls_group, doc_item[0], doc_item[1]), (starts_row, lengths_row))
        placed, unused = lax.scan(place, jnp.zeros((GROUP + DOC_LONG, D), jnp.float32), (doc_res, starts_row))
        new_cls.append(placed[:GROUP])
        owner_hot = (doc_owners[group_idx][:, None] == jnp.arange(N_SEQ, dtype=jnp.int32)[None, :]).astype(jnp.float32)
        states.append(jnp.einsum('io,ild->old', owner_hot, doc_res, precision=HIGHEST_PREC))
    final_rows = out_one.at[:, :, 0, :].set(jnp.stack(new_cls))
    return (final_rows, jnp.stack(states))

def reference(tokens, cotangent, doc_lengths, doc_owners, small_params, slot_block, master_blocks, left_stats, right_stats, left_roots, right_roots):
    tokens_in = tokens.astype(jnp.float32).reshape(N_REP, GROUP, SEG_LEN, D)
    cot_in = cotangent.astype(jnp.float32).reshape(N_REP, GROUP, SEG_LEN, D)
    matches = slot_block[None, :] == jnp.arange(NBLK, dtype=jnp.int32)[:, None]
    slot_of = lax.optimization_barrier(jnp.sum(jnp.where(matches, jnp.arange(SLOTS, dtype=jnp.int32)[None, :], 0), axis=1)).astype(jnp.int32)
    mats_flat = join_all(jnp.take(master_blocks, slot_of, axis=0))

    def loss_of(inputs_f, mats_f, small_f):
        final_rows, doc_out = forward(inputs_f, mats_f, small_f, doc_lengths, doc_owners)
        return (jnp.sum(final_rows * cot_in), (final_rows, doc_out))
    loss_value, pull_back, aux_out = jax.vjp(loss_of, tokens_in, mats_flat, small_params, has_aux=True)
    final_rows, doc_out = aux_out
    grad_tokens, grad_mats, grad_small = pull_back(jnp.ones((), jnp.float32))
    blocks_grad = jnp.concatenate([split_blocks(matrix) for matrix in grad_mats], axis=0)
    padded = jnp.concatenate([blocks_grad, jnp.zeros((SLOTS - NBLK, B, B), jnp.float32)], axis=0)
    block_grads = jnp.take(padded, slot_block, axis=0)
    left_out, right_out, new_blocks = shampoo_step(block_grads, left_stats, right_stats, left_roots, right_roots, master_blocks)
    new_small = small_step(small_params, grad_small, 2 * (8 * D + FF))
    return (final_rows.reshape(TOKENS, D).astype(jnp.bfloat16), grad_tokens.reshape(TOKENS, D), doc_out.reshape(N_REP * N_SEQ, DOC_LONG, D).astype(jnp.bfloat16), block_grads, left_out, right_out, new_blocks, grad_small, new_small)
```

```python
import functools

import jax
import jax.numpy as jnp
import numpy as np
from jax import lax
from jax.experimental import pallas as pl
from jax.experimental.pallas import tpu as pltpu
from jax.sharding import PartitionSpec as P

D = 768
HEAD_DIM = 64
FF = 3072
SEG_LEN = 128
DOC_LONG = 64
B = 256
PER_LAYER = 108
NBLK = 2 * PER_LAYER
NPAR = 8 * D + FF
NPAIR = D // 128

NORM_EPS = 1e-05
RMS_EPS = 1e-06
DECAY = 0.5
BLOCK_RATE = 0.02
SMALL_RATE = 0.1
MASKED_SCORE = -1000000000.0
SCALE = HEAD_DIM**-0.5

C_QKV, C_OUT, C_UP, C_DOWN, W_COLS = 0, 3 * D, 4 * D, 4 * D + FF, 4 * D + 2 * FF
W_SPANS = ((C_QKV, C_OUT), (C_OUT, C_UP), (C_UP, C_DOWN), (C_DOWN, W_COLS))
L_X, L_A, L_H, L_E, L_ROWS = 0, D, 2 * D, 3 * D, 3 * D + FF
R_QKV, R_OUT, R_UP, R_DOWN, R_COLS = 0, 3 * D, 4 * D, 4 * D + FF, 5 * D + FF
O_BQ, O_BV, O_BO, O_G1, O_C1, O_B1 = 0, D, 2 * D, 3 * D, 4 * D, 5 * D
O_B2, O_G2, O_C2 = 5 * D + FF, 6 * D + FF, 7 * D + FF

VMEM_LIMIT = 60 * 1024 * 1024
BF = jnp.bfloat16
F32 = jnp.float32


def block_tables():
    w_i, w_j, l_i, r_j = [], [], [], []
    for i in range(3):
        for j in range(9):
            w_i.append(i), w_j.append(j), l_i.append(i), r_j.append(j)
    for i in range(3):
        for j in range(3):
            w_i.append(i), w_j.append(9 + j), l_i.append(3 + i), r_j.append(9 + j)
    for i in range(3):
        for j in range(12):
            w_i.append(i), w_j.append(12 + j), l_i.append(6 + i), r_j.append(12 + j)
    for i in range(12):
        for j in range(3):
            w_i.append(i % 3), w_j.append(24 + 3 * (i // 3) + j)
            l_i.append(9 + i), r_j.append(24 + j)
    return [np.array(t, np.int32) for t in (w_i, w_j, l_i, r_j)]


W_I, W_J, L_I, R_J = block_tables()


def mm(a, b):
    return jnp.dot(a, b, preferred_element_type=F32)


def mm_t(a, b):
    return lax.dot_general(a, b, (((1,), (1,)), ((), ())), preferred_element_type=F32)


def tmm(a, b):
    return lax.dot_general(a, b, (((0,), (0,)), ((), ())), preferred_element_type=F32)


def norm_parts(values):
    center = values - jnp.mean(values, axis=-1, keepdims=True)
    spread = jnp.mean(center * center, axis=-1, keepdims=True)
    scale = lax.rsqrt(spread + NORM_EPS)
    return center * scale, scale


def gelu_parts(u):
    density = jnp.exp(-0.5 * u * u)
    denom = 1.0 + (0.3275911 * 0.7071067811865476) * jnp.abs(u)
    t = pl.reciprocal(denom, approx=True)
    t = t * (2.0 - denom * t)
    poly = t * (
        0.127414796
        + t * (-0.142248368 + t * (0.7107068705 + t * (-0.7265760135 + t * 0.5307027145)))
    )
    tail = poly * density
    cdf = jnp.where(u >= 0, 1.0 - tail, tail)
    return u * cdf, cdf + u * density * 0.3989422804014327


def head_masks():
    lane = lax.broadcasted_iota(jnp.int32, (1, 128), 1)
    first = jnp.where(lane < HEAD_DIM, 1.0, 0.0).astype(BF)
    return first, (1.0 - first.astype(F32)).astype(BF)


def stack_heads(pair, masks):
    return jnp.concatenate([pair * masks[0], pair * masks[1]], axis=0)


def beside(stacked):
    half = stacked.shape[0] // 2
    return jnp.concatenate([stacked[:half], stacked[half:]], axis=1)


def load_weights(first_block, tables, entry_block, bufs, w_ref, sems):
    w_i, w_j = tables
    offset = 0
    for buf in bufs:
        count = buf.shape[0]

        def body(e, carry, buf=buf, offset=offset):
            n = entry_block[offset + e] - first_block

            @pl.when((n >= 0) & (n < PER_LAYER))
            def _():
                row = pl.multiple_of(w_i[n] * B, B)
                col = pl.multiple_of(w_j[n] * B, B)
                mat = (
                    (n >= 27).astype(jnp.int32)
                    + (n >= 36).astype(jnp.int32)
                    + (n >= 72).astype(jnp.int32)
                )
                pltpu.make_async_copy(
                    buf.at[e], w_ref.at[pl.ds(row, B), pl.ds(col, B)], sems.at[mat]
                ).start()

            return carry

        lax.fori_loop(0, count, body, 0)
        offset += count


def wait_weights(w_ref, sems, mat):
    lo, hi = W_SPANS[mat]
    part = w_ref.at[:, lo:hi]
    pltpu.make_async_copy(part, part, sems.at[mat]).wait()


def fwd_tile(x32, xb, w, par, key_bias, qkv_ref, p_ref, r1_ref, r2_ref, gp_ref, lt_ref, a_ref, wait):
    n_rows = xb.shape[0]
    lt_ref[L_X : L_X + D, :] = xb.T
    wait(0)
    for c, off in ((0, O_BQ), (1, None), (2, O_BV)):
        part = mm(xb, w[:, C_QKV + c * D : C_QKV + (c + 1) * D])
        if off is not None:
            part = part + par[:, off : off + D]
        qkv_ref[:, c * D : (c + 1) * D] = part.astype(BF)
    masks = head_masks()
    for s in range(n_rows // SEG_LEN):
        rows = slice(s * SEG_LEN, (s + 1) * SEG_LEN)
        for h in range(NPAIR):
            q = qkv_ref[rows, h * 128 : (h + 1) * 128]
            k = qkv_ref[rows, D + h * 128 : D + (h + 1) * 128]
            v = qkv_ref[rows, 2 * D + h * 128 : 2 * D + (h + 1) * 128]
            scores = mm_t(stack_heads(q, masks), k) * SCALE
            if key_bias is not None:
                scores = scores + key_bias
            exps = jnp.exp(scores - jnp.max(scores, axis=-1, keepdims=True))
            probs = exps * (1.0 / jnp.sum(exps, axis=-1, keepdims=True))
            probs = beside(probs.astype(BF))
            p_ref[rows, h * 256 : (h + 1) * 256] = probs
            a_ref[rows, h * 128 : (h + 1) * 128] = mm(probs, stack_heads(v, masks)).astype(BF)
    a = a_ref[...]
    lt_ref[L_A : L_A + D, :] = a.T
    wait(1)
    r1 = x32 + (mm(a, w[:, C_OUT : C_OUT + D]) + par[:, O_BO : O_BO + D])
    r1_ref[...] = r1
    xhat, unused = norm_parts(r1)
    h = xhat * par[:, O_G1 : O_G1 + D] + par[:, O_C1 : O_C1 + D]
    hb = h.astype(BF)
    lt_ref[L_H : L_H + D, :] = hb.T
    wait(2)
    total = h + par[:, O_B2 : O_B2 + D]
    for c in range(FF // D):
        u = mm(hb, w[:, C_UP + c * D : C_UP + (c + 1) * D]) + par[:, O_B1 + c * D : O_B1 + (c + 1) * D]
        e, gp = gelu_parts(u)
        gp_ref[:, c * D : (c + 1) * D] = gp.astype(BF)
        eb = e.astype(BF)
        lt_ref[L_E + c * D : L_E + (c + 1) * D, :] = eb.T
        if c == 0:
            wait(3)
        total = total + mm(eb, w[:, C_DOWN + c * D : C_DOWN + (c + 1) * D])
    r2_ref[...] = total
    xhat, unused = norm_parts(total)
    return xhat * par[:, O_G2 : O_G2 + D] + par[:, O_C2 : O_C2 + D]


def col_sum(values):
    return jnp.sum(values.astype(F32), axis=0, keepdims=True)


def norm_back(dout, values, gain):
    xhat, scale = norm_parts(values)
    dxhat = dout * gain
    mean_one = jnp.mean(dxhat, axis=-1, keepdims=True)
    mean_two = jnp.mean(dxhat * xhat, axis=-1, keepdims=True)
    return scale * (dxhat - mean_one - xhat * mean_two), col_sum(dout * xhat), col_sum(dout)


def bwd_tile(dout, w, par, qkv_ref, p_ref, r1_ref, r2_ref, gp_ref, r_ref, pg_ref, da_ref, wait):
    n_rows = dout.shape[0]

    def add_small(off, value):
        pg_ref[:, off : off + value.shape[1]] += value

    dr2, dgain, dshift = norm_back(dout, r2_ref[...], par[:, O_G2 : O_G2 + D])
    add_small(O_G2, dgain)
    add_small(O_C2, dshift)
    dy = dr2.astype(BF)
    r_ref[:, R_DOWN : R_DOWN + D] = dy
    add_small(O_B2, col_sum(dy))
    wait(3)
    dh = dr2
    for c in range(FF // D):
        de = mm_t(dy, w[:, C_DOWN + c * D : C_DOWN + (c + 1) * D])
        du = (gp_ref[:, c * D : (c + 1) * D].astype(F32) * de).astype(BF)
        r_ref[:, R_UP + c * D : R_UP + (c + 1) * D] = du
        add_small(O_B1 + c * D, col_sum(du))
        if c == 0:
            wait(2)
        dh = dh + mm_t(du, w[:, C_UP + c * D : C_UP + (c + 1) * D])
    dr1, dgain, dshift = norm_back(dh, r1_ref[...], par[:, O_G1 : O_G1 + D])
    add_small(O_G1, dgain)
    add_small(O_C1, dshift)
    do = dr1.astype(BF)
    r_ref[:, R_OUT : R_OUT + D] = do
    add_small(O_BO, col_sum(do))
    wait(1)
    da_ref[...] = mm_t(do, w[:, C_OUT : C_OUT + D]).astype(BF)
    masks = head_masks()
    for s in range(n_rows // SEG_LEN):
        rows = slice(s * SEG_LEN, (s + 1) * SEG_LEN)
        for h in range(NPAIR):
            q = qkv_ref[rows, h * 128 : (h + 1) * 128]
            k = qkv_ref[rows, D + h * 128 : D + (h + 1) * 128]
            v = qkv_ref[rows, 2 * D + h * 128 : 2 * D + (h + 1) * 128]
            probs = jnp.concatenate(
                [p_ref[rows, h * 256 : h * 256 + 128], p_ref[rows, h * 256 + 128 : h * 256 + 256]], axis=0
            )
            da = stack_heads(da_ref[rows, h * 128 : (h + 1) * 128], masks)
            dprobs = mm_t(da, v)
            dv = tmm(probs, da)
            probs = probs.astype(F32)
            inner = jnp.sum(dprobs * probs, axis=-1, keepdims=True)
            dscores = (probs * (dprobs - inner) * SCALE).astype(BF)
            dq = mm(beside(dscores), stack_heads(k, masks))
            dk = tmm(dscores, stack_heads(q, masks))
            r_ref[rows, h * 128 : (h + 1) * 128] = dq.astype(BF)
            r_ref[rows, D + h * 128 : D + (h + 1) * 128] = dk.astype(BF)
            r_ref[rows, 2 * D + h * 128 : 2 * D + (h + 1) * 128] = dv.astype(BF)
    add_small(O_BQ, col_sum(r_ref[:, 0:D]))
    add_small(O_BV, col_sum(r_ref[:, 2 * D : 3 * D]))
    wait(0)
    return dr1 + mm_t(r_ref[:, R_QKV : R_QKV + 3 * D], w[:, C_QKV : C_QKV + 3 * D])


TILE = 256


def first_fwd_kernel(nbuf, w_i, w_j, entry, x_ref, par, *rest):
    bufs = rest[:nbuf]
    out_ref, cls_ref, qkv_ref, p_ref, r1_ref, r2_ref, gp_ref, lt_ref, w, a_ref, sems = rest[nbuf:]
    first = pl.program_id(0) == 0

    @pl.when(first)
    def _():
        load_weights(0, (w_i, w_j), entry, bufs, w, sems)

    def wait(mat):
        @pl.when(first)
        def _():
            wait_weights(w, sems, mat)

    xb = x_ref[...]
    out = fwd_tile(
        xb.astype(F32), xb, w, par, None, qkv_ref, p_ref, r1_ref, r2_ref, gp_ref, lt_ref, a_ref, wait
    ).astype(BF)
    out_ref[...] = out
    for s in range(TILE // SEG_LEN):
        cls_ref[0, s : s + 1, :] = out[s * SEG_LEN : s * SEG_LEN + 1, :]


def any_spec():
    return pl.BlockSpec(memory_space=pl.ANY)


def row_spec(width, tile=TILE):
    return pl.BlockSpec((tile, width), lambda i, *_: (i, 0))


def whole_spec(shape):
    return pl.BlockSpec(shape, lambda i, *_: (0,) * len(shape))


def first_fwd(entry, bufs, tokens, par):
    rows = tokens.shape[0]
    steps = rows // TILE
    nseg = TILE // SEG_LEN
    return pl.pallas_call(
        functools.partial(first_fwd_kernel, len(bufs)),
        grid_spec=pltpu.PrefetchScalarGridSpec(
            num_scalar_prefetch=3,
            grid=(steps,),
            in_specs=[row_spec(D), whole_spec((1, NPAR))] + [any_spec()] * len(bufs),
            out_specs=[
                row_spec(D),
                pl.BlockSpec((1, nseg, D), lambda i, *_: (i, 0, 0)),
                row_spec(3 * D),
                row_spec(NPAIR * 256),
                row_spec(D),
                row_spec(D),
                row_spec(FF),
                pl.BlockSpec((L_ROWS, TILE), lambda i, *_: (0, i)),
            ],
            scratch_shapes=[
                pltpu.VMEM((D, W_COLS), BF),
                pltpu.VMEM((TILE, D), BF),
                pltpu.SemaphoreType.DMA((4,)),
            ],
        ),
        out_shape=[
            jax.ShapeDtypeStruct((rows, D), BF),
            jax.ShapeDtypeStruct((steps, nseg, D), BF),
            jax.ShapeDtypeStruct((rows, 3 * D), BF),
            jax.ShapeDtypeStruct((rows, NPAIR * 256), BF),
            jax.ShapeDtypeStruct((rows, D), F32),
            jax.ShapeDtypeStruct((rows, D), F32),
            jax.ShapeDtypeStruct((rows, FF), BF),
            jax.ShapeDtypeStruct((L_ROWS, rows), BF),
        ],
        compiler_params=pltpu.CompilerParams(vmem_limit_bytes=VMEM_LIMIT),
        cost_estimate=pl.CostEstimate(flops=15_000_000_000, bytes_accessed=60_000_000, transcendentals=4_000_000),
        name="first_forward",
    )(jnp.asarray(W_I), jnp.asarray(W_J), entry, tokens, par, *bufs)


def first_bwd_kernel(nbuf, w_i, w_j, entry, cot_ref, dcls_ref, par, qkv_ref, p_ref, r1_ref, r2_ref, gp_ref, *rest):
    bufs = rest[:nbuf]
    r_ref, dx_ref, pg_ref, w, da_ref, sems = rest[nbuf:]
    first = pl.program_id(0) == 0

    @pl.when(first)
    def _():
        load_weights(0, (w_i, w_j), entry, bufs, w, sems)
        pg_ref[...] = jnp.zeros_like(pg_ref)

    def wait(mat):
        @pl.when(first)
        def _():
            wait_weights(w, sems, mat)

    dout = cot_ref[...].astype(F32)
    index = lax.broadcasted_iota(jnp.int32, (TILE, 1), 0)
    for s in range(TILE // SEG_LEN):
        dout = jnp.where(index == s * SEG_LEN, dcls_ref[0, s : s + 1, :], dout)
    dx_ref[...] = bwd_tile(
        dout, w, par, qkv_ref, p_ref, r1_ref, r2_ref, gp_ref, r_ref, pg_ref, da_ref, wait
    )


def first_bwd(entry, bufs, cot, dcls, par, kept):
    rows = cot.shape[0]
    steps = rows // TILE
    nseg = TILE // SEG_LEN
    qkv, probs, r1, r2, gp = kept
    return pl.pallas_call(
        functools.partial(first_bwd_kernel, len(bufs)),
        grid_spec=pltpu.PrefetchScalarGridSpec(
            num_scalar_prefetch=3,
            grid=(steps,),
            in_specs=[
                row_spec(D),
                pl.BlockSpec((1, nseg, D), lambda i, *_: (i, 0, 0)),
                whole_spec((1, NPAR)),
                row_spec(3 * D),
                row_spec(NPAIR * 256),
                row_spec(D),
                row_spec(D),
                row_spec(FF),
            ]
            + [any_spec()] * len(bufs),
            out_specs=[row_spec(R_COLS), row_spec(D), whole_spec((1, NPAR))],
            scratch_shapes=[
                pltpu.VMEM((D, W_COLS), BF),
                pltpu.VMEM((TILE, D), BF),
                pltpu.SemaphoreType.DMA((4,)),
            ],
        ),
        out_shape=[
            jax.ShapeDtypeStruct((rows, R_COLS), BF),
            jax.ShapeDtypeStruct((rows, D), F32),
            jax.ShapeDtypeStruct((1, NPAR), F32),
        ],
        compiler_params=pltpu.CompilerParams(vmem_limit_bytes=VMEM_LIMIT),
        cost_estimate=pl.CostEstimate(flops=16_000_000_000, bytes_accessed=60_000_000, transcendentals=0),
        name="first_backward",
    )(jnp.asarray(W_I), jnp.asarray(W_J), entry, cot, dcls.reshape(steps, nseg, D), par, qkv, probs, r1, r2, gp, *bufs)


def second_kernel(nbuf, w_i, w_j, entry, x_ref, dout_ref, bias_ref, par, *rest):
    bufs = rest[:nbuf]
    out_ref, lt_ref, r_ref, dx_ref, pg_ref = rest[nbuf : nbuf + 5]
    w, a_ref, qkv_ref, p_ref, r1_ref, r2_ref, gp_ref, sems = rest[nbuf + 5 :]
    load_weights(PER_LAYER, (w_i, w_j), entry, bufs, w, sems)
    pg_ref[...] = jnp.zeros_like(pg_ref)
    x32 = x_ref[...]
    out = fwd_tile(
        x32,
        x32.astype(BF),
        w,
        par,
        bias_ref[...],
        qkv_ref,
        p_ref,
        r1_ref,
        r2_ref,
        gp_ref,
        lt_ref,
        a_ref,
        lambda mat: wait_weights(w, sems, mat),
    )
    out_ref[...] = out.astype(BF)
    dx_ref[...] = bwd_tile(
        dout_ref[...],
        w,
        par,
        qkv_ref,
        p_ref,
        r1_ref,
        r2_ref,
        gp_ref,
        r_ref,
        pg_ref,
        a_ref,
        lambda mat: None,
    )


def second_layer(entry, bufs, doc_in, dout, key_bias, par):
    rows = SEG_LEN
    vmem = pl.BlockSpec(memory_space=pltpu.VMEM)
    smem = pl.BlockSpec(memory_space=pltpu.SMEM)
    return pl.pallas_call(
        functools.partial(second_kernel, len(bufs)),
        in_specs=[smem] * 3 + [vmem] * 4 + [any_spec()] * len(bufs),
        out_specs=[vmem] * 5,
        scratch_shapes=[
            pltpu.VMEM((D, W_COLS), BF),
            pltpu.VMEM((rows, D), BF),
            pltpu.VMEM((rows, 3 * D), BF),
            pltpu.VMEM((rows, NPAIR * 256), BF),
            pltpu.VMEM((rows, D), F32),
            pltpu.VMEM((rows, D), F32),
            pltpu.VMEM((rows, FF), BF),
            pltpu.SemaphoreType.DMA((4,)),
        ],
        out_shape=[
            jax.ShapeDtypeStruct((rows, D), BF),
            jax.ShapeDtypeStruct((L_ROWS, rows), BF),
            jax.ShapeDtypeStruct((rows, R_COLS), BF),
            jax.ShapeDtypeStruct((rows, D), F32),
            jax.ShapeDtypeStruct((1, NPAR), F32),
        ],
        compiler_params=pltpu.CompilerParams(vmem_limit_bytes=VMEM_LIMIT),
        cost_estimate=pl.CostEstimate(flops=8_000_000_000, bytes_accessed=40_000_000, transcendentals=1_000_000),
        name="second_layer",
    )(jnp.asarray(W_I), jnp.asarray(W_J), entry, doc_in, dout, key_bias, par, *bufs)


WG_UNROLL = 4


def weight_grad_kernel(l_i, r_j, tab, lt1, r1, lt2, r2, out_ref, lt1_s, r1_s, lt2_s, r2_s, sems):
    step = pl.program_id(0)

    @pl.when(step == 0)
    def _():
        copies = [
            pltpu.make_async_copy(src, dst, sems.at[i])
            for i, (src, dst) in enumerate(((lt1, lt1_s), (r1, r1_s), (lt2, lt2_s), (r2, r2_s)))
        ]
        for copy in copies:
            copy.start()
        for copy in copies:
            copy.wait()

    for u in range(WG_UNROLL):
        n = tab[step * WG_UNROLL + u]
        local = jnp.where(n >= PER_LAYER, n - PER_LAYER, n)
        local = jnp.where(n >= NBLK, 0, local)
        row = pl.multiple_of(l_i[local] * B, B)
        col = pl.multiple_of(r_j[local] * B, B)

        @pl.when(n < PER_LAYER)
        def _():
            out_ref[u] = mm(lt1_s[pl.ds(row, B), :], r1_s[:, pl.ds(col, B)]).astype(BF)

        @pl.when((n >= PER_LAYER) & (n < NBLK))
        def _():
            out_ref[u] = mm(lt2_s[pl.ds(row, B), :], r2_s[:, pl.ds(col, B)]).astype(BF)

        @pl.when(n >= NBLK)
        def _():
            out_ref[u] = jnp.zeros((B, B), BF)


def weight_grad(tab, lt1, r1, lt2, r2):
    count = tab.shape[0]
    return pl.pallas_call(
        weight_grad_kernel,
        grid_spec=pltpu.PrefetchScalarGridSpec(
            num_scalar_prefetch=3,
            grid=(count // WG_UNROLL,),
            in_specs=[any_spec()] * 4,
            out_specs=pl.BlockSpec((WG_UNROLL, B, B), lambda i, *_: (i, 0, 0)),
            scratch_shapes=[pltpu.VMEM(a.shape, BF) for a in (lt1, r1, lt2, r2)]
            + [pltpu.SemaphoreType.DMA((4,))],
        ),
        out_shape=jax.ShapeDtypeStruct((count, B, B), BF),
        compiler_params=pltpu.CompilerParams(vmem_limit_bytes=VMEM_LIMIT),
        cost_estimate=pl.CostEstimate(
            flops=count * 100_000_000, bytes_accessed=28_000_000 + count * 131072, transcendentals=0
        ),
        name="weight_gradients",
    )(jnp.asarray(L_I), jnp.asarray(R_J), tab, lt1, r1, lt2, r2)


def shampoo_kernel(n_piece, bounds, place, *rest):
    pieces = rest[:n_piece]
    left, right, lroot, rroot, master = rest[n_piece : n_piece + 5]
    grad_out, left_out, right_out, new_out, g_ref = rest[-5:]
    for i, (piece, size) in enumerate(zip(pieces, bounds)):
        g_ref[pl.ds(pl.multiple_of(place[i], 32), size), :] = piece[0]
    g = g_ref[...]
    grad_out[0] = g.astype(F32)
    left_out[0] = DECAY * left[0] + (1.0 - DECAY) * mm_t(g, g)
    right_out[0] = DECAY * right[0] + (1.0 - DECAY) * tmm(g, g)
    part = mm(lroot[0].astype(BF), g)
    direction = mm(part.astype(BF), rroot[0].astype(BF))
    scale = lax.rsqrt(jnp.mean(direction * direction) + RMS_EPS)
    new_out[0] = master[0] - BLOCK_RATE * direction * scale


def shampoo(first, place, pieces, stats, previous):
    count = pieces[0].shape[0]
    total = stats[0].shape[0]
    bounds = tuple(p.shape[1] for p in pieces)
    chunk_spec = pl.BlockSpec((1, B, B), lambda i, *_: (i + first, 0, 0))
    n_in = 1 + len(pieces) + len(stats)
    return pl.pallas_call(
        functools.partial(shampoo_kernel, len(pieces), bounds),
        grid_spec=pltpu.PrefetchScalarGridSpec(
            num_scalar_prefetch=1,
            grid=(count,),
            in_specs=[pl.BlockSpec((1, size, B), lambda i, *_: (i, 0, 0)) for size in bounds]
            + [chunk_spec] * len(stats)
            + [any_spec()] * len(previous),
            out_specs=[chunk_spec] * 4,
            scratch_shapes=[pltpu.VMEM((B, B), BF)],
        ),
        out_shape=[jax.ShapeDtypeStruct((total, B, B), F32)] * 4,
        input_output_aliases={n_in + i: i for i in range(len(previous))},
        compiler_params=pltpu.CompilerParams(vmem_limit_bytes=VMEM_LIMIT),
        cost_estimate=pl.CostEstimate(
            flops=count * 134_000_000, bytes_accessed=count * 2_400_000, transcendentals=0
        ),
        name="shampoo",
    )(place, *pieces, *stats, *previous)


def swap(value, axis, bit):
    size = lax.axis_size(axis)
    return lax.ppermute(value, axis, [(i, i ^ bit) for i in range(size)])


def bits_of(size):
    return [1 << i for i in range(size.bit_length() - 1)]


def rep_bits(n_rep):
    bits = bits_of(n_rep)
    return bits, bits[::-1]


def gather_weights(master, my_rep, my_seq):
    n_rep, n_seq = lax.axis_size("rep"), lax.axis_size("seq")
    spd = master.shape[0]
    quarter = spd // n_rep
    own = master.astype(BF)
    own_quarter = lax.dynamic_slice_in_dim(master, my_rep * quarter, quarter, 0).astype(BF)
    lanes = jnp.arange(quarter, dtype=jnp.int32)

    def quarter_slots(seq_index, rep_index):
        return seq_index * spd + rep_index * quarter + lanes

    seq_bits = bits_of(n_seq)[1:]
    pieces = {0: own_quarter}
    for bit in seq_bits:
        for delta in list(pieces):
            pieces[delta ^ bit] = swap(pieces[delta], "seq", bit)
    result = [(own, my_seq * spd + jnp.arange(spd, dtype=jnp.int32))]
    order_one, order_two = rep_bits(n_rep)
    half = (quarter + 1) // 2
    for delta, piece in pieces.items():
        if delta == 0:
            continue
        parts = []
        for order, lo, hi in ((order_one, 0, half), (order_two, half, quarter)):
            if lo == hi:
                continue
            held = piece[lo:hi]
            ids = quarter_slots(my_seq ^ delta, my_rep)[lo:hi]
            for bit in order:
                other = quarter_ids_flip(ids, bit, my_rep, quarter)
                held = jnp.concatenate([held, swap(held, "rep", bit)], axis=0)
                ids = jnp.concatenate([ids, other])
            parts.append((held, ids))
        held = jnp.concatenate([p for p, unused in parts], axis=0)
        ids = jnp.concatenate([i for unused, i in parts])
        result.append((held, ids))
    siblings = []
    for held, ids in result:
        base = ids // spd
        siblings.append((swap(held, "seq", 1), (base ^ 1) * spd + ids % spd))
    return result + siblings


def quarter_ids_flip(ids, bit, my_rep, quarter):
    spd_part = ids // quarter
    return (spd_part ^ bit) * quarter + ids % quarter


def chunk_sizes(spd):
    return [7] * (spd // 7) if spd % 7 == 0 else [spd]


def reduce_chunk(own, sibling, my_rep):
    n_rep = lax.axis_size("rep")
    got = swap(sibling, "seq", 1)
    order_one, order_two = rep_bits(n_rep)
    half = B // 2
    outs = []
    for order, base in ((order_one, 0), (order_two, half)):
        size = half
        start = jnp.int32(base)
        mine, theirs = own, got
        first = True
        for bit in order:
            size //= 2
            high = (my_rep // bit) % 2
            keep_at, send_at = start + high * size, start + (1 - high) * size

            def cut(at, size=size, first=first, mine=mine, theirs=theirs):
                a = lax.dynamic_slice_in_dim(mine, at, size, 2).astype(F32)
                if theirs is None:
                    return a
                return a + lax.dynamic_slice_in_dim(theirs, at, size, 2).astype(F32)

            sent = swap(cut(send_at).astype(BF), "rep", bit)
            mine = cut(keep_at) + sent.astype(F32)
            theirs = None
            start = jnp.int32(0)
        outs.append(mine)
    held = jnp.concatenate(outs, axis=2)
    n_target = held.shape[0]
    while n_target > 1:
        n_target //= 2
        sent = swap(held[n_target:].astype(BF), "seq", 2 * n_target)
        held = held[:n_target] + sent.astype(F32)
    held = held[0].astype(BF)
    size = held.shape[1] // 2
    pieces, places = [], []
    for order, base, value in (
        (order_one, 0, held[:, :size]),
        (order_two, half, held[:, size:]),
    ):
        offset = jnp.int32(base)
        span = half
        for bit in order:
            span //= 2
            offset = offset + ((my_rep // bit) % 2) * span
        for bit in order[::-1]:
            pieces_here = swap(value, "rep", bit)
            high = (my_rep // bit) % 2
            value = jnp.where(
                high == 1,
                jnp.concatenate([pieces_here, value], axis=1),
                jnp.concatenate([value, pieces_here], axis=1),
            )
        pieces.append(value)
        places.append(jnp.int32(base))
    return pieces, places


def small_step(old_values, grads, split_at):
    head_grad = grads[:split_at]
    tail_grad = grads[split_at:]
    head_new = old_values[:split_at] - SMALL_RATE * head_grad * lax.rsqrt(
        jnp.mean(head_grad * head_grad) + RMS_EPS
    )
    tail_new = old_values[split_at:] - SMALL_RATE * tail_grad * lax.rsqrt(
        jnp.mean(tail_grad * tail_grad) + RMS_EPS
    )
    return jnp.concatenate([head_new, tail_new])


def shards(
    tokens,
    cotangent,
    doc_lengths,
    doc_owners,
    small_params,
    slot_block,
    master_blocks,
    left_stats,
    right_stats,
    left_roots,
    right_roots,
):
    seg_dev = tokens.shape[0] // SEG_LEN
    n_seq = lax.axis_size("seq")
    my_seq = lax.axis_index("seq")
    my_rep = lax.axis_index("rep")
    spd = master_blocks.shape[0]

    gathered = gather_weights(master_blocks, my_rep, my_seq)
    bufs = [held for held, unused in gathered]
    entry = jnp.take(slot_block, jnp.concatenate([ids for unused, ids in gathered]))

    par_one = small_params[None, :NPAR]
    par_two = small_params[None, NPAR : 2 * NPAR]
    position = small_params[2 * NPAR :].reshape(DOC_LONG, D)

    out_one, cls, qkv, probs, r1, r2, gp, lt_one = first_fwd(entry, bufs, tokens, par_one)
    cls_low = cls.reshape(seg_dev, D)

    lengths_row = doc_lengths[0]
    owners_row = doc_owners[0]
    starts_row = jnp.cumsum(lengths_row) - lengths_row
    first_seg = my_seq * seg_dev
    inside = (starts_row <= first_seg) & (first_seg < starts_row + lengths_row)
    owner = jnp.sum(jnp.where(inside, owners_row, 0))
    target = (jnp.arange(n_seq, dtype=jnp.int32) == owner)[:, None, None]
    zero_low = jnp.zeros((), BF)
    cot_first = cotangent.reshape(seg_dev, SEG_LEN, D)[:, 0, :]
    got_cot = lax.all_to_all(
        jnp.where(target, cot_first[None], zero_low), "seq", split_axis=0, concat_axis=0, tiled=True
    )
    got_cls = lax.all_to_all(
        jnp.where(target, cls_low[None], zero_low), "seq", split_axis=0, concat_axis=0, tiled=True
    )
    mine = (owners_row == my_seq) & (lengths_row > 0)
    my_start = jnp.sum(jnp.where(mine, starts_row, 0))
    my_len = jnp.sum(jnp.where(mine, lengths_row, 0))
    group_rows = n_seq * seg_dev
    padding = jnp.zeros((SEG_LEN, D), BF)

    def window(got):
        rows = jnp.concatenate([got.reshape(group_rows, D), padding], axis=0)
        return lax.dynamic_slice_in_dim(rows, my_start, SEG_LEN, 0).astype(F32)

    row_valid = jnp.arange(SEG_LEN) < my_len
    in_doc = (jnp.arange(SEG_LEN) < DOC_LONG)[:, None]
    pos_rows = jnp.concatenate([position, jnp.zeros((SEG_LEN - DOC_LONG, D), F32)], axis=0)
    doc_in = jnp.where(in_doc, window(got_cls) + pos_rows, 0.0)
    dout_two = jnp.where(row_valid[:, None], window(got_cot), 0.0)
    key_bias = jnp.where(row_valid, 0.0, MASKED_SCORE).astype(F32)[None]
    y_two, lt_two, r_two, dx_two, pg_two = second_layer(entry, bufs, doc_in, dout_two, key_bias, par_two)
    out_low = jnp.where(row_valid[:, None], y_two, zero_low)[:DOC_LONG]
    grad_pos = dx_two[:DOC_LONG]
    dcls_low = jnp.where(row_valid[:, None], dx_two, 0.0).astype(BF)[:DOC_LONG]

    blank = jnp.zeros((group_rows + DOC_LONG, D), BF)

    def reply(rows):
        placed = lax.dynamic_update_slice_in_dim(blank, rows, my_start, 0)[:group_rows]
        back = lax.all_to_all(
            placed.reshape(n_seq, seg_dev, D), "seq", split_axis=0, concat_axis=0, tiled=True
        )
        return jnp.sum(back.astype(F32), axis=0)

    dcls = reply(dcls_low)
    cls_new = reply(out_low)
    hidden_out = (
        out_one.reshape(seg_dev, SEG_LEN, D).at[:, 0, :].set(cls_new.astype(BF)).reshape(seg_dev * SEG_LEN, D)
    )
    r_one, input_grad, pg_one = first_bwd(entry, bufs, cotangent, dcls, par_one, (qkv, probs, r1, r2, gp))

    small_local = jnp.concatenate([pg_one[0], pg_two[0], grad_pos.reshape(-1)])
    small_grads = lax.psum(small_local, ("rep", "seq"))

    n_target = n_seq // 2
    stats = (left_stats, right_stats, left_roots, right_roots, master_blocks)
    results = ()
    first = 0
    targets = (my_seq // 2) ^ jnp.arange(n_target, dtype=jnp.int32)
    for m in chunk_sizes(spd):
        local = first + jnp.arange(m, dtype=jnp.int32)

        def entries(core):
            return ((targets * 2 + core)[:, None] * spd + local[None]).reshape(-1)

        tab = jnp.take(slot_block, jnp.concatenate([entries(1 - my_seq % 2), entries(my_seq % 2)]))
        grads = weight_grad(tab, lt_one, r_one, lt_two, r_two).reshape(2, n_target, m, B, B)
        pieces, places = reduce_chunk(grads[1], grads[0], my_rep)
        results = shampoo(first, jnp.stack(places), pieces, stats, results)
        first += m
    block_grads, left_new, right_new, new_blocks = results
    new_small = small_step(small_params, small_grads, 2 * NPAR)
    return (
        hidden_out,
        input_grad,
        out_low[None],
        block_grads,
        left_new,
        right_new,
        new_blocks,
        small_grads,
        new_small,
    )


def solution(mesh):
    in_specs = (
        P(("rep", "seq"), None),
        P(("rep", "seq"), None),
        P("rep", None),
        P("rep", None),
        P(),
        P(),
        P("seq", None, None),
        P("seq", None, None),
        P("seq", None, None),
        P("seq", None, None),
        P("seq", None, None),
    )
    out_specs = (
        P(("rep", "seq"), None),
        P(("rep", "seq"), None),
        P(("rep", "seq"), None, None),
        P("seq", None, None),
        P("seq", None, None),
        P("seq", None, None),
        P("seq", None, None),
        P(),
        P(),
    )
    return jax.shard_map(shards, mesh=mesh, in_specs=in_specs, out_specs=out_specs, check_vma=False)
```

```python
import functools

import jax
import jax.numpy as jnp
import numpy as np
from jax import lax
from jax.experimental import pallas as pl
from jax.experimental.pallas import tpu as pltpu
from jax.sharding import PartitionSpec as P

D = 768
HEAD_DIM = 64
FF = 3072
SEG_LEN = 128
DOC_LONG = 64
B = 256
PER_LAYER = 108
NBLK = 2 * PER_LAYER
NPAR = 8 * D + FF
NPAIR = D // 128

NORM_EPS = 1e-05
RMS_EPS = 1e-06
DECAY = 0.5
BLOCK_RATE = 0.02
SMALL_RATE = 0.1
MASKED_SCORE = -1000000000.0
SCALE = HEAD_DIM**-0.5

C_QKV, C_OUT, C_UP, C_DOWN, W_COLS = 0, 3 * D, 4 * D, 4 * D + FF, 4 * D + 2 * FF
W_SPANS = ((C_QKV, C_OUT), (C_OUT, C_UP), (C_UP, C_DOWN), (C_DOWN, W_COLS))
L_X, L_A, L_H, L_E, L_ROWS = 0, D, 2 * D, 3 * D, 3 * D + FF
R_QKV, R_OUT, R_UP, R_DOWN, R_COLS = 0, 3 * D, 4 * D, 4 * D + FF, 5 * D + FF
O_BQ, O_BV, O_BO, O_G1, O_C1, O_B1 = 0, D, 2 * D, 3 * D, 4 * D, 5 * D
O_B2, O_G2, O_C2 = 5 * D + FF, 6 * D + FF, 7 * D + FF

VMEM_LIMIT = 60 * 1024 * 1024
BF = jnp.bfloat16
F32 = jnp.float32


def block_tables():
    w_i, w_j, l_i, r_j = [], [], [], []
    for i in range(3):
        for j in range(9):
            w_i.append(i), w_j.append(j), l_i.append(i), r_j.append(j)
    for i in range(3):
        for j in range(3):
            w_i.append(i), w_j.append(9 + j), l_i.append(3 + i), r_j.append(9 + j)
    for i in range(3):
        for j in range(12):
            w_i.append(i), w_j.append(12 + j), l_i.append(6 + i), r_j.append(12 + j)
    for i in range(12):
        for j in range(3):
            w_i.append(i % 3), w_j.append(24 + 3 * (i // 3) + j)
            l_i.append(9 + i), r_j.append(24 + j)
    return [np.array(t, np.int32) for t in (w_i, w_j, l_i, r_j)]


W_I, W_J, L_I, R_J = block_tables()


def mm(a, b):
    return jnp.dot(a, b, preferred_element_type=F32)


def mm_t(a, b):
    return lax.dot_general(a, b, (((1,), (1,)), ((), ())), preferred_element_type=F32)


def tmm(a, b):
    return lax.dot_general(a, b, (((0,), (0,)), ((), ())), preferred_element_type=F32)


def norm_parts(values):
    center = values - jnp.mean(values, axis=-1, keepdims=True)
    spread = jnp.mean(center * center, axis=-1, keepdims=True)
    scale = lax.rsqrt(spread + NORM_EPS)
    return center * scale, scale


def gelu_parts(u):
    cdf = 0.5 + 0.5 * lax.erf(u * 0.7071067811865476)
    return u * cdf, cdf + u * jnp.exp(-0.5 * u * u) * 0.3989422804014327


def head_masks():
    lane = lax.broadcasted_iota(jnp.int32, (1, 128), 1)
    first = jnp.where(lane < HEAD_DIM, 1.0, 0.0).astype(BF)
    return first, (1.0 - first.astype(F32)).astype(BF)


def stack_heads(pair, masks):
    return jnp.concatenate([pair * masks[0], pair * masks[1]], axis=0)


def beside(stacked):
    half = stacked.shape[0] // 2
    return jnp.concatenate([stacked[:half], stacked[half:]], axis=1)


def wait_weights(w_ref, sems, mat):
    lo, hi = W_SPANS[mat]
    part = w_ref.at[:, lo:hi]
    pltpu.make_async_copy(part, part, sems.at[mat]).wait()


def fwd_tile(x32, xb, w, par, key_bias, qkv_ref, p_ref, r1_ref, r2_ref, gp_ref, lt_ref, a_ref, wait):
    n_rows = xb.shape[0]
    lt_ref[L_X : L_X + D, :] = xb.T
    wait(0)
    for c, off in ((0, O_BQ), (1, None), (2, O_BV)):
        part = mm(xb, w[:, C_QKV + c * D : C_QKV + (c + 1) * D])
        if off is not None:
            part = part + par[:, off : off + D]
        qkv_ref[:, c * D : (c + 1) * D] = part.astype(BF)
    masks = head_masks()
    for s in range(n_rows // SEG_LEN):
        rows = slice(s * SEG_LEN, (s + 1) * SEG_LEN)
        for h in range(NPAIR):
            q = qkv_ref[rows, h * 128 : (h + 1) * 128]
            k = qkv_ref[rows, D + h * 128 : D + (h + 1) * 128]
            v = qkv_ref[rows, 2 * D + h * 128 : 2 * D + (h + 1) * 128]
            scores = mm_t(stack_heads(q, masks), k) * SCALE
            if key_bias is not None:
                scores = scores + key_bias
            exps = jnp.exp(scores - jnp.max(scores, axis=-1, keepdims=True))
            probs = exps * (1.0 / jnp.sum(exps, axis=-1, keepdims=True))
            probs = beside(probs.astype(BF))
            p_ref[rows, h * 256 : (h + 1) * 256] = probs
            a_ref[rows, h * 128 : (h + 1) * 128] = mm(probs, stack_heads(v, masks)).astype(BF)
    a = a_ref[...]
    lt_ref[L_A : L_A + D, :] = a.T
    wait(1)
    r1 = x32 + (mm(a, w[:, C_OUT : C_OUT + D]) + par[:, O_BO : O_BO + D])
    r1_ref[...] = r1
    xhat, unused = norm_parts(r1)
    h = xhat * par[:, O_G1 : O_G1 + D] + par[:, O_C1 : O_C1 + D]
    hb = h.astype(BF)
    lt_ref[L_H : L_H + D, :] = hb.T
    wait(2)
    total = h + par[:, O_B2 : O_B2 + D]
    for c in range(FF // D):
        u = mm(hb, w[:, C_UP + c * D : C_UP + (c + 1) * D]) + par[:, O_B1 + c * D : O_B1 + (c + 1) * D]
        e, gp = gelu_parts(u)
        gp_ref[:, c * D : (c + 1) * D] = gp.astype(BF)
        eb = e.astype(BF)
        lt_ref[L_E + c * D : L_E + (c + 1) * D, :] = eb.T
        if c == 0:
            wait(3)
        total = total + mm(eb, w[:, C_DOWN + c * D : C_DOWN + (c + 1) * D])
    r2_ref[...] = total
    xhat, unused = norm_parts(total)
    return xhat * par[:, O_G2 : O_G2 + D] + par[:, O_C2 : O_C2 + D]


def col_sum(values):
    return jnp.sum(values.astype(F32), axis=0, keepdims=True)


def norm_back(dout, values, gain):
    xhat, scale = norm_parts(values)
    dxhat = dout * gain
    mean_one = jnp.mean(dxhat, axis=-1, keepdims=True)
    mean_two = jnp.mean(dxhat * xhat, axis=-1, keepdims=True)
    return scale * (dxhat - mean_one - xhat * mean_two), col_sum(dout * xhat), col_sum(dout)


def bwd_tile(dout, w, par, qkv_ref, p_ref, r1_ref, r2_ref, gp_ref, r_ref, pg_ref, da_ref, wait):
    n_rows = dout.shape[0]

    def add_small(off, value):
        pg_ref[:, off : off + value.shape[1]] += value

    dr2, dgain, dshift = norm_back(dout, r2_ref[...], par[:, O_G2 : O_G2 + D])
    add_small(O_G2, dgain)
    add_small(O_C2, dshift)
    dy = dr2.astype(BF)
    r_ref[:, R_DOWN : R_DOWN + D] = dy
    add_small(O_B2, col_sum(dy))
    wait(3)
    dh = dr2
    for c in range(FF // D):
        de = mm_t(dy, w[:, C_DOWN + c * D : C_DOWN + (c + 1) * D])
        du = (gp_ref[:, c * D : (c + 1) * D].astype(F32) * de).astype(BF)
        r_ref[:, R_UP + c * D : R_UP + (c + 1) * D] = du
        add_small(O_B1 + c * D, col_sum(du))
        if c == 0:
            wait(2)
        dh = dh + mm_t(du, w[:, C_UP + c * D : C_UP + (c + 1) * D])
    dr1, dgain, dshift = norm_back(dh, r1_ref[...], par[:, O_G1 : O_G1 + D])
    add_small(O_G1, dgain)
    add_small(O_C1, dshift)
    do = dr1.astype(BF)
    r_ref[:, R_OUT : R_OUT + D] = do
    add_small(O_BO, col_sum(do))
    wait(1)
    da_ref[...] = mm_t(do, w[:, C_OUT : C_OUT + D]).astype(BF)
    masks = head_masks()
    for s in range(n_rows // SEG_LEN):
        rows = slice(s * SEG_LEN, (s + 1) * SEG_LEN)
        for h in range(NPAIR):
            q = qkv_ref[rows, h * 128 : (h + 1) * 128]
            k = qkv_ref[rows, D + h * 128 : D + (h + 1) * 128]
            v = qkv_ref[rows, 2 * D + h * 128 : 2 * D + (h + 1) * 128]
            probs = jnp.concatenate(
                [p_ref[rows, h * 256 : h * 256 + 128], p_ref[rows, h * 256 + 128 : h * 256 + 256]], axis=0
            )
            da = stack_heads(da_ref[rows, h * 128 : (h + 1) * 128], masks)
            dprobs = mm_t(da, v)
            dv = tmm(probs, da)
            probs = probs.astype(F32)
            inner = jnp.sum(dprobs * probs, axis=-1, keepdims=True)
            dscores = (probs * (dprobs - inner) * SCALE).astype(BF)
            dq = mm(beside(dscores), stack_heads(k, masks))
            dk = tmm(dscores, stack_heads(q, masks))
            r_ref[rows, h * 128 : (h + 1) * 128] = dq.astype(BF)
            r_ref[rows, D + h * 128 : D + (h + 1) * 128] = dk.astype(BF)
            r_ref[rows, 2 * D + h * 128 : 2 * D + (h + 1) * 128] = dv.astype(BF)
    add_small(O_BQ, col_sum(r_ref[:, 0:D]))
    add_small(O_BV, col_sum(r_ref[:, 2 * D : 3 * D]))
    wait(0)
    return dr1 + mm_t(r_ref[:, R_QKV : R_QKV + 3 * D], w[:, C_QKV : C_QKV + 3 * D])


TILE = 256


def any_spec():
    return pl.BlockSpec(memory_space=pl.ANY)


def smem_spec():
    return pl.BlockSpec(memory_space=pltpu.SMEM)


def vmem_spec():
    return pl.BlockSpec(memory_space=pltpu.VMEM)


def row_spec(width, tile=TILE):
    return pl.BlockSpec((tile, width), lambda i, *_: (i, 0))


def whole_spec(shape):
    return pl.BlockSpec(shape, lambda i, *_: (0,) * len(shape))


def params():
    return pltpu.CompilerParams(vmem_limit_bytes=VMEM_LIMIT)


def cost(flops, nbytes):
    return pl.CostEstimate(flops=flops, bytes_accessed=nbytes, transcendentals=0)


def sort_slots(slot_block, base, order, at, spd):
    def first(j, count):
        take = slot_block[base + j] < PER_LAYER

        @pl.when(take)
        def _():
            order[at + count] = j

        return count + take.astype(jnp.int32)

    def second(j, count):
        take = slot_block[base + j] >= PER_LAYER

        @pl.when(take)
        def _():
            order[at + count] = j

        return count + take.astype(jnp.int32)

    lax.fori_loop(0, spd, second, lax.fori_loop(0, spd, first, 0))


def quarter_kernel(spd, n_rep, spans, slot_block, info, master, out, extra, order, stage, sem):
    sort_slots(slot_block, info[0] * spd, order, 0, spd)
    at = 0
    for lo, count in spans:
        quarter = count // n_rep
        for i in range(quarter):
            slot = order[lo + info[1] * quarter + i]
            pltpu.make_async_copy(master.at[slot], stage.at[at], sem).start()
            at += 1
    pltpu.make_async_copy(stage, stage, sem).wait()
    for i in range(at):
        if i < out.shape[0]:
            out[i] = stage[i].astype(BF)
        else:
            extra[i - out.shape[0]] = stage[i].astype(BF)


def quarter_blocks(slot_block, info, master, spans, n_rep):
    spd = master.shape[0]
    total_rows = spd // n_rep
    return pl.pallas_call(
        functools.partial(quarter_kernel, spd, n_rep, spans),
        in_specs=[smem_spec(), smem_spec(), any_spec()],
        out_specs=[vmem_spec()] * 2,
        out_shape=[
            jax.ShapeDtypeStruct((spans[0][1] // n_rep, B, B), BF),
            jax.ShapeDtypeStruct((max(total_rows - spans[0][1] // n_rep, 1), B, B), BF),
        ],
        scratch_shapes=[
            pltpu.SMEM((spd,), jnp.int32),
            pltpu.VMEM((total_rows, B, B), F32),
            pltpu.SemaphoreType.DMA(()),
        ],
        compiler_params=params(),
        cost_estimate=cost(1, 3_000_000),
        name="quarter_blocks",
    )(slot_block, info, master)


def plan_kernel(spd, n_seq, spans, n_after, slot_block, info, master, *rest):
    order, blocks, where, *rest = rest[n_after:]
    outs, (stage, sem) = rest[: len(spans)], rest[len(spans) :]
    my_seq = info[0]
    sort_slots(slot_block, my_seq * spd, order, my_seq * spd, spd)

    def fetch(k, carry):
        pltpu.make_async_copy(master.at[order[my_seq * spd + k]], stage.at[k], sem).start()
        return carry

    lax.fori_loop(0, spd, fetch, 0)

    def group(s, carry):
        sort_slots(slot_block, s * spd, order, s * spd, spd)

        def number(k, inner):
            n = slot_block[s * spd + order[s * spd + k]]
            blocks[s * spd + k] = n
            where[n] = s * spd + k
            return inner

        return lax.fori_loop(0, spd, number, carry)

    lax.fori_loop(0, n_seq, group, 0)
    pltpu.make_async_copy(stage, stage, sem).wait()
    for out, (lo, count) in zip(outs, spans):

        def convert(k, carry, out=out, lo=lo):
            out[k] = stage[lo + k].astype(BF)
            return carry

        lax.fori_loop(0, count, convert, 0)


def plan_slots(slot_block, info, master, spans, n_seq, after):
    spd = master.shape[0]
    table = jax.ShapeDtypeStruct((n_seq * spd,), jnp.int32)
    return pl.pallas_call(
        functools.partial(plan_kernel, spd, n_seq, spans, len(after)),
        in_specs=[smem_spec(), smem_spec(), any_spec()] + [any_spec()] * len(after),
        out_specs=[smem_spec()] * 3 + [vmem_spec()] * len(spans),
        out_shape=[table, table, table]
        + [jax.ShapeDtypeStruct((count, B, B), BF) for unused, count in spans],
        scratch_shapes=[pltpu.VMEM((spd, B, B), F32), pltpu.SemaphoreType.DMA(())],
        compiler_params=params(),
        cost_estimate=cost(1, 12_000_000),
        name="plan_slots",
    )(slot_block, info, master, *after)


def swap(value, axis, bit):
    size = lax.axis_size(axis)
    return lax.ppermute(value, axis, [(i, i ^ bit) for i in range(size)])


def rep_swap(value, step):
    n_rep, n_seq = lax.axis_size("rep"), lax.axis_size("seq")
    bits = rep_orders(n_rep)
    pairs = []
    for r in range(n_rep):
        for s in range(n_seq):
            pairs.append((r * n_seq + s, (r ^ bits[s % 2][step]) * n_seq + s))
    return lax.ppermute(value, ("rep", "seq"), pairs)


def rep_orders(n_rep):
    bits = [1 << i for i in range(n_rep.bit_length() - 1)]
    return bits, bits[::-1]


def held_order(n_rep):
    result = []
    for bits in rep_orders(n_rep):
        held = [0]
        for bit in bits:
            held = held + [e ^ bit for e in held]
        result.append(held)
    return result


def shift_seq(value, step):
    n_seq = lax.axis_size("seq")
    pairs = [(i, i + 2 * step) for i in range(n_seq) if 0 <= i + 2 * step < n_seq]
    return lax.ppermute(value, "seq", pairs)


def relay_kernel(n_in, jobs, info, *rest):
    ins, outs = rest[:n_in], rest[-len(jobs) :]
    z = info[0] // 2
    for out, (rows, parts) in zip(outs, jobs):
        for lo, size, cases in parts:
            for zs, src, at in cases:
                if not zs:
                    out[lo : lo + size] = ins[src][at : at + size]
                    continue

                @pl.when(functools.reduce(lambda a, b: a | b, [z == v for v in zs]))
                def _(src=src, at=at, lo=lo, size=size, out=out):
                    out[lo : lo + size] = ins[src][at : at + size]


def relay(info, ins, jobs, after=()):
    extra = list(after)
    return pl.pallas_call(
        functools.partial(relay_kernel, len(ins), jobs),
        in_specs=[smem_spec()] + [vmem_spec()] * len(ins) + [any_spec()] * len(extra),
        out_specs=[vmem_spec()] * len(jobs),
        out_shape=[jax.ShapeDtypeStruct((rows, B, B), BF) for rows, unused in jobs],
        compiler_params=params(),
        cost_estimate=cost(1, 1),
        name="relay",
    )(info, *ins, *extra)


def gather_line(quarter, extra, info, my_seq, plan):
    q = quarter.shape[0]
    z = my_seq // 2
    core = my_seq % 2
    n_rep = lax.axis_size("rep")

    def pair(first, second, after=()):
        return relay(info, [first, second], [(2 * q, [(0, q, [((), 0, 0)]), (q, q, [((), 1, 0)])])], after)[0]

    def nearer(at):
        return [((0, 1), 1, at), ((2, 3), 0, at)]

    up, down = shift_seq(quarter, 1), shift_seq(quarter, -1)
    (near,) = relay(info, [up, down], [(q, [(0, q, nearer(0))])])
    up2, down2 = shift_seq(up, 1), shift_seq(down, -1)
    near1 = rep_swap(near, 0)
    order, blocks, where, *owns = plan(near)
    own = owns[0]
    near_pair = pair(near, near1, [order])
    near2 = rep_swap(near_pair, 1)
    (mid,) = relay(info, [up2, down2], [(q, [(0, q, nearer(0))])], [near_pair])
    up3, down3 = shift_seq(up2, 1), shift_seq(down2, -1)
    mid1 = rep_swap(mid, 0)

    def farthest(at):
        return [((0,), 3, at), ((1,), 0, at), ((2,), 1, at), ((3,), 2, at)]

    far, held = relay(
        info,
        [up, down, up3, down3, extra],
        [(q, [(0, q, farthest(0))]), (extra.shape[0], [(0, extra.shape[0], [((), 4, 0)])])],
        [mid],
    )
    late = [swap(held, "seq", 2 * delta) for delta in range(1, 4)]
    far1 = rep_swap(far, 0)
    mid_pair = pair(mid, mid1, [near2, far])
    mid2 = rep_swap(mid_pair, 1)
    sib_near = [swap(near_pair, "seq", 1), swap(near2, "seq", 1)]
    sib = swap(own, "seq", 1)
    far_pair = pair(far, far1, [mid2, mid_pair, sib] + sib_near + late)
    far2 = rep_swap(far_pair, 1)
    sib_mid = [swap(mid_pair, "seq", 1), swap(mid2, "seq", 1)]
    far_sib = [swap(far_pair, "seq", 1), swap(far2, "seq", 1)]
    my_rep = info[1]
    z_near = jnp.where(z < 2, z + 1, z - 1)
    z_mid = jnp.where(z < 2, z + 2, z - 2)
    z_far = jnp.where(z % 2 == 0, 3, 0)
    half = n_rep // 2
    result = [part_of(own, z, core), part_of(sib, z, 1 - core)]
    for zs, mine, theirs in (
        (z_near, (near_pair, near2), sib_near),
        (z_mid, (mid_pair, mid2), sib_mid),
        (z_far, (far_pair, far2), far_sib),
    ):
        for part in range(2):
            result.append(part_of(mine[part], zs, core, part * half, my_rep, q))
            result.append(part_of(theirs[part], zs, 1 - core, part * half, my_rep, q))
    return (order, blocks, where, owns), result, (late, tuple(z ^ delta for delta in range(1, 4)))


def gather_direct(quarter, own, my_seq, my_rep):
    z = my_seq // 2
    core = my_seq % 2
    n_rep, n_z = lax.axis_size("rep"), lax.axis_size("seq") // 2
    sib = swap(own, "seq", 1)
    result = [part_of(own, z, core), part_of(sib, z, 1 - core)]
    q = quarter.shape[0]
    for delta in range(1, n_z):
        held = swap(quarter, "seq", 2 * delta)
        for step in range(len(rep_orders(n_rep)[0])):
            held = jnp.concatenate([held, rep_swap(held, step)], axis=0)
        result.append(part_of(held, z ^ delta, core, 0, my_rep, q))
        result.append(part_of(swap(held, "seq", 1), z ^ delta, 1 - core, 0, my_rep, q))
    return result


def part_of(buf, z, core, part=0, rep=0, quarter=0, rows=None):
    return buf, rows or (0, buf.shape[0]), quarter, (z, core, part, rep)


def late_parts(late, own, sib, info, my_seq, my_rep):
    pieces, planes = late
    n_rep = lax.axis_size("rep")
    z, core = my_seq // 2, my_seq % 2
    q, n = pieces[0].shape[0], len(pieces)
    (here,) = relay(info, pieces, [(n * q, [(i * q, q, [((), i, 0)]) for i in range(n)])])
    result = [part_of(own, z, core), part_of(sib, z, 1 - core)]
    for e in range(n_rep):
        held = swap(here, "rep", e) if e else here
        other = swap(held, "seq", 1)
        for i, plane in enumerate(planes):
            rows = (i * q, q)
            result.append(part_of(held, plane, core, 0, my_rep ^ e, q, rows))
            result.append(part_of(other, plane, 1 - core, 0, my_rep ^ e, q, rows))
    return result


def describe(spans_parts, spd):
    bufs, layout, rows = [], [], []
    for (first, unused), parts in spans_parts:
        for buf, (row, count), quarter, (z, core, part, rep) in parts:
            index = [i for i, b in enumerate(bufs) if b is buf]
            if not index:
                bufs.append(buf)
                index = [len(bufs) - 1]
            layout.append((index[0], row, count, quarter))
            rows += [(z * 2 + core) * spd + first, core, part, rep]
    return jnp.stack([jnp.asarray(r, jnp.int32) for r in rows]), bufs, tuple(layout)


def load_weights(first_block, n_rep, layout, tables, blocks, desc, bufs, w_ref, sems):
    w_i, w_j, held = tables
    for index, (b, row0, count, quarter) in enumerate(layout):
        base, core, part, rep = (desc[4 * index + i] for i in range(4))

        def body(e, carry, buf=bufs[b], row0=row0, quarter=quarter, base=base, core=core, part=part, rep=rep):
            if quarter:
                place = (held[core * n_rep + part + e // quarter] ^ rep) * quarter + e % quarter
            else:
                place = e
            n = blocks[base + place] - first_block

            @pl.when((n >= 0) & (n < PER_LAYER))
            def _():
                row = pl.multiple_of(w_i[n] * B, B)
                col = pl.multiple_of(w_j[n] * B, B)
                mat = (
                    (n >= 27).astype(jnp.int32)
                    + (n >= 36).astype(jnp.int32)
                    + (n >= 72).astype(jnp.int32)
                )
                pltpu.make_async_copy(
                    buf.at[row0 + e], w_ref.at[pl.ds(row, B), pl.ds(col, B)], sems.at[mat]
                ).start()

            return carry

        lax.fori_loop(0, count, body, 0)


def weight_tables(n_rep):
    return [jnp.asarray(t) for t in (W_I, W_J, np.array(sum(held_order(n_rep), []), np.int32))]


def first_fwd_kernel(n_rep, nbuf, quarters, w_i, w_j, held, blocks, desc, x_ref, par, *rest):
    bufs = rest[:nbuf]
    out_ref, cls_ref, qkv_ref, p_ref, r1_ref, r2_ref, gp_ref, lt_ref, w, a_ref, sems = rest[nbuf:]
    first = pl.program_id(0) == 0

    @pl.when(first)
    def _():
        load_weights(0, n_rep, quarters, (w_i, w_j, held), blocks, desc, bufs, w, sems)

    def wait(mat):
        @pl.when(first)
        def _():
            wait_weights(w, sems, mat)

    xb = x_ref[...]
    out = fwd_tile(
        xb.astype(F32), xb, w, par, None, qkv_ref, p_ref, r1_ref, r2_ref, gp_ref, lt_ref, a_ref, wait
    ).astype(BF)
    out_ref[...] = out
    for s in range(TILE // SEG_LEN):
        cls_ref[0, s : s + 1, :] = out[s * SEG_LEN : s * SEG_LEN + 1, :]


def first_fwd(n_rep, weights, tokens, par):
    blocks, desc, bufs, quarters = weights
    rows = tokens.shape[0]
    steps = rows // TILE
    nseg = TILE // SEG_LEN
    return pl.pallas_call(
        functools.partial(first_fwd_kernel, n_rep, len(bufs), quarters),
        grid_spec=pltpu.PrefetchScalarGridSpec(
            num_scalar_prefetch=5,
            grid=(steps,),
            in_specs=[row_spec(D), whole_spec((1, NPAR))] + [any_spec()] * len(bufs),
            out_specs=[
                row_spec(D),
                pl.BlockSpec((1, nseg, D), lambda i, *_: (i, 0, 0)),
                row_spec(3 * D),
                row_spec(NPAIR * 256),
                row_spec(D),
                row_spec(D),
                row_spec(FF),
                pl.BlockSpec((L_ROWS, TILE), lambda i, *_: (0, i)),
            ],
            scratch_shapes=[
                pltpu.VMEM((D, W_COLS), BF),
                pltpu.VMEM((TILE, D), BF),
                pltpu.SemaphoreType.DMA((4,)),
            ],
        ),
        out_shape=[
            jax.ShapeDtypeStruct((rows, D), BF),
            jax.ShapeDtypeStruct((steps, nseg, D), BF),
            jax.ShapeDtypeStruct((rows, 3 * D), BF),
            jax.ShapeDtypeStruct((rows, NPAIR * 256), BF),
            jax.ShapeDtypeStruct((rows, D), F32),
            jax.ShapeDtypeStruct((rows, D), F32),
            jax.ShapeDtypeStruct((rows, FF), BF),
            jax.ShapeDtypeStruct((L_ROWS, rows), BF),
        ],
        compiler_params=params(),
        cost_estimate=cost(15_000_000_000, 60_000_000),
        name="first_forward",
    )(*weight_tables(n_rep), blocks, desc, tokens, par, *bufs)


def first_bwd_kernel(
    n_rep, nbuf, quarters, n_after, w_i, w_j, held, blocks, desc, cot_ref, back_ref, out_ref, par, *rest
):
    qkv_ref, p_ref, r1_ref, r2_ref, gp_ref = rest[:5]
    bufs = rest[5 : 5 + nbuf]
    hid_ref, r_ref, dx_ref, pg_ref, w, da_ref, rows_ref, sems = rest[5 + nbuf + n_after :]
    step = pl.program_id(0)
    first = step == 0

    @pl.when(first)
    def _():
        load_weights(0, n_rep, quarters, (w_i, w_j, held), blocks, desc, bufs, w, sems)
        pg_ref[...] = jnp.zeros_like(pg_ref)
        rows_ref[...] = jnp.sum(back_ref[...].astype(F32), axis=0)

    def wait(mat):
        @pl.when(first)
        def _():
            wait_weights(w, sems, mat)

    dout = cot_ref[...].astype(F32)
    out = out_ref[...]
    index = lax.broadcasted_iota(jnp.int32, (TILE, 1), 0)
    nseg = TILE // SEG_LEN
    for s in range(nseg):
        row = rows_ref[pl.ds(step * nseg + s, 1), :]
        dout = jnp.where(index == s * SEG_LEN, row[:, :D], dout)
        out = jnp.where(index == s * SEG_LEN, row[:, D:], out.astype(F32)).astype(BF)
    hid_ref[...] = out
    dx_ref[...] = bwd_tile(
        dout, w, par, qkv_ref, p_ref, r1_ref, r2_ref, gp_ref, r_ref, pg_ref, da_ref, wait
    )


def first_bwd(n_rep, weights, cot, back, out_one, par, kept, after):
    blocks, desc, bufs, quarters = weights
    rows = cot.shape[0]
    steps = rows // TILE
    nseg = TILE // SEG_LEN
    return pl.pallas_call(
        functools.partial(first_bwd_kernel, n_rep, len(bufs), quarters, len(after)),
        grid_spec=pltpu.PrefetchScalarGridSpec(
            num_scalar_prefetch=5,
            grid=(steps,),
            in_specs=[
                row_spec(D),
                whole_spec(back.shape),
                row_spec(D),
                whole_spec((1, NPAR)),
                row_spec(3 * D),
                row_spec(NPAIR * 256),
                row_spec(D),
                row_spec(D),
                row_spec(FF),
            ]
            + [any_spec()] * (len(bufs) + len(after)),
            out_specs=[row_spec(D), row_spec(R_COLS), row_spec(D), whole_spec((1, NPAR))],
            scratch_shapes=[
                pltpu.VMEM((D, W_COLS), BF),
                pltpu.VMEM((TILE, D), BF),
                pltpu.VMEM((steps * nseg, 2 * D), F32),
                pltpu.SemaphoreType.DMA((4,)),
            ],
        ),
        out_shape=[
            jax.ShapeDtypeStruct((rows, D), BF),
            jax.ShapeDtypeStruct((rows, R_COLS), BF),
            jax.ShapeDtypeStruct((rows, D), F32),
            jax.ShapeDtypeStruct((1, NPAR), F32),
        ],
        compiler_params=params(),
        cost_estimate=cost(30_000_000_000, 60_000_000),
        name="first_backward",
    )(*weight_tables(n_rep), blocks, desc, cot, back, out_one, par, *kept, *bufs, *after)


def second_kernel(
    n_rep, nbuf, quarters, w_i, w_j, held, blocks, desc, doc, got, pos, par, *rest
):
    bufs = rest[:nbuf]
    reply_ref, state_ref, lt_ref, r_ref, dx_ref, pg_ref = rest[nbuf : nbuf + 6]
    w, a_ref, qkv_ref, p_ref, r1_ref, r2_ref, gp_ref, x_ref, cot_ref, sems = rest[nbuf + 6 :]
    load_weights(PER_LAYER, n_rep, quarters, (w_i, w_j, held), blocks, desc, bufs, w, sems)
    pg_ref[...] = jnp.zeros_like(pg_ref)
    reply_ref[...] = jnp.zeros_like(reply_ref)
    x_ref[...] = jnp.zeros_like(x_ref)
    cot_ref[...] = jnp.zeros_like(cot_ref)
    start, length = doc[0], doc[1]
    for j in range(0, DOC_LONG, 16):
        rows = slice(j, j + 16)
        x_ref[rows, :] = pos[rows, :]

        @pl.when(j < length)
        def _(j=j, rows=rows):
            at = pl.ds(pl.multiple_of(start + j, 16), 16)
            x_ref[rows, :] = pos[rows, :] + got[at, :D].astype(F32)
            cot_ref[rows, :] = got[at, D:].astype(F32)

    key = lax.broadcasted_iota(jnp.int32, (1, SEG_LEN), 1)
    key_bias = jnp.where(key < length, 0.0, MASKED_SCORE).astype(F32)
    x32 = x_ref[...]
    y = fwd_tile(
        x32,
        x32.astype(BF),
        w,
        par,
        key_bias,
        qkv_ref,
        p_ref,
        r1_ref,
        r2_ref,
        gp_ref,
        lt_ref,
        a_ref,
        lambda mat: wait_weights(w, sems, mat),
    )
    row = lax.broadcasted_iota(jnp.int32, (SEG_LEN, 1), 0)
    y = jnp.where(row < length, y, 0.0)
    state_ref[...] = y[:DOC_LONG].astype(BF)
    dx = bwd_tile(
        cot_ref[...],
        w,
        par,
        qkv_ref,
        p_ref,
        r1_ref,
        r2_ref,
        gp_ref,
        r_ref,
        pg_ref,
        a_ref,
        lambda mat: None,
    )
    dx = jnp.where(row < length, dx, 0.0)
    dx_ref[...] = dx[:DOC_LONG]
    for j in range(0, DOC_LONG, 16):

        @pl.when(j < length)
        def _(j=j):
            at = pl.ds(pl.multiple_of(start + j, 16), 16)
            reply_ref[at, :D] = dx[j : j + 16].astype(BF)
            reply_ref[at, D:] = y[j : j + 16].astype(BF)


def second_layer(n_rep, weights, doc, got, pos, par):
    blocks, desc, bufs, quarters = weights
    rows = SEG_LEN
    group = got.shape[0]
    return pl.pallas_call(
        functools.partial(second_kernel, n_rep, len(bufs), quarters),
        in_specs=[smem_spec()] * 6 + [vmem_spec()] * 3 + [any_spec()] * len(bufs),
        out_specs=[vmem_spec()] * 6,
        scratch_shapes=[
            pltpu.VMEM((D, W_COLS), BF),
            pltpu.VMEM((rows, D), BF),
            pltpu.VMEM((rows, 3 * D), BF),
            pltpu.VMEM((rows, NPAIR * 256), BF),
            pltpu.VMEM((rows, D), F32),
            pltpu.VMEM((rows, D), F32),
            pltpu.VMEM((rows, FF), BF),
            pltpu.VMEM((rows, D), F32),
            pltpu.VMEM((rows, D), F32),
            pltpu.SemaphoreType.DMA((4,)),
        ],
        out_shape=[
            jax.ShapeDtypeStruct((group, 2 * D), BF),
            jax.ShapeDtypeStruct((DOC_LONG, D), BF),
            jax.ShapeDtypeStruct((L_ROWS, rows), BF),
            jax.ShapeDtypeStruct((rows, R_COLS), BF),
            jax.ShapeDtypeStruct((DOC_LONG, D), F32),
            jax.ShapeDtypeStruct((1, NPAR), F32),
        ],
        compiler_params=params(),
        cost_estimate=cost(8_000_000_000, 40_000_000),
        name="second_layer",
    )(*weight_tables(n_rep), blocks, desc, doc, got, pos, par, *bufs)


PRODUCTS = (
    (L_X, R_QKV, 9, 0),
    (L_A, R_OUT, 3, 27),
    (L_H, R_UP, 12, 36),
    (L_E, R_DOWN, 3, 72),
    (L_E + D, R_DOWN, 3, 81),
    (L_E + 2 * D, R_DOWN, 3, 90),
    (L_E + 3 * D, R_DOWN, 3, 99),
)


def send_block(src, n, ctx, where, info, outs, sem):
    spd, unused, chunks = ctx
    at = where[n]
    owner = at // spd
    k = at % spd
    target = (owner // 2) ^ (info[0] // 2)
    mine = (owner % 2) == (info[0] % 2)
    for c, (first, m) in enumerate(chunks):
        inside = (k >= first) & (k < first + m)
        for side, cond in ((0, inside & jnp.logical_not(mine)), (1, inside & mine)):

            @pl.when(cond)
            def _(c=c, side=side, first=first):
                pltpu.make_async_copy(src, outs[2 * c + side].at[target, k - first], sem).start()


def all_products(lt, r, stage, base, ctx, where, info, outs, sem, before=None):
    for lrow, rcol, across, first in PRODUCTS:
        if before is not None:
            before(lrow)
        for j in range(across):
            value = mm(lt[lrow : lrow + D, :], r[:, rcol + j * B : rcol + (j + 1) * B]).astype(BF)
            for i in range(D // B):
                local = first + i * across + j
                stage[local] = value[i * B : (i + 1) * B]
                send_block(stage.at[local], base + local, ctx, where, info, outs, sem)


def wait_blocks(stage, sem, count):
    part = stage.at[pl.ds(0, count)]
    pltpu.make_async_copy(part, part, sem).wait()


def second_grad_kernel(ctx, n_empty, n_after, where, info, lt, r, *rest):
    outs, (stage, zero, sem) = rest[n_after:-3], rest[-3:]
    zero[...] = jnp.zeros_like(zero)
    for n in range(NBLK, NBLK + n_empty):
        send_block(zero.at[n - NBLK], n, ctx, where, info, outs, sem)
    all_products(lt, r, stage, PER_LAYER, ctx, where, info, outs, sem)
    wait_blocks(stage, sem, PER_LAYER)
    if n_empty:
        wait_blocks(zero, sem, n_empty)


def chunk_arrays(ctx):
    return [jax.ShapeDtypeStruct((ctx[1], m, B, B), BF) for unused, m in ctx[2] for side in range(2)]


def second_grad(ctx, where, info, lt, r, after):
    shapes = chunk_arrays(ctx)
    n_empty = where.shape[0] - NBLK
    return pl.pallas_call(
        functools.partial(second_grad_kernel, ctx, n_empty, len(after)),
        in_specs=[smem_spec()] * 2 + [vmem_spec()] * 2 + [any_spec()] * len(after),
        out_specs=[any_spec()] * len(shapes),
        out_shape=shapes,
        scratch_shapes=[
            pltpu.VMEM((PER_LAYER, B, B), BF),
            pltpu.VMEM((max(n_empty, 1), B, B), BF),
            pltpu.SemaphoreType.DMA(()),
        ],
        compiler_params=params(),
        cost_estimate=cost(2_000_000_000, 18_000_000),
        name="second_gradients",
    )(where, info, lt, r, *after)


def first_grad_kernel(ctx, n_after, where, info, lt, r, *rest):
    n_out = 2 * len(ctx[2])
    outs = rest[n_out + n_after : 2 * n_out + n_after]
    lt_s, r_s, stage, sem, sems = rest[2 * n_out + n_after :]
    spans = ((L_X, L_A, R_QKV, R_OUT), (L_A, L_H, R_OUT, R_UP), (L_H, L_E, R_UP, R_DOWN), (L_E, L_ROWS, R_DOWN, R_COLS))
    copies = []
    for i, (la, lb, ra, rb) in enumerate(spans):
        pair = (
            pltpu.make_async_copy(lt.at[la:lb], lt_s.at[la:lb], sems.at[2 * i]),
            pltpu.make_async_copy(r.at[:, ra:rb], r_s.at[:, ra:rb], sems.at[2 * i + 1]),
        )
        for copy in pair:
            copy.start()
        copies.append((la, pair))

    def before(lrow):
        for la, pair in copies:
            if la == lrow:
                for copy in pair:
                    copy.wait()

    all_products(lt_s, r_s, stage, 0, ctx, where, info, outs, sem, before)
    wait_blocks(stage, sem, PER_LAYER)


def first_grad(ctx, where, info, lt, r, arrays, after):
    n = len(arrays)
    return pl.pallas_call(
        functools.partial(first_grad_kernel, ctx, len(after)),
        in_specs=[smem_spec()] * 2 + [any_spec()] * (2 + n + len(after)),
        out_specs=[any_spec()] * n,
        out_shape=[jax.ShapeDtypeStruct(a.shape, BF) for a in arrays],
        scratch_shapes=[
            pltpu.VMEM(lt.shape, BF),
            pltpu.VMEM(r.shape, BF),
            pltpu.VMEM((PER_LAYER, B, B), BF),
            pltpu.SemaphoreType.DMA(()),
            pltpu.SemaphoreType.DMA((8,)),
        ],
        input_output_aliases={4 + i: i for i in range(n)},
        compiler_params=params(),
        cost_estimate=cost(15_000_000_000, 40_000_000),
        name="first_gradients",
    )(where, info, lt, r, *arrays, *after)


def halve_kernel(step, n_after, info, a_ref, b_ref, *rest):
    send_ref, keep_ref = rest[n_after:]
    half = send_ref.shape[2]
    high = high_bit(info, step)
    for side, ref in ((1 - high, send_ref), (high, keep_ref)):
        rows = pl.ds(pl.multiple_of(side * half, half), half)
        ref[...] = a_ref[:, :, rows, :] + b_ref[:, :, rows, :]


def high_bit(info, step):
    orders = rep_orders(4)
    core, rep = info[0] % 2, info[1]
    bit = jnp.where(core == 0, orders[0][step], orders[1][step])
    return jnp.where((rep & bit) != 0, 1, 0)


def halve(info, step, a, b, after):
    n_target, m, rows, cols = a.shape
    shape = jax.ShapeDtypeStruct((n_target, m, rows // 2, cols), BF)

    def spec(r):
        return pl.BlockSpec((1, m, r, cols), lambda i, *_: (i, 0, 0, 0))

    return pl.pallas_call(
        functools.partial(halve_kernel, step, len(after)),
        grid_spec=pltpu.PrefetchScalarGridSpec(
            num_scalar_prefetch=1,
            grid=(n_target,),
            in_specs=[spec(rows)] * 2 + [any_spec()] * len(after),
            out_specs=[spec(rows // 2)] * 2,
        ),
        out_shape=[shape, shape],
        compiler_params=params(),
        cost_estimate=cost(1, 1),
        name="halve",
    )(info, a, b, *after)


def spread_kernel(n_after, a_ref, b_ref, *rest):
    for i, out in enumerate(rest[n_after:]):
        out[...] = a_ref[i] + b_ref[i]


def spread(a, b, after):
    shape = jax.ShapeDtypeStruct(a.shape[1:], BF)
    return pl.pallas_call(
        functools.partial(spread_kernel, len(after)),
        in_specs=[vmem_spec()] * 2 + [any_spec()] * len(after),
        out_specs=[vmem_spec()] * a.shape[0],
        out_shape=[shape] * a.shape[0],
        compiler_params=params(),
        cost_estimate=cost(1, 1),
        name="spread",
    )(a, b, *after)


def total_kernel(count, *rest):
    total = rest[0][...].astype(F32)
    for ref in rest[1:count]:
        total = total + ref[...].astype(F32)
    rest[-1][...] = total.astype(BF)


def total(parts, after):
    shape = jax.ShapeDtypeStruct(parts[0].shape, BF)
    return pl.pallas_call(
        functools.partial(total_kernel, len(parts)),
        in_specs=[vmem_spec()] * len(parts) + [any_spec()] * len(after),
        out_specs=vmem_spec(),
        out_shape=shape,
        compiler_params=params(),
        cost_estimate=cost(1, 1),
        name="total",
    )(*parts, *after)


def shampoo_kernel(n_rep, spd, first, n_previous, order, info, *rest):
    pieces, stats = rest[:n_rep], rest[n_rep : n_rep + 5]
    outs, token, (ins_ref, outs_ref, g_ref, ins_sem, outs_sem) = rest[-10:-6], rest[-6], rest[-5:]
    token[...] = jnp.zeros_like(token)
    count = pieces[0].shape[0]
    slots = [order[info[0] * spd + first + i] for i in range(count)]
    for i, slot in enumerate(slots):
        for a, stat in enumerate(stats):
            pltpu.make_async_copy(stat.at[slot], ins_ref.at[i, a], ins_sem.at[i]).start()
    orders = rep_orders(n_rep)
    size = B // n_rep
    places = []
    for e in range(n_rep):
        rep = info[1] ^ e
        place = jnp.int32(0)
        for level in range(len(orders[0])):
            bit = jnp.where(info[0] % 2 == 0, orders[0][level], orders[1][level])
            place = place + jnp.where((rep & bit) != 0, B >> (level + 1), 0)
        places.append(pl.multiple_of(place, size))
    for i, slot in enumerate(slots):
        for place, piece in zip(places, pieces):
            g_ref[i, pl.ds(place, size), :] = piece[i]
        g = g_ref[i]
        pltpu.make_async_copy(ins_ref.at[i], ins_ref.at[i], ins_sem.at[i]).wait()
        left, right, lroot, rroot, master = (ins_ref[i, a] for a in range(5))
        part = mm(lroot.astype(BF), g)
        outs_ref[i, 0] = g.astype(F32)
        outs_ref[i, 1] = DECAY * left + (1.0 - DECAY) * mm_t(g, g)
        outs_ref[i, 2] = DECAY * right + (1.0 - DECAY) * tmm(g, g)
        direction = mm(part.astype(BF), rroot.astype(BF))
        scale = BLOCK_RATE * lax.rsqrt(jnp.mean(direction * direction) + RMS_EPS)
        outs_ref[i, 3] = master - direction * scale
        for a, out in enumerate(outs):
            pltpu.make_async_copy(outs_ref.at[i, a], out.at[slot], outs_sem).start()
    pltpu.make_async_copy(outs_ref, outs_ref, outs_sem).wait()


def shampoo(order, info, spd, first, pieces, stats, previous, after):
    count = pieces[0].shape[0]
    n_rep = len(pieces)
    n_in = 2 + n_rep + len(stats)
    return pl.pallas_call(
        functools.partial(shampoo_kernel, n_rep, spd, first, len(previous)),
        in_specs=[smem_spec()] * 2
        + [vmem_spec()] * n_rep
        + [any_spec()] * (len(stats) + len(previous) + len(after)),
        out_specs=[any_spec()] * 4 + [vmem_spec()],
        out_shape=[jax.ShapeDtypeStruct((spd, B, B), F32)] * 4 + [jax.ShapeDtypeStruct((8, 128), F32)],
        scratch_shapes=[
            pltpu.VMEM((count, 5, B, B), F32),
            pltpu.VMEM((count, 4, B, B), F32),
            pltpu.VMEM((count, B, B), BF),
            pltpu.SemaphoreType.DMA((count,)),
            pltpu.SemaphoreType.DMA(()),
        ],
        input_output_aliases={n_in + i: i for i in range(len(previous))},
        compiler_params=params(),
        cost_estimate=cost(1, 1),
        name="shampoo",
    )(order, info, *pieces, *stats, *previous, *after)


def reduce_pipeline(ctx, chunks, ready, idle, stats, after):
    order, info, spd, n_rep = ctx
    state = {}
    results = ()
    for batch in range(len(chunks) + 5):
        for run in ready.get(batch, ()):
            after = run(after)
        for i in range(len(chunks))[::-1]:
            stage = batch - i
            if chunks[i] is None or stage < 1:
                continue
            first, m, products = chunks[i]
            if stage == 1:
                got, own = state[i]
                send, keep = halve(info, 0, own, got, after)
                state[i] = (rep_swap(send, 0), keep)
                after = (keep,)
            elif stage == 2:
                got, kept = state[i]
                send, keep = halve(info, 1, kept, got, after)
                state[i] = (rep_swap(send, 1), keep)
                after = (keep,)
            elif stage == 3:
                got, kept = state[i]
                parts = spread(kept, got, after)
                moved = [swap(part, "seq", 2 * d) for d, part in enumerate(parts) if d]
                state[i] = [parts[0]] + moved
                after = (parts[0],)
            elif stage == 4:
                mine = total(state[i], after)
                state[i] = [mine] + [swap(mine, "rep", e) for e in range(1, n_rep)]
                after = (mine,)
            elif stage == 5:
                *results, token = shampoo(order, info, spd, first, state[i], stats, results, after)
                after = (token,)
        for run in idle.get(batch, ()):
            after = run(after)
        if batch < len(chunks) and chunks[batch] is not None:
            sib, own = chunks[batch][2]()
            state[batch] = (swap(sib, "seq", 1), own)
    return results, after


def small_kernel(old, grads, *rest):
    out = rest[-1]
    rows = 2 * NPAR // 128
    for part in (slice(0, rows), slice(rows, None)):
        g = grads[part, :]
        out[part, :] = old[part, :] - SMALL_RATE * g * lax.rsqrt(jnp.mean(g * g) + RMS_EPS)


def add_kernel(a, b, *rest):
    rest[-1][...] = a[...] + b[...]


def add(a, b, after):
    return pl.pallas_call(
        add_kernel,
        in_specs=[vmem_spec()] * 2 + [any_spec()] * len(after),
        out_specs=vmem_spec(),
        out_shape=jax.ShapeDtypeStruct(a.shape, F32),
        compiler_params=params(),
        cost_estimate=cost(1, 1),
        name="add",
    )(a, b, *after)


def small_step(old, grads, after):
    shape = (old.shape[0] // 128, 128)
    return pl.pallas_call(
        small_kernel,
        in_specs=[vmem_spec()] * 2 + [any_spec()] * len(after),
        out_specs=vmem_spec(),
        out_shape=jax.ShapeDtypeStruct(shape, F32),
        compiler_params=params(),
        cost_estimate=cost(1, 1_000_000),
        name="small_step",
    )(old.reshape(shape), grads.reshape(shape), *after).reshape(-1)


def split_slots(spd):
    if spd == 28:
        return ((0, 20), (20, 8)), ((0, 8), (8, 8), (16, 4), (20, 8))
    return ((0, spd),), ((0, spd),)


def shards(
    tokens,
    cotangent,
    doc_lengths,
    doc_owners,
    small_params,
    slot_block,
    master_blocks,
    left_stats,
    right_stats,
    left_roots,
    right_roots,
):
    seg_dev = tokens.shape[0] // SEG_LEN
    n_seq, n_rep = lax.axis_size("seq"), lax.axis_size("rep")
    my_seq = lax.axis_index("seq").astype(jnp.int32)
    my_rep = lax.axis_index("rep").astype(jnp.int32)
    spd = master_blocks.shape[0]
    n_target = n_seq // 2
    info = jnp.stack([my_seq, my_rep])
    par_one = small_params[None, :NPAR]
    par_two = small_params[None, NPAR : 2 * NPAR]
    position = small_params[2 * NPAR :].reshape(DOC_LONG, D)

    line = n_seq == 8 and n_rep == 4 and spd == 28
    spans, chunk_spans = split_slots(spd) if line else (((0, spd),), ((0, spd),))
    ctx = (spd, n_target, chunk_spans)
    quarter, extra = quarter_blocks(slot_block, info, master_blocks, spans, n_rep)

    lengths_row = doc_lengths[0]
    owners_row = doc_owners[0]
    starts_row = jnp.cumsum(lengths_row) - lengths_row
    first_seg = my_seq * seg_dev
    inside = (starts_row <= first_seg) & (first_seg < starts_row + lengths_row)
    owner = jnp.sum(jnp.where(inside, owners_row, 0))
    target = (jnp.arange(n_seq, dtype=jnp.int32) == owner).astype(BF)[:, None, None]
    mine = (owners_row == my_seq) & (lengths_row > 0)
    doc = jnp.stack([jnp.sum(jnp.where(mine, starts_row, 0)), jnp.sum(jnp.where(mine, lengths_row, 0))])
    doc = doc.astype(jnp.int32)

    def to_owner(rows):
        sent = target * rows[None]
        got = lax.all_to_all(sent, "seq", split_axis=0, concat_axis=0, tiled=True)
        return got.reshape(n_seq * seg_dev, 2 * D)

    cot_first = cotangent.reshape(seg_dev, SEG_LEN, D)[:, 0, :]

    def plan(after):
        early = (after, par_one, par_two, position, target, doc, cot_first)
        return plan_slots(slot_block, info, master_blocks, spans, n_seq, early)

    stats = (left_stats, right_stats, left_roots, right_roots, master_blocks)
    if line:
        (order, blocks, where, owns), parts_one, late = gather_line(
            quarter, extra, info, my_seq, plan
        )
        late_sib = swap(owns[1], "seq", 1)
    else:
        order, blocks, where, *owns = plan(quarter)
        parts_one, late, late_sib = gather_direct(quarter, owns[0], my_seq, my_rep), None, None

    def layers(ahead):
        layers_parts = [(spans[0], parts_one)]
        first_parts = list(layers_parts)

        if line:
            layers_parts.append((spans[1], late_parts(late, owns[1], late_sib, info, my_seq, my_rep)))
        if not ahead:
            first_parts = layers_parts
        first_desc, first_bufs, first_layout = describe(first_parts, spd)
        one = (blocks, first_desc, first_bufs, first_layout)
        out_one, cls, *kept, lt_one = first_fwd(n_rep, one, tokens, par_one)
        second_desc, second_bufs, second_layout = describe(layers_parts, spd)
        two = (blocks, second_desc, second_bufs, second_layout)
        got = to_owner(jnp.concatenate([cls.reshape(seg_dev, D), cot_first], axis=1))
        reply, states, lt_two, r_two, grad_pos, pg_two = second_layer(
            n_rep, two, doc, got, position, par_two
        )
        arrays = second_grad(ctx, where, info, lt_two, r_two, ())
        back = lax.all_to_all(
            reply.reshape(n_seq, seg_dev, 2 * D), "seq", split_axis=0, concat_axis=0, tiled=True
        )
        box = {}

        def backward(after):
            box["bwd"] = first_bwd(n_rep, one, cotangent, back, out_one, par_one, kept, after)
            pg_one = box["bwd"][3]
            local = jnp.concatenate([pg_one[0], pg_two[0], grad_pos.reshape(-1)]).reshape(2, -1, 128)
            box["sum"] = lax.dynamic_index_in_dim(local, my_seq % 2, 0, False)
            box["got"] = swap(lax.dynamic_index_in_dim(local, 1 - my_seq % 2, 0, False), "seq", 1)
            return (box["bwd"][1],)

        routes = [("seq", 2 << b) for b in range((n_seq // 2).bit_length() - 1)][::-1]
        routes += [("rep", 1 << b) for b in range(n_rep.bit_length() - 1)][::-1]

        def small_hop(axis, bit):
            def run(after):
                box["sum"] = add(box["sum"], box["got"], after)
                box["got"] = swap(box["sum"], axis, bit)
                return (box["sum"],)

            return run

        per = 2
        n_done = per if ahead else 0

        def late_products(after):
            some, done = arrays[: len(arrays) - n_done], arrays[len(arrays) - n_done :]
            sub = (spd, n_target, chunk_spans[: len(some) // per])
            made = first_grad(sub, where, info, lt_one, box["bwd"][1], some, after)
            box["all"] = list(made) + list(done)
            return (made[1],)

        def chunk(c):
            return lambda: box["all"][per * c : per * c + per]

        chunks = [(first, m, chunk(c)) for c, (first, m) in enumerate(chunk_spans)]
        if ahead:
            early = chunks[-1][:2] + (lambda: arrays[-per:],)
            chunks = [early, None] + chunks[:-1]
            ready, idle = {}, {1: [backward], 2: [late_products]}
        else:
            ready, idle = {0: [backward, late_products]}, {}
        n = len(chunks)
        for at, route in zip([3, 4] + [n + 1 + i for i in range(len(routes))], routes):
            idle.setdefault(at, []).append(small_hop(*route))
        results, after = reduce_pipeline(
            (order, info, spd, n_rep), chunks, ready, idle, stats, (arrays[0],)
        )
        core = my_seq % 2
        mine = add(box["sum"], box["got"], after)
        theirs = swap(mine, "seq", 1)
        small_grads = jnp.where(
            core == 0, jnp.concatenate([mine, theirs]), jnp.concatenate([theirs, mine])
        ).reshape(-1)
        new_small = small_step(small_params, small_grads, ())
        hidden_out, unused, input_grad, unused = box["bwd"]
        return (hidden_out, input_grad, states[None], *results, small_grads, new_small)

    if not line:
        return layers(False)
    counts = jnp.sum((slot_block.reshape(n_seq, spd) < PER_LAYER).astype(jnp.int32), axis=1)
    return lax.cond(jnp.all(counts <= spans[0][1]), lambda: layers(True), lambda: layers(False))


def solution(mesh):
    in_specs = (
        P(("rep", "seq"), None),
        P(("rep", "seq"), None),
        P("rep", None),
        P("rep", None),
        P(),
        P(),
        P("seq", None, None),
        P("seq", None, None),
        P("seq", None, None),
        P("seq", None, None),
        P("seq", None, None),
    )
    out_specs = (
        P(("rep", "seq"), None),
        P(("rep", "seq"), None),
        P(("rep", "seq"), None, None),
        P("seq", None, None),
        P("seq", None, None),
        P("seq", None, None),
        P("seq", None, None),
        P(),
        P(),
    )
    return jax.shard_map(shards, mesh=mesh, in_specs=in_specs, out_specs=out_specs, check_vma=False)
```

```python
import functools

import jax
import jax.numpy as jnp
import numpy as np
from jax import lax
from jax.experimental import pallas as pl
from jax.experimental.pallas import tpu as pltpu
from jax.sharding import PartitionSpec as P

D = 768
HEAD_DIM = 64
FF = 3072
SEG_LEN = 128
DOC_LONG = 64
B = 256
PER_LAYER = 108
NBLK = 2 * PER_LAYER
NPAR = 8 * D + FF
NPAIR = D // 128

NORM_EPS = 1e-05
RMS_EPS = 1e-06
DECAY = 0.5
BLOCK_RATE = 0.02
SMALL_RATE = 0.1
MASKED_SCORE = -1000000000.0
SCALE = HEAD_DIM**-0.5

C_QKV, C_OUT, C_UP, C_DOWN, W_COLS = 0, 3 * D, 4 * D, 4 * D + FF, 4 * D + 2 * FF
W_SPANS = ((C_QKV, C_OUT), (C_OUT, C_UP), (C_UP, C_DOWN), (C_DOWN, W_COLS))
L_X, L_A, L_H, L_E, L_ROWS = 0, D, 2 * D, 3 * D, 3 * D + FF
R_QKV, R_OUT, R_UP, R_DOWN, R_COLS = 0, 3 * D, 4 * D, 4 * D + FF, 5 * D + FF
O_BQ, O_BV, O_BO, O_G1, O_C1, O_B1 = 0, D, 2 * D, 3 * D, 4 * D, 5 * D
O_B2, O_G2, O_C2 = 5 * D + FF, 6 * D + FF, 7 * D + FF

VMEM_LIMIT = 60 * 1024 * 1024
BF = jnp.bfloat16
F32 = jnp.float32


def block_tables():
    w_i, w_j, l_i, r_j = [], [], [], []
    for i in range(3):
        for j in range(9):
            w_i.append(i), w_j.append(j), l_i.append(i), r_j.append(j)
    for i in range(3):
        for j in range(3):
            w_i.append(i), w_j.append(9 + j), l_i.append(3 + i), r_j.append(9 + j)
    for i in range(3):
        for j in range(12):
            w_i.append(i), w_j.append(12 + j), l_i.append(6 + i), r_j.append(12 + j)
    for i in range(12):
        for j in range(3):
            w_i.append(i % 3), w_j.append(24 + 3 * (i // 3) + j)
            l_i.append(9 + i), r_j.append(24 + j)
    return [np.array(t, np.int32) for t in (w_i, w_j, l_i, r_j)]


W_I, W_J, L_I, R_J = block_tables()


def mm(a, b):
    return jnp.dot(a, b, preferred_element_type=F32)


def mm_t(a, b):
    return lax.dot_general(a, b, (((1,), (1,)), ((), ())), preferred_element_type=F32)


def tmm(a, b):
    return lax.dot_general(a, b, (((0,), (0,)), ((), ())), preferred_element_type=F32)


def norm_parts(values):
    center = values - jnp.mean(values, axis=-1, keepdims=True)
    spread = jnp.mean(center * center, axis=-1, keepdims=True)
    scale = lax.rsqrt(spread + NORM_EPS)
    return center * scale, scale


def gelu_parts(u):
    cdf = 0.5 + 0.5 * lax.erf(u * 0.7071067811865476)
    return u * cdf, cdf + u * jnp.exp(-0.5 * u * u) * 0.3989422804014327


def head_masks():
    lane = lax.broadcasted_iota(jnp.int32, (1, 128), 1)
    first = jnp.where(lane < HEAD_DIM, 1.0, 0.0).astype(BF)
    return first, (1.0 - first.astype(F32)).astype(BF)


def stack_heads(pair, masks):
    return jnp.concatenate([pair * masks[0], pair * masks[1]], axis=0)


def beside(stacked):
    half = stacked.shape[0] // 2
    return jnp.concatenate([stacked[:half], stacked[half:]], axis=1)


def wait_weights(w_ref, sems, mat):
    lo, hi = W_SPANS[mat]
    part = w_ref.at[:, lo:hi]
    pltpu.make_async_copy(part, part, sems.at[mat]).wait()


def fwd_tile(x32, xb, w, par, key_bias, qkv_ref, p_ref, r1_ref, r2_ref, gp_ref, lt_ref, a_ref, wait):
    n_rows = xb.shape[0]
    lt_ref[L_X : L_X + D, :] = xb.T
    wait(0)
    for c, off in ((0, O_BQ), (1, None), (2, O_BV)):
        part = mm(xb, w[:, C_QKV + c * D : C_QKV + (c + 1) * D])
        if off is not None:
            part = part + par[:, off : off + D]
        qkv_ref[:, c * D : (c + 1) * D] = part.astype(BF)
    masks = head_masks()
    for s in range(n_rows // SEG_LEN):
        rows = slice(s * SEG_LEN, (s + 1) * SEG_LEN)
        for h in range(NPAIR):
            q = qkv_ref[rows, h * 128 : (h + 1) * 128]
            k = qkv_ref[rows, D + h * 128 : D + (h + 1) * 128]
            v = qkv_ref[rows, 2 * D + h * 128 : 2 * D + (h + 1) * 128]
            scores = mm_t(stack_heads(q, masks), k) * SCALE
            if key_bias is not None:
                scores = scores + key_bias
            exps = jnp.exp(scores - jnp.max(scores, axis=-1, keepdims=True))
            probs = exps * (1.0 / jnp.sum(exps, axis=-1, keepdims=True))
            probs = beside(probs.astype(BF))
            p_ref[rows, h * 256 : (h + 1) * 256] = probs
            a_ref[rows, h * 128 : (h + 1) * 128] = mm(probs, stack_heads(v, masks)).astype(BF)
    a = a_ref[...]
    lt_ref[L_A : L_A + D, :] = a.T
    wait(1)
    r1 = x32 + (mm(a, w[:, C_OUT : C_OUT + D]) + par[:, O_BO : O_BO + D])
    r1_ref[...] = r1
    xhat, unused = norm_parts(r1)
    h = xhat * par[:, O_G1 : O_G1 + D] + par[:, O_C1 : O_C1 + D]
    hb = h.astype(BF)
    lt_ref[L_H : L_H + D, :] = hb.T
    wait(2)
    total = h + par[:, O_B2 : O_B2 + D]
    for c in range(FF // D):
        u = mm(hb, w[:, C_UP + c * D : C_UP + (c + 1) * D]) + par[:, O_B1 + c * D : O_B1 + (c + 1) * D]
        e, gp = gelu_parts(u)
        gp_ref[:, c * D : (c + 1) * D] = gp.astype(BF)
        eb = e.astype(BF)
        lt_ref[L_E + c * D : L_E + (c + 1) * D, :] = eb.T
        if c == 0:
            wait(3)
        total = total + mm(eb, w[:, C_DOWN + c * D : C_DOWN + (c + 1) * D])
    r2_ref[...] = total
    xhat, unused = norm_parts(total)
    return xhat * par[:, O_G2 : O_G2 + D] + par[:, O_C2 : O_C2 + D]


def col_sum(values):
    return jnp.sum(values.astype(F32), axis=0, keepdims=True)


def norm_back(dout, values, gain):
    xhat, scale = norm_parts(values)
    dxhat = dout * gain
    mean_one = jnp.mean(dxhat, axis=-1, keepdims=True)
    mean_two = jnp.mean(dxhat * xhat, axis=-1, keepdims=True)
    return scale * (dxhat - mean_one - xhat * mean_two), col_sum(dout * xhat), col_sum(dout)


def bwd_tile(dout, w, par, qkv_ref, p_ref, r1_ref, r2_ref, gp_ref, r_ref, pg_ref, da_ref, wait):
    n_rows = dout.shape[0]

    def add_small(off, value):
        pg_ref[:, off : off + value.shape[1]] += value

    dr2, dgain, dshift = norm_back(dout, r2_ref[...], par[:, O_G2 : O_G2 + D])
    add_small(O_G2, dgain)
    add_small(O_C2, dshift)
    dy = dr2.astype(BF)
    r_ref[:, R_DOWN : R_DOWN + D] = dy
    add_small(O_B2, col_sum(dy))
    wait(3)
    dh = dr2
    for c in range(FF // D):
        de = mm_t(dy, w[:, C_DOWN + c * D : C_DOWN + (c + 1) * D])
        du = (gp_ref[:, c * D : (c + 1) * D].astype(F32) * de).astype(BF)
        r_ref[:, R_UP + c * D : R_UP + (c + 1) * D] = du
        add_small(O_B1 + c * D, col_sum(du))
        if c == 0:
            wait(2)
        dh = dh + mm_t(du, w[:, C_UP + c * D : C_UP + (c + 1) * D])
    dr1, dgain, dshift = norm_back(dh, r1_ref[...], par[:, O_G1 : O_G1 + D])
    add_small(O_G1, dgain)
    add_small(O_C1, dshift)
    do = dr1.astype(BF)
    r_ref[:, R_OUT : R_OUT + D] = do
    add_small(O_BO, col_sum(do))
    wait(1)
    da_ref[...] = mm_t(do, w[:, C_OUT : C_OUT + D]).astype(BF)
    masks = head_masks()
    for s in range(n_rows // SEG_LEN):
        rows = slice(s * SEG_LEN, (s + 1) * SEG_LEN)
        for h in range(NPAIR):
            q = qkv_ref[rows, h * 128 : (h + 1) * 128]
            k = qkv_ref[rows, D + h * 128 : D + (h + 1) * 128]
            v = qkv_ref[rows, 2 * D + h * 128 : 2 * D + (h + 1) * 128]
            probs = jnp.concatenate(
                [p_ref[rows, h * 256 : h * 256 + 128], p_ref[rows, h * 256 + 128 : h * 256 + 256]], axis=0
            )
            da = stack_heads(da_ref[rows, h * 128 : (h + 1) * 128], masks)
            dprobs = mm_t(da, v)
            dv = tmm(probs, da)
            probs = probs.astype(F32)
            inner = jnp.sum(dprobs * probs, axis=-1, keepdims=True)
            dscores = (probs * (dprobs - inner) * SCALE).astype(BF)
            dq = mm(beside(dscores), stack_heads(k, masks))
            dk = tmm(dscores, stack_heads(q, masks))
            r_ref[rows, h * 128 : (h + 1) * 128] = dq.astype(BF)
            r_ref[rows, D + h * 128 : D + (h + 1) * 128] = dk.astype(BF)
            r_ref[rows, 2 * D + h * 128 : 2 * D + (h + 1) * 128] = dv.astype(BF)
    add_small(O_BQ, col_sum(r_ref[:, 0:D]))
    add_small(O_BV, col_sum(r_ref[:, 2 * D : 3 * D]))
    wait(0)
    return dr1 + mm_t(r_ref[:, R_QKV : R_QKV + 3 * D], w[:, C_QKV : C_QKV + 3 * D])


TILE = 256


def any_spec():
    return pl.BlockSpec(memory_space=pl.ANY)


def smem_spec():
    return pl.BlockSpec(memory_space=pltpu.SMEM)


def vmem_spec():
    return pl.BlockSpec(memory_space=pltpu.VMEM)


def row_spec(width, tile=TILE):
    return pl.BlockSpec((tile, width), lambda i, *_: (i, 0))


def whole_spec(shape):
    return pl.BlockSpec(shape, lambda i, *_: (0,) * len(shape))


def params():
    return pltpu.CompilerParams(vmem_limit_bytes=VMEM_LIMIT)


def cost(flops, nbytes):
    return pl.CostEstimate(flops=flops, bytes_accessed=nbytes, transcendentals=0)


def sort_slots(slot_block, base, order, at, spd):
    def first(j, count):
        take = slot_block[base + j] < PER_LAYER

        @pl.when(take)
        def _():
            order[at + count] = j

        return count + take.astype(jnp.int32)

    def second(j, count):
        take = slot_block[base + j] >= PER_LAYER

        @pl.when(take)
        def _():
            order[at + count] = j

        return count + take.astype(jnp.int32)

    lax.fori_loop(0, spd, second, lax.fori_loop(0, spd, first, 0))


def quarter_kernel(spd, n_rep, spans, slot_block, info, master, out, extra, order, stage, sem):
    sort_slots(slot_block, info[0] * spd, order, 0, spd)
    at = 0
    for lo, count in spans:
        quarter = count // n_rep
        for i in range(quarter):
            slot = order[lo + info[1] * quarter + i]
            pltpu.make_async_copy(master.at[slot], stage.at[at], sem).start()
            at += 1
    pltpu.make_async_copy(stage, stage, sem).wait()
    for i in range(at):
        if i < out.shape[0]:
            out[i] = stage[i].astype(BF)
        else:
            extra[i - out.shape[0]] = stage[i].astype(BF)


def quarter_blocks(slot_block, info, master, spans, n_rep):
    spd = master.shape[0]
    total_rows = spd // n_rep
    return pl.pallas_call(
        functools.partial(quarter_kernel, spd, n_rep, spans),
        in_specs=[smem_spec(), smem_spec(), any_spec()],
        out_specs=[vmem_spec()] * 2,
        out_shape=[
            jax.ShapeDtypeStruct((spans[0][1] // n_rep, B, B), BF),
            jax.ShapeDtypeStruct((max(total_rows - spans[0][1] // n_rep, 1), B, B), BF),
        ],
        scratch_shapes=[
            pltpu.SMEM((spd,), jnp.int32),
            pltpu.VMEM((total_rows, B, B), F32),
            pltpu.SemaphoreType.DMA(()),
        ],
        compiler_params=params(),
        cost_estimate=cost(1, 3_000_000),
        name="quarter_blocks",
    )(slot_block, info, master)


def plan_kernel(spd, n_seq, spans, n_after, slot_block, info, master, *rest):
    order, blocks, where, *rest = rest[n_after:]
    outs, (stage, sem) = rest[: len(spans)], rest[len(spans) :]
    my_seq = info[0]
    sort_slots(slot_block, my_seq * spd, order, my_seq * spd, spd)

    def fetch(k, carry):
        pltpu.make_async_copy(master.at[order[my_seq * spd + k]], stage.at[k], sem).start()
        return carry

    lax.fori_loop(0, spd, fetch, 0)

    def group(s, carry):
        sort_slots(slot_block, s * spd, order, s * spd, spd)

        def number(k, inner):
            n = slot_block[s * spd + order[s * spd + k]]
            blocks[s * spd + k] = n
            where[n] = s * spd + k
            return inner

        return lax.fori_loop(0, spd, number, carry)

    lax.fori_loop(0, n_seq, group, 0)
    pltpu.make_async_copy(stage, stage, sem).wait()
    for out, (lo, count) in zip(outs, spans):

        def convert(k, carry, out=out, lo=lo):
            out[k] = stage[lo + k].astype(BF)
            return carry

        lax.fori_loop(0, count, convert, 0)


def plan_slots(slot_block, info, master, spans, n_seq, after):
    spd = master.shape[0]
    table = jax.ShapeDtypeStruct((n_seq * spd,), jnp.int32)
    return pl.pallas_call(
        functools.partial(plan_kernel, spd, n_seq, spans, len(after)),
        in_specs=[smem_spec(), smem_spec(), any_spec()] + [any_spec()] * len(after),
        out_specs=[smem_spec()] * 3 + [vmem_spec()] * len(spans),
        out_shape=[table, table, table]
        + [jax.ShapeDtypeStruct((count, B, B), BF) for unused, count in spans],
        scratch_shapes=[pltpu.VMEM((spd, B, B), F32), pltpu.SemaphoreType.DMA(())],
        compiler_params=params(),
        cost_estimate=cost(1, 12_000_000),
        name="plan_slots",
    )(slot_block, info, master, *after)


def swap(value, axis, bit):
    size = lax.axis_size(axis)
    return lax.ppermute(value, axis, [(i, i ^ bit) for i in range(size)])


def rep_swap(value, step):
    n_rep, n_seq = lax.axis_size("rep"), lax.axis_size("seq")
    bits = rep_orders(n_rep)
    pairs = []
    for r in range(n_rep):
        for s in range(n_seq):
            pairs.append((r * n_seq + s, (r ^ bits[s % 2][step]) * n_seq + s))
    return lax.ppermute(value, ("rep", "seq"), pairs)


def rep_orders(n_rep):
    bits = [1 << i for i in range(n_rep.bit_length() - 1)]
    return bits, bits[::-1]


def held_order(n_rep):
    result = []
    for bits in rep_orders(n_rep):
        held = [0]
        for bit in bits:
            held = held + [e ^ bit for e in held]
        result.append(held)
    return result


def shift_seq(value, step):
    n_seq = lax.axis_size("seq")
    pairs = [(i, i + 2 * step) for i in range(n_seq) if 0 <= i + 2 * step < n_seq]
    return lax.ppermute(value, "seq", pairs)


def relay_kernel(n_in, jobs, info, *rest):
    ins, outs = rest[:n_in], rest[-len(jobs) :]
    z = info[0] // 2
    for out, (rows, parts) in zip(outs, jobs):
        for lo, size, cases in parts:
            for zs, src, at in cases:
                if not zs:
                    out[lo : lo + size] = ins[src][at : at + size]
                    continue

                @pl.when(functools.reduce(lambda a, b: a | b, [z == v for v in zs]))
                def _(src=src, at=at, lo=lo, size=size, out=out):
                    out[lo : lo + size] = ins[src][at : at + size]


def relay(info, ins, jobs, after=()):
    extra = list(after)
    return pl.pallas_call(
        functools.partial(relay_kernel, len(ins), jobs),
        in_specs=[smem_spec()] + [vmem_spec()] * len(ins) + [any_spec()] * len(extra),
        out_specs=[vmem_spec()] * len(jobs),
        out_shape=[jax.ShapeDtypeStruct((rows, B, B), BF) for rows, unused in jobs],
        compiler_params=params(),
        cost_estimate=cost(1, 1),
        name="relay",
    )(info, *ins, *extra)


def gather_line(quarter, extra, info, my_seq, plan):
    q = quarter.shape[0]
    z = my_seq // 2
    core = my_seq % 2
    n_rep = lax.axis_size("rep")

    def pair(first, second, after=()):
        return relay(info, [first, second], [(2 * q, [(0, q, [((), 0, 0)]), (q, q, [((), 1, 0)])])], after)[0]

    def nearer(at):
        return [((0, 1), 1, at), ((2, 3), 0, at)]

    up, down = shift_seq(quarter, 1), shift_seq(quarter, -1)
    (near,) = relay(info, [up, down], [(q, [(0, q, nearer(0))])])
    up2, down2 = shift_seq(up, 1), shift_seq(down, -1)
    near1 = rep_swap(near, 0)
    near_pair = pair(near, near1)
    near2 = rep_swap(near_pair, 1)
    order, blocks, where, *owns = plan(near_pair)
    own = owns[0]
    size = extra.shape[0]
    keep = (size, [(0, size, [((), 2, 0)])])
    mid, held = relay(info, [up2, down2, extra], [(q, [(0, q, nearer(0))]), keep], [order])
    late_two = swap(held, "seq", 4)
    ends = lax.ppermute(mid, "seq", [(2, 0), (3, 1), (4, 6), (5, 7)])
    mid1 = rep_swap(mid, 0)
    mid_pair = pair(mid, mid1, [near2])
    mid2 = rep_swap(mid_pair, 1)
    far, held = relay(
        info,
        [up, down, ends, extra],
        [
            (q, [(0, q, [((0, 3), 2, 0), ((1,), 0, 0), ((2,), 1, 0)])]),
            (size, [(0, size, [((), 3, 0)])]),
        ],
        [mid_pair, late_two],
    )
    late = [swap(held, "seq", 2), late_two, swap(held, "seq", 6)]
    far1 = rep_swap(far, 0)
    sib_near = [swap(near_pair, "seq", 1), swap(near2, "seq", 1)]
    sib = swap(own, "seq", 1)
    far_pair = pair(far, far1, [mid2, mid_pair, sib] + sib_near)
    far2 = rep_swap(far_pair, 1)
    sib_mid = [swap(mid_pair, "seq", 1), swap(mid2, "seq", 1)]
    far_sib = [swap(far_pair, "seq", 1), swap(far2, "seq", 1)]
    n = len(late)
    (here,) = relay(info, late, [(n * size, [(i * size, size, [((), i, 0)]) for i in range(n)])], [far_pair])
    my_rep = info[1]
    z_near = jnp.where(z < 2, z + 1, z - 1)
    z_mid = jnp.where(z < 2, z + 2, z - 2)
    z_far = jnp.where(z % 2 == 0, 3, 0)
    half = n_rep // 2
    result = [part_of(own, z, core), part_of(sib, z, 1 - core)]
    for zs, mine, theirs in (
        (z_near, (near_pair, near2), sib_near),
        (z_mid, (mid_pair, mid2), sib_mid),
        (z_far, (far_pair, far2), far_sib),
    ):
        for part in range(2):
            result.append(part_of(mine[part], zs, core, part * half, my_rep, q))
            result.append(part_of(theirs[part], zs, 1 - core, part * half, my_rep, q))
    return (order, blocks, where, owns), result, (here, tuple(z ^ delta for delta in range(1, 4)))


def gather_direct(quarter, own, my_seq, my_rep):
    z = my_seq // 2
    core = my_seq % 2
    n_rep, n_z = lax.axis_size("rep"), lax.axis_size("seq") // 2
    sib = swap(own, "seq", 1)
    result = [part_of(own, z, core), part_of(sib, z, 1 - core)]
    q = quarter.shape[0]
    for delta in range(1, n_z):
        held = swap(quarter, "seq", 2 * delta)
        for step in range(len(rep_orders(n_rep)[0])):
            held = jnp.concatenate([held, rep_swap(held, step)], axis=0)
        result.append(part_of(held, z ^ delta, core, 0, my_rep, q))
        result.append(part_of(swap(held, "seq", 1), z ^ delta, 1 - core, 0, my_rep, q))
    return result


def part_of(buf, z, core, part=0, rep=0, quarter=0, rows=None):
    return buf, rows or (0, buf.shape[0]), quarter, (z, core, part, rep)


def late_parts(late, own, sib, my_seq, my_rep):
    here, planes = late
    n_rep = lax.axis_size("rep")
    z, core = my_seq // 2, my_seq % 2
    q = here.shape[0] // len(planes)
    result = [part_of(own, z, core), part_of(sib, z, 1 - core)]
    for e in range(n_rep):
        held = swap(here, "rep", e) if e else here
        other = swap(held, "seq", 1)
        for i, plane in enumerate(planes):
            rows = (i * q, q)
            result.append(part_of(held, plane, core, 0, my_rep ^ e, q, rows))
            result.append(part_of(other, plane, 1 - core, 0, my_rep ^ e, q, rows))
    return result


def describe(spans_parts, spd):
    bufs, layout, rows = [], [], []
    for (first, unused), parts in spans_parts:
        for buf, (row, count), quarter, (z, core, part, rep) in parts:
            index = [i for i, b in enumerate(bufs) if b is buf]
            if not index:
                bufs.append(buf)
                index = [len(bufs) - 1]
            layout.append((index[0], row, count, quarter))
            rows += [(z * 2 + core) * spd + first, core, part, rep]
    return jnp.stack([jnp.asarray(r, jnp.int32) for r in rows]), bufs, tuple(layout)


def load_weights(first_block, n_rep, layout, tables, blocks, desc, bufs, w_ref, sems):
    w_i, w_j, held = tables
    for index, (b, row0, count, quarter) in enumerate(layout):
        base, core, part, rep = (desc[4 * index + i] for i in range(4))

        def body(e, carry, buf=bufs[b], row0=row0, quarter=quarter, base=base, core=core, part=part, rep=rep):
            if quarter:
                place = (held[core * n_rep + part + e // quarter] ^ rep) * quarter + e % quarter
            else:
                place = e
            n = blocks[base + place] - first_block

            @pl.when((n >= 0) & (n < PER_LAYER))
            def _():
                row = pl.multiple_of(w_i[n] * B, B)
                col = pl.multiple_of(w_j[n] * B, B)
                mat = (
                    (n >= 27).astype(jnp.int32)
                    + (n >= 36).astype(jnp.int32)
                    + (n >= 72).astype(jnp.int32)
                )
                pltpu.make_async_copy(
                    buf.at[row0 + e], w_ref.at[pl.ds(row, B), pl.ds(col, B)], sems.at[mat]
                ).start()

            return carry

        lax.fori_loop(0, count, body, 0)


def weight_tables(n_rep):
    return [jnp.asarray(t) for t in (W_I, W_J, np.array(sum(held_order(n_rep), []), np.int32))]


def first_fwd_kernel(n_rep, nbuf, quarters, w_i, w_j, held, blocks, desc, x_ref, par, *rest):
    bufs = rest[:nbuf]
    out_ref, cls_ref, qkv_ref, p_ref, r1_ref, r2_ref, gp_ref, lt_ref, w, a_ref, sems = rest[nbuf:]
    first = pl.program_id(0) == 0

    @pl.when(first)
    def _():
        load_weights(0, n_rep, quarters, (w_i, w_j, held), blocks, desc, bufs, w, sems)

    def wait(mat):
        @pl.when(first)
        def _():
            wait_weights(w, sems, mat)

    xb = x_ref[...]
    out = fwd_tile(
        xb.astype(F32), xb, w, par, None, qkv_ref, p_ref, r1_ref, r2_ref, gp_ref, lt_ref, a_ref, wait
    ).astype(BF)
    out_ref[...] = out
    for s in range(TILE // SEG_LEN):
        cls_ref[0, s : s + 1, :] = out[s * SEG_LEN : s * SEG_LEN + 1, :]


def first_fwd(n_rep, weights, tokens, par):
    blocks, desc, bufs, quarters = weights
    rows = tokens.shape[0]
    steps = rows // TILE
    nseg = TILE // SEG_LEN
    return pl.pallas_call(
        functools.partial(first_fwd_kernel, n_rep, len(bufs), quarters),
        grid_spec=pltpu.PrefetchScalarGridSpec(
            num_scalar_prefetch=5,
            grid=(steps,),
            in_specs=[row_spec(D), whole_spec((1, NPAR))] + [any_spec()] * len(bufs),
            out_specs=[
                row_spec(D),
                pl.BlockSpec((1, nseg, D), lambda i, *_: (i, 0, 0)),
                row_spec(3 * D),
                row_spec(NPAIR * 256),
                row_spec(D),
                row_spec(D),
                row_spec(FF),
                pl.BlockSpec((L_ROWS, TILE), lambda i, *_: (0, i)),
            ],
            scratch_shapes=[
                pltpu.VMEM((D, W_COLS), BF),
                pltpu.VMEM((TILE, D), BF),
                pltpu.SemaphoreType.DMA((4,)),
            ],
        ),
        out_shape=[
            jax.ShapeDtypeStruct((rows, D), BF),
            jax.ShapeDtypeStruct((steps, nseg, D), BF),
            jax.ShapeDtypeStruct((rows, 3 * D), BF),
            jax.ShapeDtypeStruct((rows, NPAIR * 256), BF),
            jax.ShapeDtypeStruct((rows, D), F32),
            jax.ShapeDtypeStruct((rows, D), F32),
            jax.ShapeDtypeStruct((rows, FF), BF),
            jax.ShapeDtypeStruct((L_ROWS, rows), BF),
        ],
        compiler_params=params(),
        cost_estimate=cost(15_000_000_000, 60_000_000),
        name="first_forward",
    )(*weight_tables(n_rep), blocks, desc, tokens, par, *bufs)


def first_bwd_kernel(
    n_rep, nbuf, quarters, n_after, w_i, w_j, held, blocks, desc, cot_ref, back_ref, out_ref, par, *rest
):
    qkv_ref, p_ref, r1_ref, r2_ref, gp_ref = rest[:5]
    bufs = rest[5 : 5 + nbuf]
    hid_ref, r_ref, dx_ref, pg_ref, w, da_ref, rows_ref, sems = rest[5 + nbuf + n_after :]
    step = pl.program_id(0)
    first = step == 0

    @pl.when(first)
    def _():
        load_weights(0, n_rep, quarters, (w_i, w_j, held), blocks, desc, bufs, w, sems)
        pg_ref[...] = jnp.zeros_like(pg_ref)
        rows_ref[...] = jnp.sum(back_ref[...].astype(F32), axis=0)

    def wait(mat):
        @pl.when(first)
        def _():
            wait_weights(w, sems, mat)

    dout = cot_ref[...].astype(F32)
    out = out_ref[...]
    index = lax.broadcasted_iota(jnp.int32, (TILE, 1), 0)
    nseg = TILE // SEG_LEN
    for s in range(nseg):
        row = rows_ref[pl.ds(step * nseg + s, 1), :]
        dout = jnp.where(index == s * SEG_LEN, row[:, :D], dout)
        out = jnp.where(index == s * SEG_LEN, row[:, D:], out.astype(F32)).astype(BF)
    hid_ref[...] = out
    dx_ref[...] = bwd_tile(
        dout, w, par, qkv_ref, p_ref, r1_ref, r2_ref, gp_ref, r_ref, pg_ref, da_ref, wait
    )


def first_bwd(n_rep, weights, cot, back, out_one, par, kept, after):
    blocks, desc, bufs, quarters = weights
    rows = cot.shape[0]
    steps = rows // TILE
    nseg = TILE // SEG_LEN
    return pl.pallas_call(
        functools.partial(first_bwd_kernel, n_rep, len(bufs), quarters, len(after)),
        grid_spec=pltpu.PrefetchScalarGridSpec(
            num_scalar_prefetch=5,
            grid=(steps,),
            in_specs=[
                row_spec(D),
                whole_spec(back.shape),
                row_spec(D),
                whole_spec((1, NPAR)),
                row_spec(3 * D),
                row_spec(NPAIR * 256),
                row_spec(D),
                row_spec(D),
                row_spec(FF),
            ]
            + [any_spec()] * (len(bufs) + len(after)),
            out_specs=[row_spec(D), row_spec(R_COLS), row_spec(D), whole_spec((1, NPAR))],
            scratch_shapes=[
                pltpu.VMEM((D, W_COLS), BF),
                pltpu.VMEM((TILE, D), BF),
                pltpu.VMEM((steps * nseg, 2 * D), F32),
                pltpu.SemaphoreType.DMA((4,)),
            ],
        ),
        out_shape=[
            jax.ShapeDtypeStruct((rows, D), BF),
            jax.ShapeDtypeStruct((rows, R_COLS), BF),
            jax.ShapeDtypeStruct((rows, D), F32),
            jax.ShapeDtypeStruct((1, NPAR), F32),
        ],
        compiler_params=params(),
        cost_estimate=cost(30_000_000_000, 60_000_000),
        name="first_backward",
    )(*weight_tables(n_rep), blocks, desc, cot, back, out_one, par, *kept, *bufs, *after)


def second_kernel(
    n_rep, nbuf, quarters, w_i, w_j, held, blocks, desc, doc, got, pos, par, *rest
):
    bufs = rest[:nbuf]
    reply_ref, state_ref, lt_ref, r_ref, dx_ref, pg_ref = rest[nbuf : nbuf + 6]
    w, a_ref, qkv_ref, p_ref, r1_ref, r2_ref, gp_ref, x_ref, cot_ref, sems = rest[nbuf + 6 :]
    load_weights(PER_LAYER, n_rep, quarters, (w_i, w_j, held), blocks, desc, bufs, w, sems)
    pg_ref[...] = jnp.zeros_like(pg_ref)
    reply_ref[...] = jnp.zeros_like(reply_ref)
    x_ref[...] = jnp.zeros_like(x_ref)
    cot_ref[...] = jnp.zeros_like(cot_ref)
    start, length = doc[0], doc[1]
    for j in range(0, DOC_LONG, 16):
        rows = slice(j, j + 16)
        x_ref[rows, :] = pos[rows, :]

        @pl.when(j < length)
        def _(j=j, rows=rows):
            at = pl.ds(pl.multiple_of(start + j, 16), 16)
            x_ref[rows, :] = pos[rows, :] + got[at, :D].astype(F32)
            cot_ref[rows, :] = got[at, D:].astype(F32)

    key = lax.broadcasted_iota(jnp.int32, (1, SEG_LEN), 1)
    key_bias = jnp.where(key < length, 0.0, MASKED_SCORE).astype(F32)
    x32 = x_ref[...]
    y = fwd_tile(
        x32,
        x32.astype(BF),
        w,
        par,
        key_bias,
        qkv_ref,
        p_ref,
        r1_ref,
        r2_ref,
        gp_ref,
        lt_ref,
        a_ref,
        lambda mat: wait_weights(w, sems, mat),
    )
    row = lax.broadcasted_iota(jnp.int32, (SEG_LEN, 1), 0)
    y = jnp.where(row < length, y, 0.0)
    state_ref[...] = y[:DOC_LONG].astype(BF)
    dx = bwd_tile(
        cot_ref[...],
        w,
        par,
        qkv_ref,
        p_ref,
        r1_ref,
        r2_ref,
        gp_ref,
        r_ref,
        pg_ref,
        a_ref,
        lambda mat: None,
    )
    dx = jnp.where(row < length, dx, 0.0)
    dx_ref[...] = dx[:DOC_LONG]
    for j in range(0, DOC_LONG, 16):

        @pl.when(j < length)
        def _(j=j):
            at = pl.ds(pl.multiple_of(start + j, 16), 16)
            reply_ref[at, :D] = dx[j : j + 16].astype(BF)
            reply_ref[at, D:] = y[j : j + 16].astype(BF)


def second_layer(n_rep, weights, doc, got, pos, par):
    blocks, desc, bufs, quarters = weights
    rows = SEG_LEN
    group = got.shape[0]
    return pl.pallas_call(
        functools.partial(second_kernel, n_rep, len(bufs), quarters),
        in_specs=[smem_spec()] * 6 + [vmem_spec()] * 3 + [any_spec()] * len(bufs),
        out_specs=[vmem_spec()] * 6,
        scratch_shapes=[
            pltpu.VMEM((D, W_COLS), BF),
            pltpu.VMEM((rows, D), BF),
            pltpu.VMEM((rows, 3 * D), BF),
            pltpu.VMEM((rows, NPAIR * 256), BF),
            pltpu.VMEM((rows, D), F32),
            pltpu.VMEM((rows, D), F32),
            pltpu.VMEM((rows, FF), BF),
            pltpu.VMEM((rows, D), F32),
            pltpu.VMEM((rows, D), F32),
            pltpu.SemaphoreType.DMA((4,)),
        ],
        out_shape=[
            jax.ShapeDtypeStruct((group, 2 * D), BF),
            jax.ShapeDtypeStruct((DOC_LONG, D), BF),
            jax.ShapeDtypeStruct((L_ROWS, rows), BF),
            jax.ShapeDtypeStruct((rows, R_COLS), BF),
            jax.ShapeDtypeStruct((DOC_LONG, D), F32),
            jax.ShapeDtypeStruct((1, NPAR), F32),
        ],
        compiler_params=params(),
        cost_estimate=cost(8_000_000_000, 40_000_000),
        name="second_layer",
    )(*weight_tables(n_rep), blocks, desc, doc, got, pos, par, *bufs)


PRODUCTS = (
    (L_X, R_QKV, 9, 0),
    (L_A, R_OUT, 3, 27),
    (L_H, R_UP, 12, 36),
    (L_E, R_DOWN, 3, 72),
    (L_E + D, R_DOWN, 3, 81),
    (L_E + 2 * D, R_DOWN, 3, 90),
    (L_E + 3 * D, R_DOWN, 3, 99),
)


def send_block(src, n, ctx, where, info, outs, sem):
    spd, unused, chunks = ctx
    at = where[n]
    owner = at // spd
    k = at % spd
    target = (owner // 2) ^ (info[0] // 2)
    mine = (owner % 2) == (info[0] % 2)
    for c, (first, m) in enumerate(chunks):
        inside = (k >= first) & (k < first + m)
        for side, cond in ((0, inside & jnp.logical_not(mine)), (1, inside & mine)):

            @pl.when(cond)
            def _(c=c, side=side, first=first):
                pltpu.make_async_copy(src, outs[2 * c + side].at[target, k - first], sem).start()


def all_products(lt, r, stage, base, ctx, where, info, outs, sem, before=None):
    for lrow, rcol, across, first in PRODUCTS:
        if before is not None:
            before(lrow)
        for j in range(across):
            value = mm(lt[lrow : lrow + D, :], r[:, rcol + j * B : rcol + (j + 1) * B]).astype(BF)
            for i in range(D // B):
                local = first + i * across + j
                stage[local] = value[i * B : (i + 1) * B]
                send_block(stage.at[local], base + local, ctx, where, info, outs, sem)


def wait_blocks(stage, sem, count):
    part = stage.at[pl.ds(0, count)]
    pltpu.make_async_copy(part, part, sem).wait()


def second_grad_kernel(ctx, n_empty, n_after, where, info, lt, r, *rest):
    outs, (stage, zero, sem) = rest[n_after:-3], rest[-3:]
    zero[...] = jnp.zeros_like(zero)
    for n in range(NBLK, NBLK + n_empty):
        send_block(zero.at[n - NBLK], n, ctx, where, info, outs, sem)
    all_products(lt, r, stage, PER_LAYER, ctx, where, info, outs, sem)
    wait_blocks(stage, sem, PER_LAYER)
    if n_empty:
        wait_blocks(zero, sem, n_empty)


def chunk_arrays(ctx):
    return [jax.ShapeDtypeStruct((ctx[1], m, B, B), BF) for unused, m in ctx[2] for side in range(2)]


def second_grad(ctx, where, info, lt, r, after):
    shapes = chunk_arrays(ctx)
    n_empty = where.shape[0] - NBLK
    return pl.pallas_call(
        functools.partial(second_grad_kernel, ctx, n_empty, len(after)),
        in_specs=[smem_spec()] * 2 + [vmem_spec()] * 2 + [any_spec()] * len(after),
        out_specs=[any_spec()] * len(shapes),
        out_shape=shapes,
        scratch_shapes=[
            pltpu.VMEM((PER_LAYER, B, B), BF),
            pltpu.VMEM((max(n_empty, 1), B, B), BF),
            pltpu.SemaphoreType.DMA(()),
        ],
        compiler_params=params(),
        cost_estimate=cost(2_000_000_000, 18_000_000),
        name="second_gradients",
    )(where, info, lt, r, *after)


def first_grad_kernel(ctx, n_after, where, info, lt, r, *rest):
    n_out = 2 * len(ctx[2])
    outs = rest[n_out + n_after : 2 * n_out + n_after]
    lt_s, r_s, stage, sem, sems = rest[2 * n_out + n_after :]
    spans = ((L_X, L_A, R_QKV, R_OUT), (L_A, L_H, R_OUT, R_UP), (L_H, L_E, R_UP, R_DOWN), (L_E, L_ROWS, R_DOWN, R_COLS))
    copies = []
    for i, (la, lb, ra, rb) in enumerate(spans):
        pair = (
            pltpu.make_async_copy(lt.at[la:lb], lt_s.at[la:lb], sems.at[2 * i]),
            pltpu.make_async_copy(r.at[:, ra:rb], r_s.at[:, ra:rb], sems.at[2 * i + 1]),
        )
        for copy in pair:
            copy.start()
        copies.append((la, pair))

    def before(lrow):
        for la, pair in copies:
            if la == lrow:
                for copy in pair:
                    copy.wait()

    all_products(lt_s, r_s, stage, 0, ctx, where, info, outs, sem, before)
    wait_blocks(stage, sem, PER_LAYER)


def first_grad(ctx, where, info, lt, r, arrays, after):
    n = len(arrays)
    return pl.pallas_call(
        functools.partial(first_grad_kernel, ctx, len(after)),
        in_specs=[smem_spec()] * 2 + [any_spec()] * (2 + n + len(after)),
        out_specs=[any_spec()] * n,
        out_shape=[jax.ShapeDtypeStruct(a.shape, BF) for a in arrays],
        scratch_shapes=[
            pltpu.VMEM(lt.shape, BF),
            pltpu.VMEM(r.shape, BF),
            pltpu.VMEM((PER_LAYER, B, B), BF),
            pltpu.SemaphoreType.DMA(()),
            pltpu.SemaphoreType.DMA((8,)),
        ],
        input_output_aliases={4 + i: i for i in range(n)},
        compiler_params=params(),
        cost_estimate=cost(15_000_000_000, 40_000_000),
        name="first_gradients",
    )(where, info, lt, r, *arrays, *after)


def halve_kernel(step, n_after, info, a_ref, b_ref, *rest):
    send_ref, keep_ref = rest[n_after:]
    half = send_ref.shape[2]
    high = high_bit(info, step)
    for side, ref in ((1 - high, send_ref), (high, keep_ref)):
        rows = pl.ds(pl.multiple_of(side * half, half), half)
        ref[...] = a_ref[:, :, rows, :] + b_ref[:, :, rows, :]


def high_bit(info, step):
    orders = rep_orders(4)
    core, rep = info[0] % 2, info[1]
    bit = jnp.where(core == 0, orders[0][step], orders[1][step])
    return jnp.where((rep & bit) != 0, 1, 0)


def halve(info, step, a, b, after):
    n_target, m, rows, cols = a.shape
    shape = jax.ShapeDtypeStruct((n_target, m, rows // 2, cols), BF)
    group = 2 if n_target * m <= 64 else 1

    def spec(r):
        return pl.BlockSpec((group, m, r, cols), lambda i, *_: (i, 0, 0, 0))

    return pl.pallas_call(
        functools.partial(halve_kernel, step, len(after)),
        grid_spec=pltpu.PrefetchScalarGridSpec(
            num_scalar_prefetch=1,
            grid=(n_target // group,),
            in_specs=[spec(rows)] * 2 + [any_spec()] * len(after),
            out_specs=[spec(rows // 2)] * 2,
        ),
        out_shape=[shape, shape],
        compiler_params=params(),
        cost_estimate=cost(1, 1),
        name="halve",
    )(info, a, b, *after)


def spread_kernel(n_after, a_ref, b_ref, *rest):
    for i, out in enumerate(rest[n_after:]):
        out[...] = a_ref[i] + b_ref[i]


def spread(a, b, after):
    shape = jax.ShapeDtypeStruct(a.shape[1:], BF)
    return pl.pallas_call(
        functools.partial(spread_kernel, len(after)),
        in_specs=[vmem_spec()] * 2 + [any_spec()] * len(after),
        out_specs=[vmem_spec()] * a.shape[0],
        out_shape=[shape] * a.shape[0],
        compiler_params=params(),
        cost_estimate=cost(1, 1),
        name="spread",
    )(a, b, *after)


def total_kernel(count, *rest):
    total = rest[0][...].astype(F32)
    for ref in rest[1:count]:
        total = total + ref[...].astype(F32)
    rest[-1][...] = total.astype(BF)


def total(parts, after):
    shape = jax.ShapeDtypeStruct(parts[0].shape, BF)
    return pl.pallas_call(
        functools.partial(total_kernel, len(parts)),
        in_specs=[vmem_spec()] * len(parts) + [any_spec()] * len(after),
        out_specs=vmem_spec(),
        out_shape=shape,
        compiler_params=params(),
        cost_estimate=cost(1, 1),
        name="total",
    )(*parts, *after)


def shampoo_kernel(n_rep, spd, first, n_previous, order, info, *rest):
    pieces, stats = rest[:n_rep], rest[n_rep : n_rep + 5]
    outs, token, (ins_ref, outs_ref, g_ref, ins_sem, outs_sem) = rest[-10:-6], rest[-6], rest[-5:]
    token[...] = jnp.zeros_like(token)
    count = pieces[0].shape[0]
    slots = [order[info[0] * spd + first + i] for i in range(count)]
    for i, slot in enumerate(slots):
        for a, stat in enumerate(stats):
            pltpu.make_async_copy(stat.at[slot], ins_ref.at[i, a], ins_sem.at[i]).start()
    orders = rep_orders(n_rep)
    size = B // n_rep
    places = []
    for e in range(n_rep):
        rep = info[1] ^ e
        place = jnp.int32(0)
        for level in range(len(orders[0])):
            bit = jnp.where(info[0] % 2 == 0, orders[0][level], orders[1][level])
            place = place + jnp.where((rep & bit) != 0, B >> (level + 1), 0)
        places.append(pl.multiple_of(place, size))
    for i, slot in enumerate(slots):
        for place, piece in zip(places, pieces):
            g_ref[i, pl.ds(place, size), :] = piece[i]
        g = g_ref[i]
        pltpu.make_async_copy(ins_ref.at[i], ins_ref.at[i], ins_sem.at[i]).wait()
        left, right, lroot, rroot, master = (ins_ref[i, a] for a in range(5))
        part = mm(lroot.astype(BF), g)
        outs_ref[i, 0] = g.astype(F32)
        outs_ref[i, 1] = DECAY * left + (1.0 - DECAY) * mm_t(g, g)
        outs_ref[i, 2] = DECAY * right + (1.0 - DECAY) * tmm(g, g)
        direction = mm(part.astype(BF), rroot.astype(BF))
        scale = BLOCK_RATE * lax.rsqrt(jnp.mean(direction * direction) + RMS_EPS)
        outs_ref[i, 3] = master - direction * scale
        for a, out in enumerate(outs):
            pltpu.make_async_copy(outs_ref.at[i, a], out.at[slot], outs_sem).start()
    pltpu.make_async_copy(outs_ref, outs_ref, outs_sem).wait()


def shampoo(order, info, spd, first, pieces, stats, previous, after):
    count = pieces[0].shape[0]
    n_rep = len(pieces)
    n_in = 2 + n_rep + len(stats)
    return pl.pallas_call(
        functools.partial(shampoo_kernel, n_rep, spd, first, len(previous)),
        in_specs=[smem_spec()] * 2
        + [vmem_spec()] * n_rep
        + [any_spec()] * (len(stats) + len(previous) + len(after)),
        out_specs=[any_spec()] * 4 + [vmem_spec()],
        out_shape=[jax.ShapeDtypeStruct((spd, B, B), F32)] * 4 + [jax.ShapeDtypeStruct((8, 128), F32)],
        scratch_shapes=[
            pltpu.VMEM((count, 5, B, B), F32),
            pltpu.VMEM((count, 4, B, B), F32),
            pltpu.VMEM((count, B, B), BF),
            pltpu.SemaphoreType.DMA((count,)),
            pltpu.SemaphoreType.DMA(()),
        ],
        input_output_aliases={n_in + i: i for i in range(len(previous))},
        compiler_params=params(),
        cost_estimate=cost(1, 1),
        name="shampoo",
    )(order, info, *pieces, *stats, *previous, *after)


def reduce_pipeline(ctx, chunks, ready, idle, stats, after):
    order, info, spd, n_rep = ctx
    state = {}
    results = ()
    for batch in range(len(chunks) + 6):
        for run in ready.get(batch, ()):
            after = run(after)
        for i in range(len(chunks))[::-1]:
            stage = batch - i
            if chunks[i] is None or stage < 1:
                continue
            first, m, products = chunks[i]
            if stage == 1:
                got, own = state[i]
                send, keep = halve(info, 0, own, got, after)
                state[i] = (rep_swap(send, 0), keep)
                after = (keep,)
            elif stage == 2:
                got, kept = state[i]
                send, keep = halve(info, 1, kept, got, after)
                state[i] = (rep_swap(send, 1), keep)
                after = (keep,)
            elif stage == 3:
                got, kept = state[i]
                parts = spread(kept, got, after)
                moved = [swap(part, "seq", 2 * d) for d, part in enumerate(parts) if d]
                state[i] = [parts[0]] + moved
                after = (parts[0],)
            elif stage == 4:
                mine = total(state[i], after)
                state[i] = [mine] + [swap(mine, "rep", e) for e in range(1, n_rep)]
                after = (mine,)
        done = batch - 6
        if 0 <= done < len(chunks) and chunks[done] is not None:
            first = chunks[done][0]
            *results, token = shampoo(order, info, spd, first, state[done], stats, results, after)
            after = (token,)
        for run in idle.get(batch, ()):
            after = run(after)
        if batch < len(chunks) and chunks[batch] is not None:
            sib, own = chunks[batch][2]()
            state[batch] = (swap(sib, "seq", 1), own)
    return results, after


def small_kernel(old, grads, *rest):
    out = rest[-1]
    rows = 2 * NPAR // 128
    for part in (slice(0, rows), slice(rows, None)):
        g = grads[part, :]
        out[part, :] = old[part, :] - SMALL_RATE * g * lax.rsqrt(jnp.mean(g * g) + RMS_EPS)


def add_kernel(a, b, *rest):
    rest[-1][...] = a[...] + b[...]


def add(a, b, after):
    return pl.pallas_call(
        add_kernel,
        in_specs=[vmem_spec()] * 2 + [any_spec()] * len(after),
        out_specs=vmem_spec(),
        out_shape=jax.ShapeDtypeStruct(a.shape, F32),
        compiler_params=params(),
        cost_estimate=cost(1, 1),
        name="add",
    )(a, b, *after)


def small_step(old, grads, after):
    shape = (old.shape[0] // 128, 128)
    return pl.pallas_call(
        small_kernel,
        in_specs=[vmem_spec()] * 2 + [any_spec()] * len(after),
        out_specs=vmem_spec(),
        out_shape=jax.ShapeDtypeStruct(shape, F32),
        compiler_params=params(),
        cost_estimate=cost(1, 1_000_000),
        name="small_step",
    )(old.reshape(shape), grads.reshape(shape), *after).reshape(-1)


def split_slots(spd):
    if spd == 28:
        return ((0, 20), (20, 8)), ((0, 10), (10, 10), (20, 8))
    return ((0, spd),), ((0, spd),)


def shards(
    tokens,
    cotangent,
    doc_lengths,
    doc_owners,
    small_params,
    slot_block,
    master_blocks,
    left_stats,
    right_stats,
    left_roots,
    right_roots,
):
    seg_dev = tokens.shape[0] // SEG_LEN
    n_seq, n_rep = lax.axis_size("seq"), lax.axis_size("rep")
    my_seq = lax.axis_index("seq").astype(jnp.int32)
    my_rep = lax.axis_index("rep").astype(jnp.int32)
    spd = master_blocks.shape[0]
    n_target = n_seq // 2
    info = jnp.stack([my_seq, my_rep])
    par_one = small_params[None, :NPAR]
    par_two = small_params[None, NPAR : 2 * NPAR]
    position = small_params[2 * NPAR :].reshape(DOC_LONG, D)

    line = n_seq == 8 and n_rep == 4 and spd == 28
    spans, chunk_spans = split_slots(spd) if line else (((0, spd),), ((0, spd),))
    ctx = (spd, n_target, chunk_spans)
    quarter, extra = quarter_blocks(slot_block, info, master_blocks, spans, n_rep)

    lengths_row = doc_lengths[0]
    owners_row = doc_owners[0]
    starts_row = jnp.cumsum(lengths_row) - lengths_row
    first_seg = my_seq * seg_dev
    inside = (starts_row <= first_seg) & (first_seg < starts_row + lengths_row)
    owner = jnp.sum(jnp.where(inside, owners_row, 0))
    target = (jnp.arange(n_seq, dtype=jnp.int32) == owner).astype(BF)[:, None, None]
    mine = (owners_row == my_seq) & (lengths_row > 0)
    doc = jnp.stack([jnp.sum(jnp.where(mine, starts_row, 0)), jnp.sum(jnp.where(mine, lengths_row, 0))])
    doc = doc.astype(jnp.int32)

    def to_owner(rows):
        sent = target * rows[None]
        got = lax.all_to_all(sent, "seq", split_axis=0, concat_axis=0, tiled=True)
        return got.reshape(n_seq * seg_dev, 2 * D)

    cot_first = cotangent.reshape(seg_dev, SEG_LEN, D)[:, 0, :]

    def plan(after):
        early = (after, par_one, par_two, position, target, doc, cot_first)
        return plan_slots(slot_block, info, master_blocks, spans, n_seq, early)

    stats = (left_stats, right_stats, left_roots, right_roots, master_blocks)
    if line:
        (order, blocks, where, owns), parts_one, late = gather_line(
            quarter, extra, info, my_seq, plan
        )
        late_sib = swap(owns[1], "seq", 1)
    else:
        order, blocks, where, *owns = plan(quarter)
        parts_one, late, late_sib = gather_direct(quarter, owns[0], my_seq, my_rep), None, None

    def layers(ahead):
        layers_parts = [(spans[0], parts_one)]
        first_parts = list(layers_parts)

        if line:
            layers_parts.append((spans[1], late_parts(late, owns[1], late_sib, my_seq, my_rep)))
        if not ahead:
            first_parts = layers_parts
        first_desc, first_bufs, first_layout = describe(first_parts, spd)
        one = (blocks, first_desc, first_bufs, first_layout)
        out_one, cls, *kept, lt_one = first_fwd(n_rep, one, tokens, par_one)
        second_desc, second_bufs, second_layout = describe(layers_parts, spd)
        two = (blocks, second_desc, second_bufs, second_layout)
        got = to_owner(jnp.concatenate([cls.reshape(seg_dev, D), cot_first], axis=1))
        reply, states, lt_two, r_two, grad_pos, pg_two = second_layer(
            n_rep, two, doc, got, position, par_two
        )
        arrays = second_grad(ctx, where, info, lt_two, r_two, ())
        back = lax.all_to_all(
            reply.reshape(n_seq, seg_dev, 2 * D), "seq", split_axis=0, concat_axis=0, tiled=True
        )
        box = {}

        def backward(after):
            box["bwd"] = first_bwd(n_rep, one, cotangent, back, out_one, par_one, kept, after)
            pg_one = box["bwd"][3]
            local = jnp.concatenate([pg_one[0], pg_two[0], grad_pos.reshape(-1)]).reshape(2, -1, 128)
            box["sum"] = lax.dynamic_index_in_dim(local, my_seq % 2, 0, False)
            box["got"] = swap(lax.dynamic_index_in_dim(local, 1 - my_seq % 2, 0, False), "seq", 1)
            return (box["bwd"][1],)

        routes = [("seq", 2 << b) for b in range((n_seq // 2).bit_length() - 1)][::-1]
        routes += [("rep", 1 << b) for b in range(n_rep.bit_length() - 1)][::-1]

        def small_hop(axis, bit):
            def run(after):
                box["sum"] = add(box["sum"], box["got"], after)
                box["got"] = swap(box["sum"], axis, bit)
                return (box["sum"],)

            return run

        per = 2
        n_done = per if ahead else 0

        def late_products(after):
            some, done = arrays[: len(arrays) - n_done], arrays[len(arrays) - n_done :]
            sub = (spd, n_target, chunk_spans[: len(some) // per])
            made = first_grad(sub, where, info, lt_one, box["bwd"][1], some, after)
            box["all"] = list(made) + list(done)
            return (made[1],)

        def chunk(c):
            return lambda: box["all"][per * c : per * c + per]

        chunks = [(first, m, chunk(c)) for c, (first, m) in enumerate(chunk_spans)]
        if ahead:
            early = chunks[-1][:2] + (lambda: arrays[-per:],)
            chunks = [early, None] + chunks[:-1]
            ready, idle = {}, {1: [backward], 2: [late_products]}
        else:
            ready, idle = {0: [backward, late_products]}, {}
        n = len(chunks)
        for at, route in zip([3, 5, 7, 8, 9, 10, 11], routes):
            idle.setdefault(at, []).append(small_hop(*route))
        results, after = reduce_pipeline(
            (order, info, spd, n_rep), chunks, ready, idle, stats, (arrays[0],)
        )
        core = my_seq % 2
        mine = add(box["sum"], box["got"], after)
        theirs = swap(mine, "seq", 1)
        small_grads = jnp.where(
            core == 0, jnp.concatenate([mine, theirs]), jnp.concatenate([theirs, mine])
        ).reshape(-1)
        new_small = small_step(small_params, small_grads, ())
        hidden_out, unused, input_grad, unused = box["bwd"]
        return (hidden_out, input_grad, states[None], *results, small_grads, new_small)

    if not line:
        return layers(False)
    counts = jnp.sum((slot_block.reshape(n_seq, spd) < PER_LAYER).astype(jnp.int32), axis=1)
    return lax.cond(jnp.all(counts <= spans[0][1]), lambda: layers(True), lambda: layers(False))


def solution(mesh):
    in_specs = (
        P(("rep", "seq"), None),
        P(("rep", "seq"), None),
        P("rep", None),
        P("rep", None),
        P(),
        P(),
        P("seq", None, None),
        P("seq", None, None),
        P("seq", None, None),
        P("seq", None, None),
        P("seq", None, None),
    )
    out_specs = (
        P(("rep", "seq"), None),
        P(("rep", "seq"), None),
        P(("rep", "seq"), None, None),
        P("seq", None, None),
        P("seq", None, None),
        P("seq", None, None),
        P("seq", None, None),
        P(),
        P(),
    )
    return jax.shard_map(shards, mesh=mesh, in_specs=in_specs, out_specs=out_specs, check_vma=False)
```

```python
import functools

import jax
import jax.numpy as jnp
import numpy as np
from jax import lax
from jax.experimental import pallas as pl
from jax.experimental.pallas import tpu as pltpu
from jax.sharding import PartitionSpec as P

D = 768
HEAD_DIM = 64
FF = 3072
SEG_LEN = 128
DOC_LONG = 64
B = 256
PER_LAYER = 108
NBLK = 2 * PER_LAYER
NPAR = 8 * D + FF
NPAIR = D // 128

NORM_EPS = 1e-05
RMS_EPS = 1e-06
DECAY = 0.5
BLOCK_RATE = 0.02
SMALL_RATE = 0.1
MASKED_SCORE = -1000000000.0
SCALE = HEAD_DIM**-0.5

C_QKV, C_OUT, C_UP, C_DOWN, W_COLS = 0, 3 * D, 4 * D, 4 * D + FF, 4 * D + 2 * FF
W_SPANS = ((C_QKV, C_OUT), (C_OUT, C_UP), (C_UP, C_DOWN), (C_DOWN, W_COLS))
L_X, L_A, L_H, L_E, L_ROWS = 0, D, 2 * D, 3 * D, 3 * D + FF
R_QKV, R_OUT, R_UP, R_DOWN, R_COLS = 0, 3 * D, 4 * D, 4 * D + FF, 5 * D + FF
O_BQ, O_BV, O_BO, O_G1, O_C1, O_B1 = 0, D, 2 * D, 3 * D, 4 * D, 5 * D
O_B2, O_G2, O_C2 = 5 * D + FF, 6 * D + FF, 7 * D + FF

VMEM_LIMIT = 60 * 1024 * 1024
BF = jnp.bfloat16
F32 = jnp.float32


def block_tables():
    w_i, w_j, l_i, r_j = [], [], [], []
    for i in range(3):
        for j in range(9):
            w_i.append(i), w_j.append(j), l_i.append(i), r_j.append(j)
    for i in range(3):
        for j in range(3):
            w_i.append(i), w_j.append(9 + j), l_i.append(3 + i), r_j.append(9 + j)
    for i in range(3):
        for j in range(12):
            w_i.append(i), w_j.append(12 + j), l_i.append(6 + i), r_j.append(12 + j)
    for i in range(12):
        for j in range(3):
            w_i.append(i % 3), w_j.append(24 + 3 * (i // 3) + j)
            l_i.append(9 + i), r_j.append(24 + j)
    w_i = [i + 4 * ((n >= 27) + (n >= 36) + (n >= 72)) for n, i in enumerate(w_i)]
    return [np.array(t, np.int32) for t in (w_i, w_j, l_i, r_j)]


W_I, W_J, L_I, R_J = block_tables()


def mm(a, b):
    return jnp.dot(a, b, preferred_element_type=F32)


def mm_t(a, b):
    return lax.dot_general(a, b, (((1,), (1,)), ((), ())), preferred_element_type=F32)


def tmm(a, b):
    return lax.dot_general(a, b, (((0,), (0,)), ((), ())), preferred_element_type=F32)


def norm_parts(values):
    center = values - jnp.mean(values, axis=-1, keepdims=True)
    spread = jnp.mean(center * center, axis=-1, keepdims=True)
    scale = lax.rsqrt(spread + NORM_EPS)
    return center * scale, scale


def gelu_parts(u):
    cdf = 0.5 + 0.5 * lax.erf(u * 0.7071067811865476)
    return u * cdf, cdf + u * jnp.exp(-0.5 * u * u) * 0.3989422804014327


def head_masks():
    lane = lax.broadcasted_iota(jnp.int32, (1, 128), 1)
    first = jnp.where(lane < HEAD_DIM, 1.0, 0.0).astype(BF)
    return first, (1.0 - first.astype(F32)).astype(BF)


def stack_heads(pair, masks):
    return jnp.concatenate([pair * masks[0], pair * masks[1]], axis=0)


def beside(stacked):
    half = stacked.shape[0] // 2
    return jnp.concatenate([stacked[:half], stacked[half:]], axis=1)


def wait_weights(w_ref, sems, mat):
    lo, hi = W_SPANS[mat]
    part = w_ref.at[:, lo:hi]
    pltpu.make_async_copy(part, part, sems.at[mat]).wait()


def fwd_tile(x32, xb, w, par, key_bias, qkv_ref, p_ref, r1_ref, r2_ref, gp_ref, lt_ref, a_ref, wait):
    n_rows = xb.shape[0]
    lt_ref[L_X : L_X + D, :] = xb.T
    wait(0)
    for c, off in ((0, O_BQ), (1, None), (2, O_BV)):
        part = mm(xb, w[:, C_QKV + c * D : C_QKV + (c + 1) * D])
        if off is not None:
            part = part + par[:, off : off + D]
        qkv_ref[:, c * D : (c + 1) * D] = part.astype(BF)
    masks = head_masks()
    for s in range(n_rows // SEG_LEN):
        rows = slice(s * SEG_LEN, (s + 1) * SEG_LEN)
        for h in range(NPAIR):
            q = qkv_ref[rows, h * 128 : (h + 1) * 128]
            k = qkv_ref[rows, D + h * 128 : D + (h + 1) * 128]
            v = qkv_ref[rows, 2 * D + h * 128 : 2 * D + (h + 1) * 128]
            scores = mm_t(stack_heads(q, masks), k) * SCALE
            if key_bias is not None:
                scores = scores + key_bias
            exps = jnp.exp(scores - jnp.max(scores, axis=-1, keepdims=True))
            probs = exps * (1.0 / jnp.sum(exps, axis=-1, keepdims=True))
            probs = beside(probs.astype(BF))
            p_ref[rows, h * 256 : (h + 1) * 256] = probs
            a_ref[rows, h * 128 : (h + 1) * 128] = mm(probs, stack_heads(v, masks)).astype(BF)
    a = a_ref[...]
    lt_ref[L_A : L_A + D, :] = a.T
    wait(1)
    r1 = x32 + (mm(a, w[:, C_OUT : C_OUT + D]) + par[:, O_BO : O_BO + D])
    r1_ref[...] = r1
    xhat, unused = norm_parts(r1)
    h = xhat * par[:, O_G1 : O_G1 + D] + par[:, O_C1 : O_C1 + D]
    hb = h.astype(BF)
    lt_ref[L_H : L_H + D, :] = hb.T
    wait(2)
    total = h + par[:, O_B2 : O_B2 + D]
    for c in range(FF // D):
        u = mm(hb, w[:, C_UP + c * D : C_UP + (c + 1) * D]) + par[:, O_B1 + c * D : O_B1 + (c + 1) * D]
        e, gp = gelu_parts(u)
        gp_ref[:, c * D : (c + 1) * D] = gp.astype(BF)
        eb = e.astype(BF)
        lt_ref[L_E + c * D : L_E + (c + 1) * D, :] = eb.T
        if c == 0:
            wait(3)
        total = total + mm(eb, w[:, C_DOWN + c * D : C_DOWN + (c + 1) * D])
    r2_ref[...] = total
    xhat, unused = norm_parts(total)
    return xhat * par[:, O_G2 : O_G2 + D] + par[:, O_C2 : O_C2 + D]


def col_sum(values):
    return jnp.sum(values.astype(F32), axis=0, keepdims=True)


def norm_back(dout, values, gain):
    xhat, scale = norm_parts(values)
    dxhat = dout * gain
    mean_one = jnp.mean(dxhat, axis=-1, keepdims=True)
    mean_two = jnp.mean(dxhat * xhat, axis=-1, keepdims=True)
    return scale * (dxhat - mean_one - xhat * mean_two), col_sum(dout * xhat), col_sum(dout)


def bwd_tile(dout, w, par, qkv_ref, p_ref, r1_ref, r2_ref, gp_ref, r_ref, pg_ref, da_ref, wait):
    n_rows = dout.shape[0]

    def add_small(off, value):
        pg_ref[:, off : off + value.shape[1]] += value

    dr2, dgain, dshift = norm_back(dout, r2_ref[...], par[:, O_G2 : O_G2 + D])
    add_small(O_G2, dgain)
    add_small(O_C2, dshift)
    dy = dr2.astype(BF)
    r_ref[:, R_DOWN : R_DOWN + D] = dy
    add_small(O_B2, col_sum(dy))
    wait(3)
    dh = dr2
    for c in range(FF // D):
        de = mm_t(dy, w[:, C_DOWN + c * D : C_DOWN + (c + 1) * D])
        du = (gp_ref[:, c * D : (c + 1) * D].astype(F32) * de).astype(BF)
        r_ref[:, R_UP + c * D : R_UP + (c + 1) * D] = du
        add_small(O_B1 + c * D, col_sum(du))
        if c == 0:
            wait(2)
        dh = dh + mm_t(du, w[:, C_UP + c * D : C_UP + (c + 1) * D])
    dr1, dgain, dshift = norm_back(dh, r1_ref[...], par[:, O_G1 : O_G1 + D])
    add_small(O_G1, dgain)
    add_small(O_C1, dshift)
    do = dr1.astype(BF)
    r_ref[:, R_OUT : R_OUT + D] = do
    add_small(O_BO, col_sum(do))
    wait(1)
    da_ref[...] = mm_t(do, w[:, C_OUT : C_OUT + D]).astype(BF)
    masks = head_masks()
    for s in range(n_rows // SEG_LEN):
        rows = slice(s * SEG_LEN, (s + 1) * SEG_LEN)
        for h in range(NPAIR):
            q = qkv_ref[rows, h * 128 : (h + 1) * 128]
            k = qkv_ref[rows, D + h * 128 : D + (h + 1) * 128]
            v = qkv_ref[rows, 2 * D + h * 128 : 2 * D + (h + 1) * 128]
            probs = jnp.concatenate(
                [p_ref[rows, h * 256 : h * 256 + 128], p_ref[rows, h * 256 + 128 : h * 256 + 256]], axis=0
            )
            da = stack_heads(da_ref[rows, h * 128 : (h + 1) * 128], masks)
            dprobs = mm_t(da, v)
            dv = tmm(probs, da)
            probs = probs.astype(F32)
            inner = jnp.sum(dprobs * probs, axis=-1, keepdims=True)
            dscores = (probs * (dprobs - inner) * SCALE).astype(BF)
            dq = mm(beside(dscores), stack_heads(k, masks))
            dk = tmm(dscores, stack_heads(q, masks))
            r_ref[rows, h * 128 : (h + 1) * 128] = dq.astype(BF)
            r_ref[rows, D + h * 128 : D + (h + 1) * 128] = dk.astype(BF)
            r_ref[rows, 2 * D + h * 128 : 2 * D + (h + 1) * 128] = dv.astype(BF)
    add_small(O_BQ, col_sum(r_ref[:, 0:D]))
    add_small(O_BV, col_sum(r_ref[:, 2 * D : 3 * D]))
    wait(0)
    return dr1 + mm_t(r_ref[:, R_QKV : R_QKV + 3 * D], w[:, C_QKV : C_QKV + 3 * D])


TILE = 256


def any_spec():
    return pl.BlockSpec(memory_space=pl.ANY)


def smem_spec():
    return pl.BlockSpec(memory_space=pltpu.SMEM)


def vmem_spec():
    return pl.BlockSpec(memory_space=pltpu.VMEM)


def row_spec(width, tile=TILE):
    return pl.BlockSpec((tile, width), lambda i, *_: (i, 0))


def whole_spec(shape):
    return pl.BlockSpec(shape, lambda i, *_: (0,) * len(shape))


def params():
    return pltpu.CompilerParams(vmem_limit_bytes=VMEM_LIMIT)


def cost(flops, nbytes):
    return pl.CostEstimate(flops=flops, bytes_accessed=nbytes, transcendentals=0)


def sort_slots(slot_block, base, order, at, spd):
    def first(j, count):
        take = slot_block[base + j] < PER_LAYER

        @pl.when(take)
        def _():
            order[at + count] = j

        return count + take.astype(jnp.int32)

    def second(j, count):
        take = slot_block[base + j] >= PER_LAYER

        @pl.when(take)
        def _():
            order[at + count] = j

        return count + take.astype(jnp.int32)

    lax.fori_loop(0, spd, second, lax.fori_loop(0, spd, first, 0))


def quarter_kernel(spd, n_rep, spans, slot_block, info, master, out, extra, order, stage, sem):
    sort_slots(slot_block, info[0] * spd, order, 0, spd)
    at = 0
    for lo, count in spans:
        quarter = count // n_rep
        for i in range(quarter):
            slot = order[lo + info[1] * quarter + i]
            pltpu.make_async_copy(master.at[slot], stage.at[at], sem).start()
            at += 1
    pltpu.make_async_copy(stage, stage, sem).wait()
    for i in range(at):
        if i < out.shape[0]:
            out[i] = stage[i].astype(BF)
        else:
            extra[i - out.shape[0]] = stage[i].astype(BF)


def quarter_blocks(slot_block, info, master, spans, n_rep):
    spd = master.shape[0]
    total_rows = spd // n_rep
    return pl.pallas_call(
        functools.partial(quarter_kernel, spd, n_rep, spans),
        in_specs=[smem_spec(), smem_spec(), any_spec()],
        out_specs=[vmem_spec()] * 2,
        out_shape=[
            jax.ShapeDtypeStruct((spans[0][1] // n_rep, B, B), BF),
            jax.ShapeDtypeStruct((max(total_rows - spans[0][1] // n_rep, 1), B, B), BF),
        ],
        scratch_shapes=[
            pltpu.SMEM((spd,), jnp.int32),
            pltpu.VMEM((total_rows, B, B), F32),
            pltpu.SemaphoreType.DMA(()),
        ],
        compiler_params=params(),
        cost_estimate=cost(1, 3_000_000),
        name="quarter_blocks",
    )(slot_block, info, master)


def plan_kernel(spd, n_seq, spans, n_after, slot_block, info, master, *rest):
    order, blocks, where, *rest = rest[n_after:]
    outs, (stage, sem) = rest[: len(spans)], rest[len(spans) :]
    my_seq = info[0]
    sort_slots(slot_block, my_seq * spd, order, my_seq * spd, spd)

    def fetch(k, carry):
        pltpu.make_async_copy(master.at[order[my_seq * spd + k]], stage.at[k], sem).start()
        return carry

    lax.fori_loop(0, spd, fetch, 0)

    def group(s, carry):
        sort_slots(slot_block, s * spd, order, s * spd, spd)

        def number(k, inner):
            n = slot_block[s * spd + order[s * spd + k]]
            blocks[s * spd + k] = n
            where[n] = s * spd + k
            return inner

        return lax.fori_loop(0, spd, number, carry)

    lax.fori_loop(0, n_seq, group, 0)
    pltpu.make_async_copy(stage, stage, sem).wait()
    for out, (lo, count) in zip(outs, spans):

        def convert(k, carry, out=out, lo=lo):
            out[k] = stage[lo + k].astype(BF)
            return carry

        lax.fori_loop(0, count, convert, 0)


def plan_slots(slot_block, info, master, spans, n_seq, after):
    spd = master.shape[0]
    table = jax.ShapeDtypeStruct((n_seq * spd,), jnp.int32)
    return pl.pallas_call(
        functools.partial(plan_kernel, spd, n_seq, spans, len(after)),
        in_specs=[smem_spec(), smem_spec(), any_spec()] + [any_spec()] * len(after),
        out_specs=[smem_spec()] * 3 + [vmem_spec()] * len(spans),
        out_shape=[table, table, table]
        + [jax.ShapeDtypeStruct((count, B, B), BF) for unused, count in spans],
        scratch_shapes=[pltpu.VMEM((spd, B, B), F32), pltpu.SemaphoreType.DMA(())],
        compiler_params=params(),
        cost_estimate=cost(1, 12_000_000),
        name="plan_slots",
    )(slot_block, info, master, *after)


def swap(value, axis, bit):
    size = lax.axis_size(axis)
    return lax.ppermute(value, axis, [(i, i ^ bit) for i in range(size)])


def rep_swap(value, step):
    n_rep, n_seq = lax.axis_size("rep"), lax.axis_size("seq")
    bits = rep_orders(n_rep)
    pairs = []
    for r in range(n_rep):
        for s in range(n_seq):
            pairs.append((r * n_seq + s, (r ^ bits[s % 2][step]) * n_seq + s))
    return lax.ppermute(value, ("rep", "seq"), pairs)


def rep_orders(n_rep):
    bits = [1 << i for i in range(n_rep.bit_length() - 1)]
    return bits, bits[::-1]


def held_order(n_rep):
    result = []
    for bits in rep_orders(n_rep):
        held = [0]
        for bit in bits:
            held = held + [e ^ bit for e in held]
        result.append(held)
    return result


def shift_seq(value, step):
    n_seq = lax.axis_size("seq")
    pairs = [(i, i + 2 * step) for i in range(n_seq) if 0 <= i + 2 * step < n_seq]
    return lax.ppermute(value, "seq", pairs)


def relay_kernel(n_in, jobs, info, *rest):
    ins, outs = rest[:n_in], rest[-len(jobs) :]
    z = info[0] // 2
    for out, (rows, parts) in zip(outs, jobs):
        for lo, size, cases in parts:
            for zs, src, at in cases:
                if not zs:
                    out[lo : lo + size] = ins[src][at : at + size]
                    continue

                @pl.when(functools.reduce(lambda a, b: a | b, [z == v for v in zs]))
                def _(src=src, at=at, lo=lo, size=size, out=out):
                    out[lo : lo + size] = ins[src][at : at + size]


def relay(info, ins, jobs, after=()):
    extra = list(after)
    return pl.pallas_call(
        functools.partial(relay_kernel, len(ins), jobs),
        in_specs=[smem_spec()] + [vmem_spec()] * len(ins) + [any_spec()] * len(extra),
        out_specs=[vmem_spec()] * len(jobs),
        out_shape=[jax.ShapeDtypeStruct((rows, B, B), BF) for rows, unused in jobs],
        compiler_params=params(),
        cost_estimate=cost(1, 1),
        name="relay",
    )(info, *ins, *extra)


def gather_line(quarter, extra, info, my_seq, plan):
    q = quarter.shape[0]
    z = my_seq // 2
    core = my_seq % 2
    n_rep = lax.axis_size("rep")

    def pair(first, second, after=()):
        return relay(info, [first, second], [(2 * q, [(0, q, [((), 0, 0)]), (q, q, [((), 1, 0)])])], after)[0]

    def nearer(at):
        return [((0, 1), 1, at), ((2, 3), 0, at)]

    up, down = shift_seq(quarter, 1), shift_seq(quarter, -1)
    (near,) = relay(info, [up, down], [(q, [(0, q, nearer(0))])])
    up2, down2 = shift_seq(up, 1), shift_seq(down, -1)
    near1 = rep_swap(near, 0)
    near_pair = pair(near, near1)
    near2 = rep_swap(near_pair, 1)
    order, blocks, where, *owns = plan(near_pair)
    own = owns[0]
    size = extra.shape[0]
    keep = (size, [(0, size, [((), 2, 0)])])
    mid, held = relay(info, [up2, down2, extra], [(q, [(0, q, nearer(0))]), keep], [order])
    late_two = swap(held, "seq", 4)
    ends = lax.ppermute(mid, "seq", [(2, 0), (3, 1), (4, 6), (5, 7)])
    mid1 = rep_swap(mid, 0)
    mid_pair = pair(mid, mid1, [near2])
    mid2 = rep_swap(mid_pair, 1)
    far, held = relay(
        info,
        [up, down, ends, extra],
        [
            (q, [(0, q, [((0, 3), 2, 0), ((1,), 0, 0), ((2,), 1, 0)])]),
            (size, [(0, size, [((), 3, 0)])]),
        ],
        [mid_pair, late_two],
    )
    late = [swap(held, "seq", 2), late_two, swap(held, "seq", 6)]
    far1 = rep_swap(far, 0)
    sib_near = [swap(near_pair, "seq", 1), swap(near2, "seq", 1)]
    sib = swap(own, "seq", 1)
    far_pair = pair(far, far1, [mid2, mid_pair, sib] + sib_near)
    far2 = rep_swap(far_pair, 1)
    sib_mid = [swap(mid_pair, "seq", 1), swap(mid2, "seq", 1)]
    far_sib = [swap(far_pair, "seq", 1), swap(far2, "seq", 1)]
    n = len(late)
    (here,) = relay(info, late, [(n * size, [(i * size, size, [((), i, 0)]) for i in range(n)])], [far_pair])
    my_rep = info[1]
    z_near = jnp.where(z < 2, z + 1, z - 1)
    z_mid = jnp.where(z < 2, z + 2, z - 2)
    z_far = jnp.where(z % 2 == 0, 3, 0)
    half = n_rep // 2
    result = [part_of(own, z, core), part_of(sib, z, 1 - core)]
    for zs, mine, theirs in (
        (z_near, (near_pair, near2), sib_near),
        (z_mid, (mid_pair, mid2), sib_mid),
        (z_far, (far_pair, far2), far_sib),
    ):
        for part in range(2):
            result.append(part_of(mine[part], zs, core, part * half, my_rep, q))
            result.append(part_of(theirs[part], zs, 1 - core, part * half, my_rep, q))
    return (order, blocks, where, owns), result, (here, tuple(z ^ delta for delta in range(1, 4)))


def gather_direct(quarter, own, my_seq, my_rep):
    z = my_seq // 2
    core = my_seq % 2
    n_rep, n_z = lax.axis_size("rep"), lax.axis_size("seq") // 2
    sib = swap(own, "seq", 1)
    result = [part_of(own, z, core), part_of(sib, z, 1 - core)]
    q = quarter.shape[0]
    for delta in range(1, n_z):
        held = swap(quarter, "seq", 2 * delta)
        for step in range(len(rep_orders(n_rep)[0])):
            held = jnp.concatenate([held, rep_swap(held, step)], axis=0)
        result.append(part_of(held, z ^ delta, core, 0, my_rep, q))
        result.append(part_of(swap(held, "seq", 1), z ^ delta, 1 - core, 0, my_rep, q))
    return result


def part_of(buf, z, core, part=0, rep=0, quarter=0, rows=None):
    return buf, rows or (0, buf.shape[0]), quarter, (z, core, part, rep)


def late_parts(late, own, sib, my_seq, my_rep):
    here, planes = late
    n_rep = lax.axis_size("rep")
    z, core = my_seq // 2, my_seq % 2
    q = here.shape[0] // len(planes)
    result = [part_of(own, z, core), part_of(sib, z, 1 - core)]
    for e in range(n_rep):
        held = swap(here, "rep", e) if e else here
        other = swap(held, "seq", 1)
        for i, plane in enumerate(planes):
            rows = (i * q, q)
            result.append(part_of(held, plane, core, 0, my_rep ^ e, q, rows))
            result.append(part_of(other, plane, 1 - core, 0, my_rep ^ e, q, rows))
    return result


def describe(spans_parts, spd):
    bufs, layout, rows = [], [], []
    for (first, unused), parts in spans_parts:
        for buf, (row, count), quarter, (z, core, part, rep) in parts:
            index = [i for i, b in enumerate(bufs) if b is buf]
            if not index:
                bufs.append(buf)
                index = [len(bufs) - 1]
            layout.append((index[0], row, count, quarter))
            rows += [(z * 2 + core) * spd + first, core, part, rep]
    return jnp.stack([jnp.asarray(r, jnp.int32) for r in rows]), bufs, tuple(layout)


def load_weights(first_block, n_rep, layout, tables, blocks, desc, bufs, w_ref, sems):
    w_i, w_j, held = tables
    for index, (b, row0, count, quarter) in enumerate(layout):
        base, core, part, rep = (desc[4 * index + i] for i in range(4))
        size = quarter or count
        for step in range(count // size):
            place = base
            if quarter:
                place = base + (held[core * n_rep + part + step] ^ rep) * quarter

            def body(e, carry, buf=bufs[b], row=row0 + step * size, place=place):
                n = blocks[place + e] - first_block

                @pl.when((n >= 0) & (n < PER_LAYER))
                def _():
                    code = w_i[n]
                    at = pl.multiple_of((code & 3) * B, B)
                    col = pl.multiple_of(w_j[n] * B, B)
                    pltpu.make_async_copy(
                        buf.at[row + e], w_ref.at[pl.ds(at, B), pl.ds(col, B)], sems.at[code >> 2]
                    ).start()

                return carry

            lax.fori_loop(0, size, body, 0)


def weight_tables(n_rep):
    return [jnp.asarray(t) for t in (W_I, W_J, np.array(sum(held_order(n_rep), []), np.int32))]


def first_fwd_kernel(n_rep, nbuf, quarters, w_i, w_j, held, blocks, desc, x_ref, par, *rest):
    bufs = rest[:nbuf]
    out_ref, cls_ref, qkv_ref, p_ref, r1_ref, r2_ref, gp_ref, lt_ref, w, a_ref, sems = rest[nbuf:]
    first = pl.program_id(0) == 0

    @pl.when(first)
    def _():
        load_weights(0, n_rep, quarters, (w_i, w_j, held), blocks, desc, bufs, w, sems)

    def wait(mat):
        @pl.when(first)
        def _():
            wait_weights(w, sems, mat)

    xb = x_ref[...]
    out = fwd_tile(
        xb.astype(F32), xb, w, par, None, qkv_ref, p_ref, r1_ref, r2_ref, gp_ref, lt_ref, a_ref, wait
    ).astype(BF)
    out_ref[...] = out
    for s in range(TILE // SEG_LEN):
        cls_ref[0, s : s + 1, :] = out[s * SEG_LEN : s * SEG_LEN + 1, :]


def first_fwd(n_rep, weights, tokens, par):
    blocks, desc, bufs, quarters = weights
    rows = tokens.shape[0]
    steps = rows // TILE
    nseg = TILE // SEG_LEN
    return pl.pallas_call(
        functools.partial(first_fwd_kernel, n_rep, len(bufs), quarters),
        grid_spec=pltpu.PrefetchScalarGridSpec(
            num_scalar_prefetch=5,
            grid=(steps,),
            in_specs=[row_spec(D), whole_spec((1, NPAR))] + [any_spec()] * len(bufs),
            out_specs=[
                row_spec(D),
                pl.BlockSpec((1, nseg, D), lambda i, *_: (i, 0, 0)),
                row_spec(3 * D),
                row_spec(NPAIR * 256),
                row_spec(D),
                row_spec(D),
                row_spec(FF),
                pl.BlockSpec((L_ROWS, TILE), lambda i, *_: (0, i)),
            ],
            scratch_shapes=[
                pltpu.VMEM((D, W_COLS), BF),
                pltpu.VMEM((TILE, D), BF),
                pltpu.SemaphoreType.DMA((4,)),
            ],
        ),
        out_shape=[
            jax.ShapeDtypeStruct((rows, D), BF),
            jax.ShapeDtypeStruct((steps, nseg, D), BF),
            jax.ShapeDtypeStruct((rows, 3 * D), BF),
            jax.ShapeDtypeStruct((rows, NPAIR * 256), BF),
            jax.ShapeDtypeStruct((rows, D), F32),
            jax.ShapeDtypeStruct((rows, D), F32),
            jax.ShapeDtypeStruct((rows, FF), BF),
            jax.ShapeDtypeStruct((L_ROWS, rows), BF),
        ],
        compiler_params=params(),
        cost_estimate=cost(15_000_000_000, 60_000_000),
        name="first_forward",
    )(*weight_tables(n_rep), blocks, desc, tokens, par, *bufs)


def first_bwd_kernel(
    n_rep, nbuf, quarters, n_after, w_i, w_j, held, blocks, desc, cot_ref, back_ref, out_ref, par, *rest
):
    qkv_ref, p_ref, r1_ref, r2_ref, gp_ref = rest[:5]
    bufs = rest[5 : 5 + nbuf]
    hid_ref, r_ref, dx_ref, pg_ref, w, da_ref, rows_ref, sems = rest[5 + nbuf + n_after :]
    step = pl.program_id(0)
    first = step == 0

    @pl.when(first)
    def _():
        load_weights(0, n_rep, quarters, (w_i, w_j, held), blocks, desc, bufs, w, sems)
        pg_ref[...] = jnp.zeros_like(pg_ref)
        rows_ref[...] = jnp.sum(back_ref[...].astype(F32), axis=0)

    def wait(mat):
        @pl.when(first)
        def _():
            wait_weights(w, sems, mat)

    dout = cot_ref[...].astype(F32)
    out = out_ref[...]
    index = lax.broadcasted_iota(jnp.int32, (TILE, 1), 0)
    nseg = TILE // SEG_LEN
    for s in range(nseg):
        row = rows_ref[pl.ds(step * nseg + s, 1), :]
        dout = jnp.where(index == s * SEG_LEN, row[:, :D], dout)
        out = jnp.where(index == s * SEG_LEN, row[:, D:], out.astype(F32)).astype(BF)
    hid_ref[...] = out
    dx_ref[...] = bwd_tile(
        dout, w, par, qkv_ref, p_ref, r1_ref, r2_ref, gp_ref, r_ref, pg_ref, da_ref, wait
    )


def first_bwd(n_rep, weights, cot, back, out_one, par, kept, after):
    blocks, desc, bufs, quarters = weights
    rows = cot.shape[0]
    steps = rows // TILE
    nseg = TILE // SEG_LEN
    return pl.pallas_call(
        functools.partial(first_bwd_kernel, n_rep, len(bufs), quarters, len(after)),
        grid_spec=pltpu.PrefetchScalarGridSpec(
            num_scalar_prefetch=5,
            grid=(steps,),
            in_specs=[
                row_spec(D),
                whole_spec(back.shape),
                row_spec(D),
                whole_spec((1, NPAR)),
                row_spec(3 * D),
                row_spec(NPAIR * 256),
                row_spec(D),
                row_spec(D),
                row_spec(FF),
            ]
            + [any_spec()] * (len(bufs) + len(after)),
            out_specs=[row_spec(D), row_spec(R_COLS), row_spec(D), whole_spec((1, NPAR))],
            scratch_shapes=[
                pltpu.VMEM((D, W_COLS), BF),
                pltpu.VMEM((TILE, D), BF),
                pltpu.VMEM((steps * nseg, 2 * D), F32),
                pltpu.SemaphoreType.DMA((4,)),
            ],
        ),
        out_shape=[
            jax.ShapeDtypeStruct((rows, D), BF),
            jax.ShapeDtypeStruct((rows, R_COLS), BF),
            jax.ShapeDtypeStruct((rows, D), F32),
            jax.ShapeDtypeStruct((1, NPAR), F32),
        ],
        compiler_params=params(),
        cost_estimate=cost(30_000_000_000, 60_000_000),
        name="first_backward",
    )(*weight_tables(n_rep), blocks, desc, cot, back, out_one, par, *kept, *bufs, *after)


def second_kernel(
    n_rep, nbuf, quarters, w_i, w_j, held, blocks, desc, doc, got, pos, par, *rest
):
    bufs = rest[:nbuf]
    reply_ref, state_ref, lt_ref, r_ref, dx_ref, pg_ref = rest[nbuf : nbuf + 6]
    w, a_ref, qkv_ref, p_ref, r1_ref, r2_ref, gp_ref, x_ref, cot_ref, sems = rest[nbuf + 6 :]
    load_weights(PER_LAYER, n_rep, quarters, (w_i, w_j, held), blocks, desc, bufs, w, sems)
    pg_ref[...] = jnp.zeros_like(pg_ref)
    reply_ref[...] = jnp.zeros_like(reply_ref)
    x_ref[...] = jnp.zeros_like(x_ref)
    cot_ref[...] = jnp.zeros_like(cot_ref)
    start, length = doc[0], doc[1]
    for j in range(0, DOC_LONG, 16):
        rows = slice(j, j + 16)
        x_ref[rows, :] = pos[rows, :]

        @pl.when(j < length)
        def _(j=j, rows=rows):
            at = pl.ds(pl.multiple_of(start + j, 16), 16)
            x_ref[rows, :] = pos[rows, :] + got[at, :D].astype(F32)
            cot_ref[rows, :] = got[at, D:].astype(F32)

    key = lax.broadcasted_iota(jnp.int32, (1, SEG_LEN), 1)
    key_bias = jnp.where(key < length, 0.0, MASKED_SCORE).astype(F32)
    x32 = x_ref[...]
    y = fwd_tile(
        x32,
        x32.astype(BF),
        w,
        par,
        key_bias,
        qkv_ref,
        p_ref,
        r1_ref,
        r2_ref,
        gp_ref,
        lt_ref,
        a_ref,
        lambda mat: wait_weights(w, sems, mat),
    )
    row = lax.broadcasted_iota(jnp.int32, (SEG_LEN, 1), 0)
    y = jnp.where(row < length, y, 0.0)
    state_ref[...] = y[:DOC_LONG].astype(BF)
    dx = bwd_tile(
        cot_ref[...],
        w,
        par,
        qkv_ref,
        p_ref,
        r1_ref,
        r2_ref,
        gp_ref,
        r_ref,
        pg_ref,
        a_ref,
        lambda mat: None,
    )
    dx = jnp.where(row < length, dx, 0.0)
    dx_ref[...] = dx[:DOC_LONG]
    for j in range(0, DOC_LONG, 16):

        @pl.when(j < length)
        def _(j=j):
            at = pl.ds(pl.multiple_of(start + j, 16), 16)
            reply_ref[at, :D] = dx[j : j + 16].astype(BF)
            reply_ref[at, D:] = y[j : j + 16].astype(BF)


def second_layer(n_rep, weights, doc, got, pos, par):
    blocks, desc, bufs, quarters = weights
    rows = SEG_LEN
    group = got.shape[0]
    return pl.pallas_call(
        functools.partial(second_kernel, n_rep, len(bufs), quarters),
        in_specs=[smem_spec()] * 6 + [vmem_spec()] * 3 + [any_spec()] * len(bufs),
        out_specs=[vmem_spec()] * 6,
        scratch_shapes=[
            pltpu.VMEM((D, W_COLS), BF),
            pltpu.VMEM((rows, D), BF),
            pltpu.VMEM((rows, 3 * D), BF),
            pltpu.VMEM((rows, NPAIR * 256), BF),
            pltpu.VMEM((rows, D), F32),
            pltpu.VMEM((rows, D), F32),
            pltpu.VMEM((rows, FF), BF),
            pltpu.VMEM((rows, D), F32),
            pltpu.VMEM((rows, D), F32),
            pltpu.SemaphoreType.DMA((4,)),
        ],
        out_shape=[
            jax.ShapeDtypeStruct((group, 2 * D), BF),
            jax.ShapeDtypeStruct((DOC_LONG, D), BF),
            jax.ShapeDtypeStruct((L_ROWS, rows), BF),
            jax.ShapeDtypeStruct((rows, R_COLS), BF),
            jax.ShapeDtypeStruct((DOC_LONG, D), F32),
            jax.ShapeDtypeStruct((1, NPAR), F32),
        ],
        compiler_params=params(),
        cost_estimate=cost(8_000_000_000, 40_000_000),
        name="second_layer",
    )(*weight_tables(n_rep), blocks, desc, doc, got, pos, par, *bufs)


PRODUCTS = (
    (L_X, R_QKV, 9, 0),
    (L_A, R_OUT, 3, 27),
    (L_H, R_UP, 12, 36),
    (L_E, R_DOWN, 3, 72),
    (L_E + D, R_DOWN, 3, 81),
    (L_E + 2 * D, R_DOWN, 3, 90),
    (L_E + 3 * D, R_DOWN, 3, 99),
)


def send_block(src, n, ctx, where, info, outs, sem):
    spd, unused, chunks = ctx
    at = where[n]
    owner = at // spd
    k = at % spd
    target = (owner // 2) ^ (info[0] // 2)
    mine = (owner % 2) == (info[0] % 2)
    for c, (first, m) in enumerate(chunks):
        inside = (k >= first) & (k < first + m)
        for side, cond in ((0, inside & jnp.logical_not(mine)), (1, inside & mine)):

            @pl.when(cond)
            def _(c=c, side=side, first=first):
                pltpu.make_async_copy(src, outs[2 * c + side].at[target, k - first], sem).start()


def all_products(lt, r, stage, base, ctx, where, info, outs, sem, before=None):
    for lrow, rcol, across, first in PRODUCTS:
        if before is not None:
            before(lrow)
        for j in range(across):
            value = mm(lt[lrow : lrow + D, :], r[:, rcol + j * B : rcol + (j + 1) * B]).astype(BF)
            for i in range(D // B):
                local = first + i * across + j
                stage[local] = value[i * B : (i + 1) * B]
                send_block(stage.at[local], base + local, ctx, where, info, outs, sem)


def wait_blocks(stage, sem, count):
    part = stage.at[pl.ds(0, count)]
    pltpu.make_async_copy(part, part, sem).wait()


def second_grad_kernel(ctx, n_empty, n_after, where, info, lt, r, *rest):
    outs, (stage, zero, sem) = rest[n_after:-3], rest[-3:]
    zero[...] = jnp.zeros_like(zero)
    for n in range(NBLK, NBLK + n_empty):
        send_block(zero.at[n - NBLK], n, ctx, where, info, outs, sem)
    all_products(lt, r, stage, PER_LAYER, ctx, where, info, outs, sem)
    wait_blocks(stage, sem, PER_LAYER)
    if n_empty:
        wait_blocks(zero, sem, n_empty)


def chunk_arrays(ctx):
    return [jax.ShapeDtypeStruct((ctx[1], m, B, B), BF) for unused, m in ctx[2] for side in range(2)]


def second_grad(ctx, where, info, lt, r, after):
    shapes = chunk_arrays(ctx)
    n_empty = where.shape[0] - NBLK
    return pl.pallas_call(
        functools.partial(second_grad_kernel, ctx, n_empty, len(after)),
        in_specs=[smem_spec()] * 2 + [vmem_spec()] * 2 + [any_spec()] * len(after),
        out_specs=[any_spec()] * len(shapes),
        out_shape=shapes,
        scratch_shapes=[
            pltpu.VMEM((PER_LAYER, B, B), BF),
            pltpu.VMEM((max(n_empty, 1), B, B), BF),
            pltpu.SemaphoreType.DMA(()),
        ],
        compiler_params=params(),
        cost_estimate=cost(2_000_000_000, 18_000_000),
        name="second_gradients",
    )(where, info, lt, r, *after)


def first_grad_kernel(ctx, n_after, where, info, lt, r, *rest):
    n_out = 2 * len(ctx[2])
    outs = rest[n_out + n_after : 2 * n_out + n_after]
    lt_s, r_s, stage, sem, sems = rest[2 * n_out + n_after :]
    spans = ((L_X, L_A, R_QKV, R_OUT), (L_A, L_H, R_OUT, R_UP), (L_H, L_E, R_UP, R_DOWN), (L_E, L_ROWS, R_DOWN, R_COLS))
    copies = []
    for i, (la, lb, ra, rb) in enumerate(spans):
        pair = (
            pltpu.make_async_copy(lt.at[la:lb], lt_s.at[la:lb], sems.at[2 * i]),
            pltpu.make_async_copy(r.at[:, ra:rb], r_s.at[:, ra:rb], sems.at[2 * i + 1]),
        )
        for copy in pair:
            copy.start()
        copies.append((la, pair))

    def before(lrow):
        for la, pair in copies:
            if la == lrow:
                for copy in pair:
                    copy.wait()

    all_products(lt_s, r_s, stage, 0, ctx, where, info, outs, sem, before)
    wait_blocks(stage, sem, PER_LAYER)


def first_grad(ctx, where, info, lt, r, arrays, after):
    n = len(arrays)
    return pl.pallas_call(
        functools.partial(first_grad_kernel, ctx, len(after)),
        in_specs=[smem_spec()] * 2 + [any_spec()] * (2 + n + len(after)),
        out_specs=[any_spec()] * n,
        out_shape=[jax.ShapeDtypeStruct(a.shape, BF) for a in arrays],
        scratch_shapes=[
            pltpu.VMEM(lt.shape, BF),
            pltpu.VMEM(r.shape, BF),
            pltpu.VMEM((PER_LAYER, B, B), BF),
            pltpu.SemaphoreType.DMA(()),
            pltpu.SemaphoreType.DMA((8,)),
        ],
        input_output_aliases={4 + i: i for i in range(n)},
        compiler_params=params(),
        cost_estimate=cost(15_000_000_000, 40_000_000),
        name="first_gradients",
    )(where, info, lt, r, *arrays, *after)


def halve_kernel(step, n_after, info, a_ref, b_ref, *rest):
    send_ref, keep_ref = rest[n_after:]
    half = send_ref.shape[2]
    high = high_bit(info, step)
    for side, ref in ((1 - high, send_ref), (high, keep_ref)):
        rows = pl.ds(pl.multiple_of(side * half, half), half)
        ref[...] = a_ref[:, :, rows, :] + b_ref[:, :, rows, :]


def high_bit(info, step):
    orders = rep_orders(4)
    core, rep = info[0] % 2, info[1]
    bit = jnp.where(core == 0, orders[0][step], orders[1][step])
    return jnp.where((rep & bit) != 0, 1, 0)


def halve(info, step, a, b, after):
    n_target, m, rows, cols = a.shape
    shape = jax.ShapeDtypeStruct((n_target, m, rows // 2, cols), BF)
    group = 2 if n_target * m <= 64 else 1

    def spec(r):
        return pl.BlockSpec((group, m, r, cols), lambda i, *_: (i, 0, 0, 0))

    return pl.pallas_call(
        functools.partial(halve_kernel, step, len(after)),
        grid_spec=pltpu.PrefetchScalarGridSpec(
            num_scalar_prefetch=1,
            grid=(n_target // group,),
            in_specs=[spec(rows)] * 2 + [any_spec()] * len(after),
            out_specs=[spec(rows // 2)] * 2,
        ),
        out_shape=[shape, shape],
        compiler_params=params(),
        cost_estimate=cost(1, 1),
        name="halve",
    )(info, a, b, *after)


def spread_kernel(n_after, a_ref, b_ref, *rest):
    for i, out in enumerate(rest[n_after:]):
        out[...] = a_ref[i] + b_ref[i]


def spread(a, b, after):
    shape = jax.ShapeDtypeStruct(a.shape[1:], BF)
    return pl.pallas_call(
        functools.partial(spread_kernel, len(after)),
        in_specs=[vmem_spec()] * 2 + [any_spec()] * len(after),
        out_specs=[vmem_spec()] * a.shape[0],
        out_shape=[shape] * a.shape[0],
        compiler_params=params(),
        cost_estimate=cost(1, 1),
        name="spread",
    )(a, b, *after)


def total_kernel(count, *rest):
    total = rest[0][...].astype(F32)
    for ref in rest[1:count]:
        total = total + ref[...].astype(F32)
    rest[-1][...] = total.astype(BF)


def total(parts, after):
    shape = jax.ShapeDtypeStruct(parts[0].shape, BF)
    return pl.pallas_call(
        functools.partial(total_kernel, len(parts)),
        in_specs=[vmem_spec()] * len(parts) + [any_spec()] * len(after),
        out_specs=vmem_spec(),
        out_shape=shape,
        compiler_params=params(),
        cost_estimate=cost(1, 1),
        name="total",
    )(*parts, *after)


def shampoo_kernel(n_rep, spd, first, n_previous, order, info, *rest):
    pieces, stats = rest[:n_rep], rest[n_rep : n_rep + 5]
    outs, token, (ins_ref, outs_ref, g_ref, ins_sem, outs_sem) = rest[-10:-6], rest[-6], rest[-5:]
    token[...] = jnp.zeros_like(token)
    count = pieces[0].shape[0]
    slots = [order[info[0] * spd + first + i] for i in range(count)]
    for i, slot in enumerate(slots):
        for a, stat in enumerate(stats):
            pltpu.make_async_copy(stat.at[slot], ins_ref.at[i, a], ins_sem.at[i]).start()
    orders = rep_orders(n_rep)
    size = B // n_rep
    places = []
    for e in range(n_rep):
        rep = info[1] ^ e
        place = jnp.int32(0)
        for level in range(len(orders[0])):
            bit = jnp.where(info[0] % 2 == 0, orders[0][level], orders[1][level])
            place = place + jnp.where((rep & bit) != 0, B >> (level + 1), 0)
        places.append(pl.multiple_of(place, size))
    for i, slot in enumerate(slots):
        for place, piece in zip(places, pieces):
            g_ref[i, pl.ds(place, size), :] = piece[i]
        g = g_ref[i]
        pltpu.make_async_copy(ins_ref.at[i], ins_ref.at[i], ins_sem.at[i]).wait()
        left, right, lroot, rroot, master = (ins_ref[i, a] for a in range(5))
        part = mm(lroot.astype(BF), g)
        outs_ref[i, 0] = g.astype(F32)
        outs_ref[i, 1] = DECAY * left + (1.0 - DECAY) * mm_t(g, g)
        outs_ref[i, 2] = DECAY * right + (1.0 - DECAY) * tmm(g, g)
        direction = mm(part.astype(BF), rroot.astype(BF))
        scale = BLOCK_RATE * lax.rsqrt(jnp.mean(direction * direction) + RMS_EPS)
        outs_ref[i, 3] = master - direction * scale
        for a, out in enumerate(outs):
            pltpu.make_async_copy(outs_ref.at[i, a], out.at[slot], outs_sem).start()
    pltpu.make_async_copy(outs_ref, outs_ref, outs_sem).wait()


def shampoo(order, info, spd, first, pieces, stats, previous, after):
    count = pieces[0].shape[0]
    n_rep = len(pieces)
    n_in = 2 + n_rep + len(stats)
    return pl.pallas_call(
        functools.partial(shampoo_kernel, n_rep, spd, first, len(previous)),
        in_specs=[smem_spec()] * 2
        + [vmem_spec()] * n_rep
        + [any_spec()] * (len(stats) + len(previous) + len(after)),
        out_specs=[any_spec()] * 4 + [vmem_spec()],
        out_shape=[jax.ShapeDtypeStruct((spd, B, B), F32)] * 4 + [jax.ShapeDtypeStruct((8, 128), F32)],
        scratch_shapes=[
            pltpu.VMEM((count, 5, B, B), F32),
            pltpu.VMEM((count, 4, B, B), F32),
            pltpu.VMEM((count, B, B), BF),
            pltpu.SemaphoreType.DMA((count,)),
            pltpu.SemaphoreType.DMA(()),
        ],
        input_output_aliases={n_in + i: i for i in range(len(previous))},
        compiler_params=params(),
        cost_estimate=cost(1, 1),
        name="shampoo",
    )(order, info, *pieces, *stats, *previous, *after)


def reduce_pipeline(ctx, chunks, ready, idle, stats, after):
    order, info, spd, n_rep = ctx
    state = {}
    results = ()
    for batch in range(len(chunks) + 6):
        for run in ready.get(batch, ()):
            after = run(after)
        for i in range(len(chunks))[::-1]:
            stage = batch - i
            if chunks[i] is None or stage < 1:
                continue
            first, m, products = chunks[i]
            if stage == 1:
                got, own = state[i]
                send, keep = halve(info, 0, own, got, after)
                state[i] = (rep_swap(send, 0), keep)
                after = (keep,)
            elif stage == 2:
                got, kept = state[i]
                send, keep = halve(info, 1, kept, got, after)
                state[i] = (rep_swap(send, 1), keep)
                after = (keep,)
            elif stage == 3:
                got, kept = state[i]
                parts = spread(kept, got, after)
                moved = [swap(part, "seq", 2 * d) for d, part in enumerate(parts) if d]
                state[i] = [parts[0]] + moved
                after = (parts[0],)
            elif stage == 4:
                mine = total(state[i], after)
                state[i] = [mine] + [swap(mine, "rep", e) for e in range(1, n_rep)]
                after = (mine,)
        done = batch - 6
        if 0 <= done < len(chunks) and chunks[done] is not None:
            first = chunks[done][0]
            *results, token = shampoo(order, info, spd, first, state[done], stats, results, after)
            after = (token,)
        for run in idle.get(batch, ()):
            after = run(after)
        if batch < len(chunks) and chunks[batch] is not None:
            sib, own = chunks[batch][2]()
            state[batch] = (swap(sib, "seq", 1), own)
    return results, after


def small_kernel(old, grads, *rest):
    out = rest[-1]
    rows = 2 * NPAR // 128
    for part in (slice(0, rows), slice(rows, None)):
        g = grads[part, :]
        out[part, :] = old[part, :] - SMALL_RATE * g * lax.rsqrt(jnp.mean(g * g) + RMS_EPS)


def add_kernel(a, b, *rest):
    rest[-1][...] = a[...] + b[...]


def add(a, b, after):
    return pl.pallas_call(
        add_kernel,
        in_specs=[vmem_spec()] * 2 + [any_spec()] * len(after),
        out_specs=vmem_spec(),
        out_shape=jax.ShapeDtypeStruct(a.shape, F32),
        compiler_params=params(),
        cost_estimate=cost(1, 1),
        name="add",
    )(a, b, *after)


def small_step(old, grads, after):
    shape = (old.shape[0] // 128, 128)
    return pl.pallas_call(
        small_kernel,
        in_specs=[vmem_spec()] * 2 + [any_spec()] * len(after),
        out_specs=vmem_spec(),
        out_shape=jax.ShapeDtypeStruct(shape, F32),
        compiler_params=params(),
        cost_estimate=cost(1, 1_000_000),
        name="small_step",
    )(old.reshape(shape), grads.reshape(shape), *after).reshape(-1)


def split_slots(spd):
    if spd == 28:
        return ((0, 20), (20, 8)), ((0, 10), (10, 10), (20, 8))
    return ((0, spd),), ((0, spd),)


def shards(
    tokens,
    cotangent,
    doc_lengths,
    doc_owners,
    small_params,
    slot_block,
    master_blocks,
    left_stats,
    right_stats,
    left_roots,
    right_roots,
):
    seg_dev = tokens.shape[0] // SEG_LEN
    n_seq, n_rep = lax.axis_size("seq"), lax.axis_size("rep")
    my_seq = lax.axis_index("seq").astype(jnp.int32)
    my_rep = lax.axis_index("rep").astype(jnp.int32)
    spd = master_blocks.shape[0]
    n_target = n_seq // 2
    info = jnp.stack([my_seq, my_rep])
    par_one = small_params[None, :NPAR]
    par_two = small_params[None, NPAR : 2 * NPAR]
    position = small_params[2 * NPAR :].reshape(DOC_LONG, D)

    line = n_seq == 8 and n_rep == 4 and spd == 28
    spans, chunk_spans = split_slots(spd) if line else (((0, spd),), ((0, spd),))
    ctx = (spd, n_target, chunk_spans)
    quarter, extra = quarter_blocks(slot_block, info, master_blocks, spans, n_rep)

    lengths_row = doc_lengths[0]
    owners_row = doc_owners[0]
    starts_row = jnp.cumsum(lengths_row) - lengths_row
    first_seg = my_seq * seg_dev
    inside = (starts_row <= first_seg) & (first_seg < starts_row + lengths_row)
    owner = jnp.sum(jnp.where(inside, owners_row, 0))
    target = (jnp.arange(n_seq, dtype=jnp.int32) == owner).astype(BF)[:, None, None]
    mine = (owners_row == my_seq) & (lengths_row > 0)
    doc = jnp.stack([jnp.sum(jnp.where(mine, starts_row, 0)), jnp.sum(jnp.where(mine, lengths_row, 0))])
    doc = doc.astype(jnp.int32)

    def to_owner(rows):
        sent = target * rows[None]
        got = lax.all_to_all(sent, "seq", split_axis=0, concat_axis=0, tiled=True)
        return got.reshape(n_seq * seg_dev, 2 * D)

    cot_first = cotangent.reshape(seg_dev, SEG_LEN, D)[:, 0, :]

    def plan(after):
        early = (after, par_one, par_two, position, target, doc, cot_first)
        return plan_slots(slot_block, info, master_blocks, spans, n_seq, early)

    stats = (left_stats, right_stats, left_roots, right_roots, master_blocks)
    if line:
        (order, blocks, where, owns), parts_one, late = gather_line(
            quarter, extra, info, my_seq, plan
        )
        late_sib = swap(owns[1], "seq", 1)
    else:
        order, blocks, where, *owns = plan(quarter)
        parts_one, late, late_sib = gather_direct(quarter, owns[0], my_seq, my_rep), None, None

    def layers(ahead):
        layers_parts = [(spans[0], parts_one)]
        first_parts = list(layers_parts)

        if line:
            layers_parts.append((spans[1], late_parts(late, owns[1], late_sib, my_seq, my_rep)))
        if not ahead:
            first_parts = layers_parts
        first_desc, first_bufs, first_layout = describe(first_parts, spd)
        one = (blocks, first_desc, first_bufs, first_layout)
        out_one, cls, *kept, lt_one = first_fwd(n_rep, one, tokens, par_one)
        second_desc, second_bufs, second_layout = describe(layers_parts, spd)
        two = (blocks, second_desc, second_bufs, second_layout)
        got = to_owner(jnp.concatenate([cls.reshape(seg_dev, D), cot_first], axis=1))
        reply, states, lt_two, r_two, grad_pos, pg_two = second_layer(
            n_rep, two, doc, got, position, par_two
        )
        arrays = second_grad(ctx, where, info, lt_two, r_two, ())
        back = lax.all_to_all(
            reply.reshape(n_seq, seg_dev, 2 * D), "seq", split_axis=0, concat_axis=0, tiled=True
        )
        box = {}

        def backward(after):
            box["bwd"] = first_bwd(n_rep, one, cotangent, back, out_one, par_one, kept, after)
            pg_one = box["bwd"][3]
            local = jnp.concatenate([pg_one[0], pg_two[0], grad_pos.reshape(-1)]).reshape(2, -1, 128)
            box["sum"] = lax.dynamic_index_in_dim(local, my_seq % 2, 0, False)
            box["got"] = swap(lax.dynamic_index_in_dim(local, 1 - my_seq % 2, 0, False), "seq", 1)
            return (box["bwd"][1],)

        routes = [("seq", 2 << b) for b in range((n_seq // 2).bit_length() - 1)][::-1]
        routes += [("rep", 1 << b) for b in range(n_rep.bit_length() - 1)][::-1]

        def small_hop(axis, bit):
            def run(after):
                box["sum"] = add(box["sum"], box["got"], after)
                box["got"] = swap(box["sum"], axis, bit)
                return (box["sum"],)

            return run

        per = 2
        n_done = per if ahead else 0

        def late_products(after):
            some, done = arrays[: len(arrays) - n_done], arrays[len(arrays) - n_done :]
            sub = (spd, n_target, chunk_spans[: len(some) // per])
            made = first_grad(sub, where, info, lt_one, box["bwd"][1], some, after)
            box["all"] = list(made) + list(done)
            return (made[1],)

        def chunk(c):
            return lambda: box["all"][per * c : per * c + per]

        chunks = [(first, m, chunk(c)) for c, (first, m) in enumerate(chunk_spans)]
        if ahead:
            early = chunks[-1][:2] + (lambda: arrays[-per:],)
            chunks = [early, None] + chunks[:-1]
            ready, idle = {}, {1: [backward], 2: [late_products]}
        else:
            ready, idle = {0: [backward, late_products]}, {}
        n = len(chunks)
        for at, route in zip([3, 5, 7, 8, 9, 10, 11], routes):
            idle.setdefault(at, []).append(small_hop(*route))
        results, after = reduce_pipeline(
            (order, info, spd, n_rep), chunks, ready, idle, stats, (arrays[0],)
        )
        core = my_seq % 2
        mine = add(box["sum"], box["got"], after)
        theirs = swap(mine, "seq", 1)
        small_grads = jnp.where(
            core == 0, jnp.concatenate([mine, theirs]), jnp.concatenate([theirs, mine])
        ).reshape(-1)
        new_small = small_step(small_params, small_grads, ())
        hidden_out, unused, input_grad, unused = box["bwd"]
        return (hidden_out, input_grad, states[None], *results, small_grads, new_small)

    if not line:
        return layers(False)
    counts = jnp.sum((slot_block.reshape(n_seq, spd) < PER_LAYER).astype(jnp.int32), axis=1)
    return lax.cond(jnp.all(counts <= spans[0][1]), lambda: layers(True), lambda: layers(False))


def solution(mesh):
    in_specs = (
        P(("rep", "seq"), None),
        P(("rep", "seq"), None),
        P("rep", None),
        P("rep", None),
        P(),
        P(),
        P("seq", None, None),
        P("seq", None, None),
        P("seq", None, None),
        P("seq", None, None),
        P("seq", None, None),
    )
    out_specs = (
        P(("rep", "seq"), None),
        P(("rep", "seq"), None),
        P(("rep", "seq"), None, None),
        P("seq", None, None),
        P("seq", None, None),
        P("seq", None, None),
        P("seq", None, None),
        P(),
        P(),
    )
    return jax.shard_map(shards, mesh=mesh, in_specs=in_specs, out_specs=out_specs, check_vma=False)
```

```python
import functools

import jax
import jax.numpy as jnp
import numpy as np
from jax import lax
from jax.experimental import pallas as pl
from jax.experimental.pallas import tpu as pltpu
from jax.sharding import PartitionSpec as P

D = 768
HEAD_DIM = 64
FF = 3072
SEG_LEN = 128
DOC_LONG = 64
B = 256
PER_LAYER = 108
NBLK = 2 * PER_LAYER
NPAR = 8 * D + FF
NPAIR = D // 128

NORM_EPS = 1e-05
RMS_EPS = 1e-06
DECAY = 0.5
BLOCK_RATE = 0.02
SMALL_RATE = 0.1
MASKED_SCORE = -1000000000.0
SCALE = HEAD_DIM**-0.5

C_QKV, C_OUT, C_UP, C_DOWN, W_COLS = 0, 3 * D, 4 * D, 4 * D + FF, 4 * D + 2 * FF
W_SPANS = ((C_QKV, C_OUT), (C_OUT, C_UP), (C_UP, C_DOWN), (C_DOWN, W_COLS))
L_X, L_A, L_H, L_E, L_ROWS = 0, D, 2 * D, 3 * D, 3 * D + FF
R_QKV, R_OUT, R_UP, R_DOWN, R_COLS = 0, 3 * D, 4 * D, 4 * D + FF, 5 * D + FF
O_BQ, O_BV, O_BO, O_G1, O_C1, O_B1 = 0, D, 2 * D, 3 * D, 4 * D, 5 * D
O_B2, O_G2, O_C2 = 5 * D + FF, 6 * D + FF, 7 * D + FF

VMEM_LIMIT = 60 * 1024 * 1024
BF = jnp.bfloat16
F32 = jnp.float32


def block_tables():
    w_i, w_j, l_i, r_j = [], [], [], []
    for i in range(3):
        for j in range(9):
            w_i.append(i), w_j.append(j), l_i.append(i), r_j.append(j)
    for i in range(3):
        for j in range(3):
            w_i.append(i), w_j.append(9 + j), l_i.append(3 + i), r_j.append(9 + j)
    for i in range(3):
        for j in range(12):
            w_i.append(i), w_j.append(12 + j), l_i.append(6 + i), r_j.append(12 + j)
    for i in range(12):
        for j in range(3):
            w_i.append(i % 3), w_j.append(24 + 3 * (i // 3) + j)
            l_i.append(9 + i), r_j.append(24 + j)
    w_i = [i + 4 * ((n >= 27) + (n >= 36) + (n >= 72)) for n, i in enumerate(w_i)]
    return [np.array(t, np.int32) for t in (w_i, w_j, l_i, r_j)]


W_I, W_J, L_I, R_J = block_tables()


def mm(a, b):
    return jnp.dot(a, b, preferred_element_type=F32)


def mm_t(a, b):
    return lax.dot_general(a, b, (((1,), (1,)), ((), ())), preferred_element_type=F32)


def tmm(a, b):
    return lax.dot_general(a, b, (((0,), (0,)), ((), ())), preferred_element_type=F32)


def norm_parts(values):
    center = values - jnp.mean(values, axis=-1, keepdims=True)
    spread = jnp.mean(center * center, axis=-1, keepdims=True)
    scale = lax.rsqrt(spread + NORM_EPS)
    return center * scale, scale


def gelu_parts(u):
    cdf = 0.5 + 0.5 * lax.erf(u * 0.7071067811865476)
    return u * cdf, cdf + u * jnp.exp(-0.5 * u * u) * 0.3989422804014327


def head_masks():
    lane = lax.broadcasted_iota(jnp.int32, (1, 128), 1)
    first = jnp.where(lane < HEAD_DIM, 1.0, 0.0).astype(BF)
    return first, (1.0 - first.astype(F32)).astype(BF)


def stack_heads(pair, masks):
    return jnp.concatenate([pair * masks[0], pair * masks[1]], axis=0)


def beside(stacked):
    half = stacked.shape[0] // 2
    return jnp.concatenate([stacked[:half], stacked[half:]], axis=1)


def wait_weights(w_ref, sems, mat):
    lo, hi = W_SPANS[mat]
    part = w_ref.at[:, lo:hi]
    pltpu.make_async_copy(part, part, sems.at[mat]).wait()


def fwd_tile(x32, xb, w, par, key_bias, qkv_ref, p_ref, r1_ref, r2_ref, gp_ref, lt_ref, a_ref, wait):
    n_rows = xb.shape[0]
    lt_ref[L_X : L_X + D, :] = xb.T
    wait(0)
    for c, off in ((0, O_BQ), (1, None), (2, O_BV)):
        part = mm(xb, w[:, C_QKV + c * D : C_QKV + (c + 1) * D])
        if off is not None:
            part = part + par[:, off : off + D]
        qkv_ref[:, c * D : (c + 1) * D] = part.astype(BF)
    masks = head_masks()
    for s in range(n_rows // SEG_LEN):
        rows = slice(s * SEG_LEN, (s + 1) * SEG_LEN)
        for h in range(NPAIR):
            q = qkv_ref[rows, h * 128 : (h + 1) * 128]
            k = qkv_ref[rows, D + h * 128 : D + (h + 1) * 128]
            v = qkv_ref[rows, 2 * D + h * 128 : 2 * D + (h + 1) * 128]
            scores = mm_t(stack_heads(q, masks), k) * SCALE
            if key_bias is not None:
                scores = scores + key_bias
            exps = jnp.exp(scores - jnp.max(scores, axis=-1, keepdims=True))
            probs = exps * (1.0 / jnp.sum(exps, axis=-1, keepdims=True))
            probs = beside(probs.astype(BF))
            p_ref[rows, h * 256 : (h + 1) * 256] = probs
            a_ref[rows, h * 128 : (h + 1) * 128] = mm(probs, stack_heads(v, masks)).astype(BF)
    a = a_ref[...]
    lt_ref[L_A : L_A + D, :] = a.T
    wait(1)
    r1 = x32 + (mm(a, w[:, C_OUT : C_OUT + D]) + par[:, O_BO : O_BO + D])
    r1_ref[...] = r1
    xhat, unused = norm_parts(r1)
    h = xhat * par[:, O_G1 : O_G1 + D] + par[:, O_C1 : O_C1 + D]
    hb = h.astype(BF)
    lt_ref[L_H : L_H + D, :] = hb.T
    wait(2)
    total = h + par[:, O_B2 : O_B2 + D]
    for c in range(FF // D):
        u = mm(hb, w[:, C_UP + c * D : C_UP + (c + 1) * D]) + par[:, O_B1 + c * D : O_B1 + (c + 1) * D]
        e, gp = gelu_parts(u)
        gp_ref[:, c * D : (c + 1) * D] = gp.astype(BF)
        eb = e.astype(BF)
        lt_ref[L_E + c * D : L_E + (c + 1) * D, :] = eb.T
        if c == 0:
            wait(3)
        total = total + mm(eb, w[:, C_DOWN + c * D : C_DOWN + (c + 1) * D])
    r2_ref[...] = total
    xhat, unused = norm_parts(total)
    return xhat * par[:, O_G2 : O_G2 + D] + par[:, O_C2 : O_C2 + D]


def col_sum(values):
    return jnp.sum(values.astype(F32), axis=0, keepdims=True)


def norm_back(dout, values, gain):
    xhat, scale = norm_parts(values)
    dxhat = dout * gain
    mean_one = jnp.mean(dxhat, axis=-1, keepdims=True)
    mean_two = jnp.mean(dxhat * xhat, axis=-1, keepdims=True)
    return scale * (dxhat - mean_one - xhat * mean_two), col_sum(dout * xhat), col_sum(dout)


def bwd_tile(dout, w, par, qkv_ref, p_ref, r1_ref, r2_ref, gp_ref, r_ref, pg_ref, da_ref, wait):
    n_rows = dout.shape[0]

    def add_small(off, value):
        pg_ref[:, off : off + value.shape[1]] += value

    dr2, dgain, dshift = norm_back(dout, r2_ref[...], par[:, O_G2 : O_G2 + D])
    add_small(O_G2, dgain)
    add_small(O_C2, dshift)
    dy = dr2.astype(BF)
    r_ref[:, R_DOWN : R_DOWN + D] = dy
    add_small(O_B2, col_sum(dy))
    wait(3)
    dh = dr2
    for c in range(FF // D):
        de = mm_t(dy, w[:, C_DOWN + c * D : C_DOWN + (c + 1) * D])
        du = (gp_ref[:, c * D : (c + 1) * D].astype(F32) * de).astype(BF)
        r_ref[:, R_UP + c * D : R_UP + (c + 1) * D] = du
        add_small(O_B1 + c * D, col_sum(du))
        if c == 0:
            wait(2)
        dh = dh + mm_t(du, w[:, C_UP + c * D : C_UP + (c + 1) * D])
    dr1, dgain, dshift = norm_back(dh, r1_ref[...], par[:, O_G1 : O_G1 + D])
    add_small(O_G1, dgain)
    add_small(O_C1, dshift)
    do = dr1.astype(BF)
    r_ref[:, R_OUT : R_OUT + D] = do
    add_small(O_BO, col_sum(do))
    wait(1)
    da_ref[...] = mm_t(do, w[:, C_OUT : C_OUT + D]).astype(BF)
    masks = head_masks()
    for s in range(n_rows // SEG_LEN):
        rows = slice(s * SEG_LEN, (s + 1) * SEG_LEN)
        for h in range(NPAIR):
            q = qkv_ref[rows, h * 128 : (h + 1) * 128]
            k = qkv_ref[rows, D + h * 128 : D + (h + 1) * 128]
            v = qkv_ref[rows, 2 * D + h * 128 : 2 * D + (h + 1) * 128]
            probs = jnp.concatenate(
                [p_ref[rows, h * 256 : h * 256 + 128], p_ref[rows, h * 256 + 128 : h * 256 + 256]], axis=0
            )
            da = stack_heads(da_ref[rows, h * 128 : (h + 1) * 128], masks)
            dprobs = mm_t(da, v)
            dv = tmm(probs, da)
            probs = probs.astype(F32)
            inner = jnp.sum(dprobs * probs, axis=-1, keepdims=True)
            dscores = (probs * (dprobs - inner) * SCALE).astype(BF)
            dq = mm(beside(dscores), stack_heads(k, masks))
            dk = tmm(dscores, stack_heads(q, masks))
            r_ref[rows, h * 128 : (h + 1) * 128] = dq.astype(BF)
            r_ref[rows, D + h * 128 : D + (h + 1) * 128] = dk.astype(BF)
            r_ref[rows, 2 * D + h * 128 : 2 * D + (h + 1) * 128] = dv.astype(BF)
    add_small(O_BQ, col_sum(r_ref[:, 0:D]))
    add_small(O_BV, col_sum(r_ref[:, 2 * D : 3 * D]))
    wait(0)
    return dr1 + mm_t(r_ref[:, R_QKV : R_QKV + 3 * D], w[:, C_QKV : C_QKV + 3 * D])


TILE = 256


def any_spec():
    return pl.BlockSpec(memory_space=pl.ANY)


def smem_spec():
    return pl.BlockSpec(memory_space=pltpu.SMEM)


def vmem_spec():
    return pl.BlockSpec(memory_space=pltpu.VMEM)


def row_spec(width, tile=TILE):
    return pl.BlockSpec((tile, width), lambda i, *_: (i, 0))


def whole_spec(shape):
    return pl.BlockSpec(shape, lambda i, *_: (0,) * len(shape))


def params():
    return pltpu.CompilerParams(vmem_limit_bytes=VMEM_LIMIT)


def cost(flops, nbytes):
    return pl.CostEstimate(flops=flops, bytes_accessed=nbytes, transcendentals=0)


def sort_slots(slot_block, base, order, at, spd):
    def first(j, count):
        take = slot_block[base + j] < PER_LAYER

        @pl.when(take)
        def _():
            order[at + count] = j

        return count + take.astype(jnp.int32)

    def second(j, count):
        take = slot_block[base + j] >= PER_LAYER

        @pl.when(take)
        def _():
            order[at + count] = j

        return count + take.astype(jnp.int32)

    lax.fori_loop(0, spd, second, lax.fori_loop(0, spd, first, 0))


def quarter_kernel(spd, n_rep, spans, slot_block, info, master, out, extra, order, stage, sem):
    sort_slots(slot_block, info[0] * spd, order, 0, spd)
    at = 0
    for lo, count in spans:
        quarter = count // n_rep
        for i in range(quarter):
            slot = order[lo + info[1] * quarter + i]
            pltpu.make_async_copy(master.at[slot], stage.at[at], sem).start()
            at += 1
    pltpu.make_async_copy(stage, stage, sem).wait()
    for i in range(at):
        if i < out.shape[0]:
            out[i] = stage[i].astype(BF)
        else:
            extra[i - out.shape[0]] = stage[i].astype(BF)


def quarter_blocks(slot_block, info, master, spans, n_rep):
    spd = master.shape[0]
    total_rows = spd // n_rep
    return pl.pallas_call(
        functools.partial(quarter_kernel, spd, n_rep, spans),
        in_specs=[smem_spec(), smem_spec(), any_spec()],
        out_specs=[vmem_spec()] * 2,
        out_shape=[
            jax.ShapeDtypeStruct((spans[0][1] // n_rep, B, B), BF),
            jax.ShapeDtypeStruct((max(total_rows - spans[0][1] // n_rep, 1), B, B), BF),
        ],
        scratch_shapes=[
            pltpu.SMEM((spd,), jnp.int32),
            pltpu.VMEM((total_rows, B, B), F32),
            pltpu.SemaphoreType.DMA(()),
        ],
        compiler_params=params(),
        cost_estimate=cost(1, 3_000_000),
        name="quarter_blocks",
    )(slot_block, info, master)


def plan_kernel(spd, n_seq, spans, n_after, slot_block, info, master, *rest):
    order, blocks, where, *rest = rest[n_after:]
    outs, (stage, sem) = rest[: len(spans)], rest[len(spans) :]
    my_seq = info[0]
    sort_slots(slot_block, my_seq * spd, order, my_seq * spd, spd)

    def fetch(k, carry):
        pltpu.make_async_copy(master.at[order[my_seq * spd + k]], stage.at[k], sem).start()
        return carry

    lax.fori_loop(0, spd, fetch, 0)

    def group(s, carry):
        sort_slots(slot_block, s * spd, order, s * spd, spd)

        def number(k, inner):
            n = slot_block[s * spd + order[s * spd + k]]
            blocks[s * spd + k] = n
            where[n] = (s << 8) | k
            return inner

        return lax.fori_loop(0, spd, number, carry)

    lax.fori_loop(0, n_seq, group, 0)
    pltpu.make_async_copy(stage, stage, sem).wait()
    for out, (lo, count) in zip(outs, spans):

        def convert(k, carry, out=out, lo=lo):
            out[k] = stage[lo + k].astype(BF)
            return carry

        lax.fori_loop(0, count, convert, 0)


def plan_slots(slot_block, info, master, spans, n_seq, after):
    spd = master.shape[0]
    table = jax.ShapeDtypeStruct((n_seq * spd,), jnp.int32)
    return pl.pallas_call(
        functools.partial(plan_kernel, spd, n_seq, spans, len(after)),
        in_specs=[smem_spec(), smem_spec(), any_spec()] + [any_spec()] * len(after),
        out_specs=[smem_spec()] * 3 + [vmem_spec()] * len(spans),
        out_shape=[table, table, table]
        + [jax.ShapeDtypeStruct((count, B, B), BF) for unused, count in spans],
        scratch_shapes=[pltpu.VMEM((spd, B, B), F32), pltpu.SemaphoreType.DMA(())],
        compiler_params=params(),
        cost_estimate=cost(1, 12_000_000),
        name="plan_slots",
    )(slot_block, info, master, *after)


def swap(value, axis, bit):
    size = lax.axis_size(axis)
    return lax.ppermute(value, axis, [(i, i ^ bit) for i in range(size)])


def rep_swap(value, step):
    n_rep, n_seq = lax.axis_size("rep"), lax.axis_size("seq")
    bits = rep_orders(n_rep)
    pairs = []
    for r in range(n_rep):
        for s in range(n_seq):
            pairs.append((r * n_seq + s, (r ^ bits[s % 2][step]) * n_seq + s))
    return lax.ppermute(value, ("rep", "seq"), pairs)


def rep_orders(n_rep):
    bits = [1 << i for i in range(n_rep.bit_length() - 1)]
    return bits, bits[::-1]


def held_order(n_rep):
    result = []
    for bits in rep_orders(n_rep):
        held = [0]
        for bit in bits:
            held = held + [e ^ bit for e in held]
        result.append(held)
    return result


def shift_seq(value, step):
    n_seq = lax.axis_size("seq")
    pairs = [(i, i + 2 * step) for i in range(n_seq) if 0 <= i + 2 * step < n_seq]
    return lax.ppermute(value, "seq", pairs)


def relay_kernel(n_in, jobs, info, *rest):
    ins, outs = rest[:n_in], rest[-len(jobs) :]
    z = info[0] // 2
    for out, (rows, parts) in zip(outs, jobs):
        for lo, size, cases in parts:
            for zs, src, at in cases:
                if not zs:
                    out[lo : lo + size] = ins[src][at : at + size]
                    continue

                @pl.when(functools.reduce(lambda a, b: a | b, [z == v for v in zs]))
                def _(src=src, at=at, lo=lo, size=size, out=out):
                    out[lo : lo + size] = ins[src][at : at + size]


def relay(info, ins, jobs, after=()):
    extra = list(after)
    return pl.pallas_call(
        functools.partial(relay_kernel, len(ins), jobs),
        in_specs=[smem_spec()] + [vmem_spec()] * len(ins) + [any_spec()] * len(extra),
        out_specs=[vmem_spec()] * len(jobs),
        out_shape=[jax.ShapeDtypeStruct((rows, B, B), BF) for rows, unused in jobs],
        compiler_params=params(),
        cost_estimate=cost(1, 1),
        name="relay",
    )(info, *ins, *extra)


def gather_line(quarter, extra, info, my_seq, plan):
    q = quarter.shape[0]
    z = my_seq // 2
    core = my_seq % 2
    n_rep = lax.axis_size("rep")

    def pair(first, second, after=()):
        return relay(info, [first, second], [(2 * q, [(0, q, [((), 0, 0)]), (q, q, [((), 1, 0)])])], after)[0]

    def nearer(at):
        return [((0, 1), 1, at), ((2, 3), 0, at)]

    up, down = shift_seq(quarter, 1), shift_seq(quarter, -1)
    (near,) = relay(info, [up, down], [(q, [(0, q, nearer(0))])])
    up2, down2 = shift_seq(up, 1), shift_seq(down, -1)
    near1 = rep_swap(near, 0)
    near_pair = pair(near, near1)
    near2 = rep_swap(near_pair, 1)
    order, blocks, where, *owns = plan(near_pair)
    own = owns[0]
    size = extra.shape[0]
    keep = (size, [(0, size, [((), 2, 0)])])
    mid, held = relay(info, [up2, down2, extra], [(q, [(0, q, nearer(0))]), keep], [order])
    late_two = swap(held, "seq", 4)
    ends = lax.ppermute(mid, "seq", [(2, 0), (3, 1), (4, 6), (5, 7)])
    mid1 = rep_swap(mid, 0)
    mid_pair = pair(mid, mid1, [near2])
    mid2 = rep_swap(mid_pair, 1)
    far, held = relay(
        info,
        [up, down, ends, extra],
        [
            (q, [(0, q, [((0, 3), 2, 0), ((1,), 0, 0), ((2,), 1, 0)])]),
            (size, [(0, size, [((), 3, 0)])]),
        ],
        [mid_pair, late_two],
    )
    late = [swap(held, "seq", 2), late_two, swap(held, "seq", 6)]
    far1 = rep_swap(far, 0)
    sib_near = [swap(near_pair, "seq", 1), swap(near2, "seq", 1)]
    sib = swap(own, "seq", 1)
    far_pair = pair(far, far1, [mid2, mid_pair, sib] + sib_near)
    far2 = rep_swap(far_pair, 1)
    sib_mid = [swap(mid_pair, "seq", 1), swap(mid2, "seq", 1)]
    far_sib = [swap(far_pair, "seq", 1), swap(far2, "seq", 1)]
    n = len(late)
    (here,) = relay(info, late, [(n * size, [(i * size, size, [((), i, 0)]) for i in range(n)])], [far_pair])
    my_rep = info[1]
    z_near = jnp.where(z < 2, z + 1, z - 1)
    z_mid = jnp.where(z < 2, z + 2, z - 2)
    z_far = jnp.where(z % 2 == 0, 3, 0)
    half = n_rep // 2
    result = [part_of(own, z, core), part_of(sib, z, 1 - core)]
    for zs, mine, theirs in (
        (z_near, (near_pair, near2), sib_near),
        (z_mid, (mid_pair, mid2), sib_mid),
        (z_far, (far_pair, far2), far_sib),
    ):
        for part in range(2):
            result.append(part_of(mine[part], zs, core, part * half, my_rep, q))
            result.append(part_of(theirs[part], zs, 1 - core, part * half, my_rep, q))
    return (order, blocks, where, owns), result, (here, tuple(z ^ delta for delta in range(1, 4)))


def gather_direct(quarter, own, my_seq, my_rep):
    z = my_seq // 2
    core = my_seq % 2
    n_rep, n_z = lax.axis_size("rep"), lax.axis_size("seq") // 2
    sib = swap(own, "seq", 1)
    result = [part_of(own, z, core), part_of(sib, z, 1 - core)]
    q = quarter.shape[0]
    for delta in range(1, n_z):
        held = swap(quarter, "seq", 2 * delta)
        for step in range(len(rep_orders(n_rep)[0])):
            held = jnp.concatenate([held, rep_swap(held, step)], axis=0)
        result.append(part_of(held, z ^ delta, core, 0, my_rep, q))
        result.append(part_of(swap(held, "seq", 1), z ^ delta, 1 - core, 0, my_rep, q))
    return result


def part_of(buf, z, core, part=0, rep=0, quarter=0, rows=None):
    return buf, rows or (0, buf.shape[0]), quarter, (z, core, part, rep)


def late_parts(late, own, sib, my_seq, my_rep):
    here, planes = late
    n_rep = lax.axis_size("rep")
    z, core = my_seq // 2, my_seq % 2
    q = here.shape[0] // len(planes)
    result = [part_of(own, z, core), part_of(sib, z, 1 - core)]
    for e in range(n_rep):
        held = swap(here, "rep", e) if e else here
        other = swap(held, "seq", 1)
        for i, plane in enumerate(planes):
            rows = (i * q, q)
            result.append(part_of(held, plane, core, 0, my_rep ^ e, q, rows))
            result.append(part_of(other, plane, 1 - core, 0, my_rep ^ e, q, rows))
    return result


def describe(spans_parts, spd):
    bufs, layout, rows = [], [], []
    for (first, unused), parts in spans_parts:
        for buf, (row, count), quarter, (z, core, part, rep) in parts:
            index = [i for i, b in enumerate(bufs) if b is buf]
            if not index:
                bufs.append(buf)
                index = [len(bufs) - 1]
            layout.append((index[0], row, count, quarter))
            rows += [(z * 2 + core) * spd + first, core, part, rep]
    return jnp.stack([jnp.asarray(r, jnp.int32) for r in rows]), bufs, tuple(layout)


def load_weights(first_block, n_rep, layout, tables, blocks, desc, bufs, w_ref, sems):
    w_i, w_j, held = tables
    for index, (b, row0, count, quarter) in enumerate(layout):
        base, core, part, rep = (desc[4 * index + i] for i in range(4))
        size = quarter or count
        for step in range(count // size):
            place = base
            if quarter:
                place = base + (held[core * n_rep + part + step] ^ rep) * quarter

            def body(e, carry, buf=bufs[b], row=row0 + step * size, place=place):
                n = blocks[place + e] - first_block

                @pl.when((n >= 0) & (n < PER_LAYER))
                def _():
                    code = w_i[n]
                    at = pl.multiple_of((code & 3) * B, B)
                    col = pl.multiple_of(w_j[n] * B, B)
                    pltpu.make_async_copy(
                        buf.at[row + e], w_ref.at[pl.ds(at, B), pl.ds(col, B)], sems.at[code >> 2]
                    ).start()

                return carry

            lax.fori_loop(0, size, body, 0)


def weight_tables(n_rep):
    return [jnp.asarray(t) for t in (W_I, W_J, np.array(sum(held_order(n_rep), []), np.int32))]


def first_fwd_kernel(n_rep, nbuf, quarters, w_i, w_j, held, blocks, desc, x_ref, par, *rest):
    bufs = rest[:nbuf]
    out_ref, cls_ref, qkv_ref, p_ref, r1_ref, r2_ref, gp_ref, lt_ref, w, a_ref, sems = rest[nbuf:]
    first = pl.program_id(0) == 0

    @pl.when(first)
    def _():
        load_weights(0, n_rep, quarters, (w_i, w_j, held), blocks, desc, bufs, w, sems)

    def wait(mat):
        @pl.when(first)
        def _():
            wait_weights(w, sems, mat)

    xb = x_ref[...]
    out = fwd_tile(
        xb.astype(F32), xb, w, par, None, qkv_ref, p_ref, r1_ref, r2_ref, gp_ref, lt_ref, a_ref, wait
    ).astype(BF)
    out_ref[...] = out
    for s in range(TILE // SEG_LEN):
        cls_ref[0, s : s + 1, :] = out[s * SEG_LEN : s * SEG_LEN + 1, :]


def first_fwd(n_rep, weights, tokens, par):
    blocks, desc, bufs, quarters = weights
    rows = tokens.shape[0]
    steps = rows // TILE
    nseg = TILE // SEG_LEN
    return pl.pallas_call(
        functools.partial(first_fwd_kernel, n_rep, len(bufs), quarters),
        grid_spec=pltpu.PrefetchScalarGridSpec(
            num_scalar_prefetch=5,
            grid=(steps,),
            in_specs=[row_spec(D), whole_spec((1, NPAR))] + [any_spec()] * len(bufs),
            out_specs=[
                row_spec(D),
                pl.BlockSpec((1, nseg, D), lambda i, *_: (i, 0, 0)),
                row_spec(3 * D),
                row_spec(NPAIR * 256),
                row_spec(D),
                row_spec(D),
                row_spec(FF),
                pl.BlockSpec((L_ROWS, TILE), lambda i, *_: (0, i)),
            ],
            scratch_shapes=[
                pltpu.VMEM((D, W_COLS), BF),
                pltpu.VMEM((TILE, D), BF),
                pltpu.SemaphoreType.DMA((4,)),
            ],
        ),
        out_shape=[
            jax.ShapeDtypeStruct((rows, D), BF),
            jax.ShapeDtypeStruct((steps, nseg, D), BF),
            jax.ShapeDtypeStruct((rows, 3 * D), BF),
            jax.ShapeDtypeStruct((rows, NPAIR * 256), BF),
            jax.ShapeDtypeStruct((rows, D), F32),
            jax.ShapeDtypeStruct((rows, D), F32),
            jax.ShapeDtypeStruct((rows, FF), BF),
            jax.ShapeDtypeStruct((L_ROWS, rows), BF),
        ],
        compiler_params=params(),
        cost_estimate=cost(15_000_000_000, 60_000_000),
        name="first_forward",
    )(*weight_tables(n_rep), blocks, desc, tokens, par, *bufs)


def first_bwd_kernel(
    n_rep, nbuf, quarters, n_after, w_i, w_j, held, blocks, desc, cot_ref, back_ref, out_ref, par, *rest
):
    qkv_ref, p_ref, r1_ref, r2_ref, gp_ref = rest[:5]
    bufs = rest[5 : 5 + nbuf]
    hid_ref, r_ref, dx_ref, pg_ref, w, da_ref, rows_ref, sems = rest[5 + nbuf + n_after :]
    step = pl.program_id(0)
    first = step == 0

    @pl.when(first)
    def _():
        load_weights(0, n_rep, quarters, (w_i, w_j, held), blocks, desc, bufs, w, sems)
        pg_ref[...] = jnp.zeros_like(pg_ref)
        rows_ref[...] = jnp.sum(back_ref[...].astype(F32), axis=0)

    def wait(mat):
        @pl.when(first)
        def _():
            wait_weights(w, sems, mat)

    dout = cot_ref[...].astype(F32)
    out = out_ref[...]
    index = lax.broadcasted_iota(jnp.int32, (TILE, 1), 0)
    nseg = TILE // SEG_LEN
    for s in range(nseg):
        row = rows_ref[pl.ds(step * nseg + s, 1), :]
        dout = jnp.where(index == s * SEG_LEN, row[:, :D], dout)
        out = jnp.where(index == s * SEG_LEN, row[:, D:], out.astype(F32)).astype(BF)
    hid_ref[...] = out
    dx_ref[...] = bwd_tile(
        dout, w, par, qkv_ref, p_ref, r1_ref, r2_ref, gp_ref, r_ref, pg_ref, da_ref, wait
    )


def first_bwd(n_rep, weights, cot, back, out_one, par, kept, after):
    blocks, desc, bufs, quarters = weights
    rows = cot.shape[0]
    steps = rows // TILE
    nseg = TILE // SEG_LEN
    return pl.pallas_call(
        functools.partial(first_bwd_kernel, n_rep, len(bufs), quarters, len(after)),
        grid_spec=pltpu.PrefetchScalarGridSpec(
            num_scalar_prefetch=5,
            grid=(steps,),
            in_specs=[
                row_spec(D),
                whole_spec(back.shape),
                row_spec(D),
                whole_spec((1, NPAR)),
                row_spec(3 * D),
                row_spec(NPAIR * 256),
                row_spec(D),
                row_spec(D),
                row_spec(FF),
            ]
            + [any_spec()] * (len(bufs) + len(after)),
            out_specs=[row_spec(D), row_spec(R_COLS), row_spec(D), whole_spec((1, NPAR))],
            scratch_shapes=[
                pltpu.VMEM((D, W_COLS), BF),
                pltpu.VMEM((TILE, D), BF),
                pltpu.VMEM((steps * nseg, 2 * D), F32),
                pltpu.SemaphoreType.DMA((4,)),
            ],
        ),
        out_shape=[
            jax.ShapeDtypeStruct((rows, D), BF),
            jax.ShapeDtypeStruct((rows, R_COLS), BF),
            jax.ShapeDtypeStruct((rows, D), F32),
            jax.ShapeDtypeStruct((1, NPAR), F32),
        ],
        compiler_params=params(),
        cost_estimate=cost(30_000_000_000, 60_000_000),
        name="first_backward",
    )(*weight_tables(n_rep), blocks, desc, cot, back, out_one, par, *kept, *bufs, *after)


def second_kernel(
    n_rep, nbuf, quarters, w_i, w_j, held, blocks, desc, doc, got, pos, par, *rest
):
    bufs = rest[:nbuf]
    reply_ref, state_ref, lt_ref, r_ref, dx_ref, pg_ref = rest[nbuf : nbuf + 6]
    w, a_ref, qkv_ref, p_ref, r1_ref, r2_ref, gp_ref, x_ref, cot_ref, sems = rest[nbuf + 6 :]
    load_weights(PER_LAYER, n_rep, quarters, (w_i, w_j, held), blocks, desc, bufs, w, sems)
    pg_ref[...] = jnp.zeros_like(pg_ref)
    reply_ref[...] = jnp.zeros_like(reply_ref)
    x_ref[...] = jnp.zeros_like(x_ref)
    cot_ref[...] = jnp.zeros_like(cot_ref)
    start, length = doc[0], doc[1]
    for j in range(0, DOC_LONG, 16):
        rows = slice(j, j + 16)
        x_ref[rows, :] = pos[rows, :]

        @pl.when(j < length)
        def _(j=j, rows=rows):
            at = pl.ds(pl.multiple_of(start + j, 16), 16)
            x_ref[rows, :] = pos[rows, :] + got[at, :D].astype(F32)
            cot_ref[rows, :] = got[at, D:].astype(F32)

    key = lax.broadcasted_iota(jnp.int32, (1, SEG_LEN), 1)
    key_bias = jnp.where(key < length, 0.0, MASKED_SCORE).astype(F32)
    x32 = x_ref[...]
    y = fwd_tile(
        x32,
        x32.astype(BF),
        w,
        par,
        key_bias,
        qkv_ref,
        p_ref,
        r1_ref,
        r2_ref,
        gp_ref,
        lt_ref,
        a_ref,
        lambda mat: wait_weights(w, sems, mat),
    )
    row = lax.broadcasted_iota(jnp.int32, (SEG_LEN, 1), 0)
    y = jnp.where(row < length, y, 0.0)
    state_ref[...] = y[:DOC_LONG].astype(BF)
    dx = bwd_tile(
        cot_ref[...],
        w,
        par,
        qkv_ref,
        p_ref,
        r1_ref,
        r2_ref,
        gp_ref,
        r_ref,
        pg_ref,
        a_ref,
        lambda mat: None,
    )
    dx = jnp.where(row < length, dx, 0.0)
    dx_ref[...] = dx[:DOC_LONG]
    for j in range(0, DOC_LONG, 16):

        @pl.when(j < length)
        def _(j=j):
            at = pl.ds(pl.multiple_of(start + j, 16), 16)
            reply_ref[at, :D] = dx[j : j + 16].astype(BF)
            reply_ref[at, D:] = y[j : j + 16].astype(BF)


def second_layer(n_rep, weights, doc, got, pos, par):
    blocks, desc, bufs, quarters = weights
    rows = SEG_LEN
    group = got.shape[0]
    return pl.pallas_call(
        functools.partial(second_kernel, n_rep, len(bufs), quarters),
        in_specs=[smem_spec()] * 6 + [vmem_spec()] * 3 + [any_spec()] * len(bufs),
        out_specs=[vmem_spec()] * 6,
        scratch_shapes=[
            pltpu.VMEM((D, W_COLS), BF),
            pltpu.VMEM((rows, D), BF),
            pltpu.VMEM((rows, 3 * D), BF),
            pltpu.VMEM((rows, NPAIR * 256), BF),
            pltpu.VMEM((rows, D), F32),
            pltpu.VMEM((rows, D), F32),
            pltpu.VMEM((rows, FF), BF),
            pltpu.VMEM((rows, D), F32),
            pltpu.VMEM((rows, D), F32),
            pltpu.SemaphoreType.DMA((4,)),
        ],
        out_shape=[
            jax.ShapeDtypeStruct((group, 2 * D), BF),
            jax.ShapeDtypeStruct((DOC_LONG, D), BF),
            jax.ShapeDtypeStruct((L_ROWS, rows), BF),
            jax.ShapeDtypeStruct((rows, R_COLS), BF),
            jax.ShapeDtypeStruct((DOC_LONG, D), F32),
            jax.ShapeDtypeStruct((1, NPAR), F32),
        ],
        compiler_params=params(),
        cost_estimate=cost(8_000_000_000, 40_000_000),
        name="second_layer",
    )(*weight_tables(n_rep), blocks, desc, doc, got, pos, par, *bufs)


PRODUCTS = (
    (L_X, R_QKV, 9, 0),
    (L_A, R_OUT, 3, 27),
    (L_H, R_UP, 12, 36),
    (L_E, R_DOWN, 3, 72),
    (L_E + D, R_DOWN, 3, 81),
    (L_E + 2 * D, R_DOWN, 3, 90),
    (L_E + 3 * D, R_DOWN, 3, 99),
)


def send_block(src, n, ctx, where, info, outs, sem):
    spd, unused, chunks = ctx
    at = where[n]
    k = at & 255
    target = (at >> 9) ^ (info[0] >> 1)
    mine = ((at >> 8) & 1) == (info[0] & 1)
    for c, (first, m) in enumerate(chunks):
        inside = (k >= first) & (k < first + m)
        for side, cond in ((0, inside & jnp.logical_not(mine)), (1, inside & mine)):

            @pl.when(cond)
            def _(c=c, side=side, first=first):
                pltpu.make_async_copy(src, outs[2 * c + side].at[target, k - first], sem).start()


def all_products(lt, r, stage, base, ctx, where, info, outs, sem, before=None):
    for lrow, rcol, across, first in PRODUCTS:
        if before is not None:
            before(lrow)
        for j in range(across):
            value = mm(lt[lrow : lrow + D, :], r[:, rcol + j * B : rcol + (j + 1) * B]).astype(BF)
            for i in range(D // B):
                local = first + i * across + j
                stage[local] = value[i * B : (i + 1) * B]
                send_block(stage.at[local], base + local, ctx, where, info, outs, sem)


def wait_blocks(stage, sem, count):
    part = stage.at[pl.ds(0, count)]
    pltpu.make_async_copy(part, part, sem).wait()


def second_grad_kernel(ctx, n_empty, n_after, where, info, lt, r, *rest):
    outs, (stage, zero, sem) = rest[n_after:-3], rest[-3:]
    zero[...] = jnp.zeros_like(zero)
    for n in range(NBLK, NBLK + n_empty):
        send_block(zero.at[n - NBLK], n, ctx, where, info, outs, sem)
    all_products(lt, r, stage, PER_LAYER, ctx, where, info, outs, sem)
    wait_blocks(stage, sem, PER_LAYER)
    if n_empty:
        wait_blocks(zero, sem, n_empty)


def chunk_arrays(ctx):
    return [jax.ShapeDtypeStruct((ctx[1], m, B, B), BF) for unused, m in ctx[2] for side in range(2)]


def second_grad(ctx, where, info, lt, r, after):
    shapes = chunk_arrays(ctx)
    n_empty = where.shape[0] - NBLK
    return pl.pallas_call(
        functools.partial(second_grad_kernel, ctx, n_empty, len(after)),
        in_specs=[smem_spec()] * 2 + [vmem_spec()] * 2 + [any_spec()] * len(after),
        out_specs=[any_spec()] * len(shapes),
        out_shape=shapes,
        scratch_shapes=[
            pltpu.VMEM((PER_LAYER, B, B), BF),
            pltpu.VMEM((max(n_empty, 1), B, B), BF),
            pltpu.SemaphoreType.DMA(()),
        ],
        compiler_params=params(),
        cost_estimate=cost(2_000_000_000, 18_000_000),
        name="second_gradients",
    )(where, info, lt, r, *after)


def first_grad_kernel(ctx, n_after, where, info, lt, r, *rest):
    n_out = 2 * len(ctx[2])
    outs = rest[n_out + n_after : 2 * n_out + n_after]
    lt_s, r_s, stage, sem, sems = rest[2 * n_out + n_after :]
    spans = ((L_X, L_A, R_QKV, R_OUT), (L_A, L_H, R_OUT, R_UP), (L_H, L_E, R_UP, R_DOWN), (L_E, L_ROWS, R_DOWN, R_COLS))
    copies = []
    for i, (la, lb, ra, rb) in enumerate(spans):
        pair = (
            pltpu.make_async_copy(lt.at[la:lb], lt_s.at[la:lb], sems.at[2 * i]),
            pltpu.make_async_copy(r.at[:, ra:rb], r_s.at[:, ra:rb], sems.at[2 * i + 1]),
        )
        for copy in pair:
            copy.start()
        copies.append((la, pair))

    def before(lrow):
        for la, pair in copies:
            if la == lrow:
                for copy in pair:
                    copy.wait()

    all_products(lt_s, r_s, stage, 0, ctx, where, info, outs, sem, before)
    wait_blocks(stage, sem, PER_LAYER)


def first_grad(ctx, where, info, lt, r, arrays, after):
    n = len(arrays)
    return pl.pallas_call(
        functools.partial(first_grad_kernel, ctx, len(after)),
        in_specs=[smem_spec()] * 2 + [any_spec()] * (2 + n + len(after)),
        out_specs=[any_spec()] * n,
        out_shape=[jax.ShapeDtypeStruct(a.shape, BF) for a in arrays],
        scratch_shapes=[
            pltpu.VMEM(lt.shape, BF),
            pltpu.VMEM(r.shape, BF),
            pltpu.VMEM((PER_LAYER, B, B), BF),
            pltpu.SemaphoreType.DMA(()),
            pltpu.SemaphoreType.DMA((8,)),
        ],
        input_output_aliases={4 + i: i for i in range(n)},
        compiler_params=params(),
        cost_estimate=cost(15_000_000_000, 40_000_000),
        name="first_gradients",
    )(where, info, lt, r, *arrays, *after)


def halve_kernel(step, n_after, info, a_ref, b_ref, *rest):
    send_ref, keep_ref = rest[n_after:]
    half = send_ref.shape[2]
    high = high_bit(info, step)
    for side, ref in ((1 - high, send_ref), (high, keep_ref)):
        rows = pl.ds(pl.multiple_of(side * half, half), half)
        ref[...] = a_ref[:, :, rows, :] + b_ref[:, :, rows, :]


def high_bit(info, step):
    orders = rep_orders(4)
    core, rep = info[0] % 2, info[1]
    bit = jnp.where(core == 0, orders[0][step], orders[1][step])
    return jnp.where((rep & bit) != 0, 1, 0)


def halve(info, step, a, b, after):
    n_target, m, rows, cols = a.shape
    shape = jax.ShapeDtypeStruct((n_target, m, rows // 2, cols), BF)
    group = 2 if n_target * m <= 64 else 1

    def spec(r):
        return pl.BlockSpec((group, m, r, cols), lambda i, *_: (i, 0, 0, 0))

    return pl.pallas_call(
        functools.partial(halve_kernel, step, len(after)),
        grid_spec=pltpu.PrefetchScalarGridSpec(
            num_scalar_prefetch=1,
            grid=(n_target // group,),
            in_specs=[spec(rows)] * 2 + [any_spec()] * len(after),
            out_specs=[spec(rows // 2)] * 2,
        ),
        out_shape=[shape, shape],
        compiler_params=params(),
        cost_estimate=cost(1, 1),
        name="halve",
    )(info, a, b, *after)


def spread_kernel(n_after, a_ref, b_ref, *rest):
    for i, out in enumerate(rest[n_after:]):
        out[...] = a_ref[i] + b_ref[i]


def spread(a, b, after):
    shape = jax.ShapeDtypeStruct(a.shape[1:], BF)
    return pl.pallas_call(
        functools.partial(spread_kernel, len(after)),
        in_specs=[vmem_spec()] * 2 + [any_spec()] * len(after),
        out_specs=[vmem_spec()] * a.shape[0],
        out_shape=[shape] * a.shape[0],
        compiler_params=params(),
        cost_estimate=cost(1, 1),
        name="spread",
    )(a, b, *after)


def total_kernel(count, *rest):
    total = rest[0][...].astype(F32)
    for ref in rest[1:count]:
        total = total + ref[...].astype(F32)
    rest[-1][...] = total.astype(BF)


def total(parts, after):
    shape = jax.ShapeDtypeStruct(parts[0].shape, BF)
    return pl.pallas_call(
        functools.partial(total_kernel, len(parts)),
        in_specs=[vmem_spec()] * len(parts) + [any_spec()] * len(after),
        out_specs=vmem_spec(),
        out_shape=shape,
        compiler_params=params(),
        cost_estimate=cost(1, 1),
        name="total",
    )(*parts, *after)


def shampoo_kernel(n_rep, spd, first, n_previous, order, info, *rest):
    pieces, stats = rest[:n_rep], rest[n_rep : n_rep + 5]
    outs, token, (ins_ref, outs_ref, g_ref, ins_sem, outs_sem) = rest[-10:-6], rest[-6], rest[-5:]
    token[...] = jnp.zeros_like(token)
    count = pieces[0].shape[0]
    slots = [order[info[0] * spd + first + i] for i in range(count)]
    for i, slot in enumerate(slots):
        for a, stat in enumerate(stats):
            pltpu.make_async_copy(stat.at[slot], ins_ref.at[i, a], ins_sem.at[i]).start()
    orders = rep_orders(n_rep)
    size = B // n_rep
    places = []
    for e in range(n_rep):
        rep = info[1] ^ e
        place = jnp.int32(0)
        for level in range(len(orders[0])):
            bit = jnp.where(info[0] % 2 == 0, orders[0][level], orders[1][level])
            place = place + jnp.where((rep & bit) != 0, B >> (level + 1), 0)
        places.append(pl.multiple_of(place, size))
    for i, slot in enumerate(slots):
        for place, piece in zip(places, pieces):
            g_ref[i, pl.ds(place, size), :] = piece[i]
        g = g_ref[i]
        pltpu.make_async_copy(ins_ref.at[i], ins_ref.at[i], ins_sem.at[i]).wait()
        left, right, lroot, rroot, master = (ins_ref[i, a] for a in range(5))
        part = mm(lroot.astype(BF), g)
        outs_ref[i, 0] = g.astype(F32)
        outs_ref[i, 1] = DECAY * left + (1.0 - DECAY) * mm_t(g, g)
        outs_ref[i, 2] = DECAY * right + (1.0 - DECAY) * tmm(g, g)
        direction = mm(part.astype(BF), rroot.astype(BF))
        scale = BLOCK_RATE * lax.rsqrt(jnp.mean(direction * direction) + RMS_EPS)
        outs_ref[i, 3] = master - direction * scale
        for a, out in enumerate(outs):
            pltpu.make_async_copy(outs_ref.at[i, a], out.at[slot], outs_sem).start()
    pltpu.make_async_copy(outs_ref, outs_ref, outs_sem).wait()


def shampoo(order, info, spd, first, pieces, stats, previous, after):
    count = pieces[0].shape[0]
    n_rep = len(pieces)
    n_in = 2 + n_rep + len(stats)
    return pl.pallas_call(
        functools.partial(shampoo_kernel, n_rep, spd, first, len(previous)),
        in_specs=[smem_spec()] * 2
        + [vmem_spec()] * n_rep
        + [any_spec()] * (len(stats) + len(previous) + len(after)),
        out_specs=[any_spec()] * 4 + [vmem_spec()],
        out_shape=[jax.ShapeDtypeStruct((spd, B, B), F32)] * 4 + [jax.ShapeDtypeStruct((8, 128), F32)],
        scratch_shapes=[
            pltpu.VMEM((count, 5, B, B), F32),
            pltpu.VMEM((count, 4, B, B), F32),
            pltpu.VMEM((count, B, B), BF),
            pltpu.SemaphoreType.DMA((count,)),
            pltpu.SemaphoreType.DMA(()),
        ],
        input_output_aliases={n_in + i: i for i in range(len(previous))},
        compiler_params=params(),
        cost_estimate=cost(1, 1),
        name="shampoo",
    )(order, info, *pieces, *stats, *previous, *after)


def reduce_pipeline(ctx, chunks, ready, idle, stats, after):
    order, info, spd, n_rep = ctx
    state = {}
    results = ()
    for batch in range(len(chunks) + 6):
        for run in ready.get(batch, ()):
            after = run(after)
        for i in range(len(chunks))[::-1]:
            stage = batch - i
            if chunks[i] is None or stage < 1:
                continue
            first, m, products = chunks[i]
            if stage == 1:
                got, own = state[i]
                send, keep = halve(info, 0, own, got, after)
                state[i] = (rep_swap(send, 0), keep)
                after = (keep,)
            elif stage == 2:
                got, kept = state[i]
                send, keep = halve(info, 1, kept, got, after)
                state[i] = (rep_swap(send, 1), keep)
                after = (keep,)
            elif stage == 3:
                got, kept = state[i]
                parts = spread(kept, got, after)
                moved = [swap(part, "seq", 2 * d) for d, part in enumerate(parts) if d]
                state[i] = [parts[0]] + moved
                after = (parts[0],)
            elif stage == 4:
                mine = total(state[i], after)
                state[i] = [mine] + [swap(mine, "rep", e) for e in range(1, n_rep)]
                after = (mine,)
        done = batch - 6
        if 0 <= done < len(chunks) and chunks[done] is not None:
            first = chunks[done][0]
            *results, token = shampoo(order, info, spd, first, state[done], stats, results, after)
            after = (token,)
        for run in idle.get(batch, ()):
            after = run(after)
        if batch < len(chunks) and chunks[batch] is not None:
            sib, own = chunks[batch][2]()
            state[batch] = (swap(sib, "seq", 1), own)
    return results, after


def small_kernel(old, grads, *rest):
    out = rest[-1]
    rows = 2 * NPAR // 128
    for part in (slice(0, rows), slice(rows, None)):
        g = grads[part, :]
        out[part, :] = old[part, :] - SMALL_RATE * g * lax.rsqrt(jnp.mean(g * g) + RMS_EPS)


def add_kernel(a, b, *rest):
    rest[-1][...] = a[...] + b[...]


def add(a, b, after):
    return pl.pallas_call(
        add_kernel,
        in_specs=[vmem_spec()] * 2 + [any_spec()] * len(after),
        out_specs=vmem_spec(),
        out_shape=jax.ShapeDtypeStruct(a.shape, F32),
        compiler_params=params(),
        cost_estimate=cost(1, 1),
        name="add",
    )(a, b, *after)


def small_step(old, grads, after):
    shape = (old.shape[0] // 128, 128)
    return pl.pallas_call(
        small_kernel,
        in_specs=[vmem_spec()] * 2 + [any_spec()] * len(after),
        out_specs=vmem_spec(),
        out_shape=jax.ShapeDtypeStruct(shape, F32),
        compiler_params=params(),
        cost_estimate=cost(1, 1_000_000),
        name="small_step",
    )(old.reshape(shape), grads.reshape(shape), *after).reshape(-1)


def split_slots(spd):
    if spd == 28:
        return ((0, 20), (20, 8)), ((0, 10), (10, 10), (20, 8))
    return ((0, spd),), ((0, spd),)


def shards(
    tokens,
    cotangent,
    doc_lengths,
    doc_owners,
    small_params,
    slot_block,
    master_blocks,
    left_stats,
    right_stats,
    left_roots,
    right_roots,
):
    seg_dev = tokens.shape[0] // SEG_LEN
    n_seq, n_rep = lax.axis_size("seq"), lax.axis_size("rep")
    my_seq = lax.axis_index("seq").astype(jnp.int32)
    my_rep = lax.axis_index("rep").astype(jnp.int32)
    spd = master_blocks.shape[0]
    n_target = n_seq // 2
    info = jnp.stack([my_seq, my_rep])
    par_one = small_params[None, :NPAR]
    par_two = small_params[None, NPAR : 2 * NPAR]
    position = small_params[2 * NPAR :].reshape(DOC_LONG, D)

    line = n_seq == 8 and n_rep == 4 and spd == 28
    spans, chunk_spans = split_slots(spd) if line else (((0, spd),), ((0, spd),))
    ctx = (spd, n_target, chunk_spans)
    quarter, extra = quarter_blocks(slot_block, info, master_blocks, spans, n_rep)

    lengths_row = doc_lengths[0]
    owners_row = doc_owners[0]
    starts_row = jnp.cumsum(lengths_row) - lengths_row
    first_seg = my_seq * seg_dev
    inside = (starts_row <= first_seg) & (first_seg < starts_row + lengths_row)
    owner = jnp.sum(jnp.where(inside, owners_row, 0))
    target = (jnp.arange(n_seq, dtype=jnp.int32) == owner).astype(BF)[:, None, None]
    mine = (owners_row == my_seq) & (lengths_row > 0)
    doc = jnp.stack([jnp.sum(jnp.where(mine, starts_row, 0)), jnp.sum(jnp.where(mine, lengths_row, 0))])
    doc = doc.astype(jnp.int32)

    def to_owner(rows):
        sent = target * rows[None]
        got = lax.all_to_all(sent, "seq", split_axis=0, concat_axis=0, tiled=True)
        return got.reshape(n_seq * seg_dev, 2 * D)

    cot_first = cotangent.reshape(seg_dev, SEG_LEN, D)[:, 0, :]

    def plan(after):
        early = (after, par_one, par_two, position, target, doc, cot_first)
        return plan_slots(slot_block, info, master_blocks, spans, n_seq, early)

    stats = (left_stats, right_stats, left_roots, right_roots, master_blocks)
    if line:
        (order, blocks, where, owns), parts_one, late = gather_line(
            quarter, extra, info, my_seq, plan
        )
        late_sib = swap(owns[1], "seq", 1)
    else:
        order, blocks, where, *owns = plan(quarter)
        parts_one, late, late_sib = gather_direct(quarter, owns[0], my_seq, my_rep), None, None

    def layers(ahead):
        layers_parts = [(spans[0], parts_one)]
        first_parts = list(layers_parts)

        if line:
            layers_parts.append((spans[1], late_parts(late, owns[1], late_sib, my_seq, my_rep)))
        if not ahead:
            first_parts = layers_parts
        first_desc, first_bufs, first_layout = describe(first_parts, spd)
        one = (blocks, first_desc, first_bufs, first_layout)
        out_one, cls, *kept, lt_one = first_fwd(n_rep, one, tokens, par_one)
        second_desc, second_bufs, second_layout = describe(layers_parts, spd)
        two = (blocks, second_desc, second_bufs, second_layout)
        got = to_owner(jnp.concatenate([cls.reshape(seg_dev, D), cot_first], axis=1))
        reply, states, lt_two, r_two, grad_pos, pg_two = second_layer(
            n_rep, two, doc, got, position, par_two
        )
        arrays = second_grad(ctx, where, info, lt_two, r_two, ())
        back = lax.all_to_all(
            reply.reshape(n_seq, seg_dev, 2 * D), "seq", split_axis=0, concat_axis=0, tiled=True
        )
        box = {}

        def backward(after):
            box["bwd"] = first_bwd(n_rep, one, cotangent, back, out_one, par_one, kept, after)
            pg_one = box["bwd"][3]
            local = jnp.concatenate([pg_one[0], pg_two[0], grad_pos.reshape(-1)]).reshape(2, -1, 128)
            box["sum"] = lax.dynamic_index_in_dim(local, my_seq % 2, 0, False)
            box["got"] = swap(lax.dynamic_index_in_dim(local, 1 - my_seq % 2, 0, False), "seq", 1)
            return (box["bwd"][1],)

        routes = [("seq", 2 << b) for b in range((n_seq // 2).bit_length() - 1)][::-1]
        routes += [("rep", 1 << b) for b in range(n_rep.bit_length() - 1)][::-1]

        def small_hop(axis, bit):
            def run(after):
                box["sum"] = add(box["sum"], box["got"], after)
                box["got"] = swap(box["sum"], axis, bit)
                return (box["sum"],)

            return run

        per = 2
        n_done = per if ahead else 0

        def late_products(after):
            some, done = arrays[: len(arrays) - n_done], arrays[len(arrays) - n_done :]
            sub = (spd, n_target, chunk_spans[: len(some) // per])
            made = first_grad(sub, where, info, lt_one, box["bwd"][1], some, after)
            box["all"] = list(made) + list(done)
            return (made[1],)

        def chunk(c):
            return lambda: box["all"][per * c : per * c + per]

        chunks = [(first, m, chunk(c)) for c, (first, m) in enumerate(chunk_spans)]
        if ahead:
            early = chunks[-1][:2] + (lambda: arrays[-per:],)
            chunks = [early, None] + chunks[:-1]
            ready, idle = {}, {1: [backward], 2: [late_products]}
        else:
            ready, idle = {0: [backward, late_products]}, {}
        n = len(chunks)
        for at, route in zip([3, 5, 7, 8, 9, 10, 11], routes):
            idle.setdefault(at, []).append(small_hop(*route))
        results, after = reduce_pipeline(
            (order, info, spd, n_rep), chunks, ready, idle, stats, (arrays[0],)
        )
        core = my_seq % 2
        mine = add(box["sum"], box["got"], after)
        theirs = swap(mine, "seq", 1)
        small_grads = jnp.where(
            core == 0, jnp.concatenate([mine, theirs]), jnp.concatenate([theirs, mine])
        ).reshape(-1)
        new_small = small_step(small_params, small_grads, ())
        hidden_out, unused, input_grad, unused = box["bwd"]
        return (hidden_out, input_grad, states[None], *results, small_grads, new_small)

    if not line:
        return layers(False)
    counts = jnp.sum((slot_block.reshape(n_seq, spd) < PER_LAYER).astype(jnp.int32), axis=1)
    return lax.cond(jnp.all(counts <= spans[0][1]), lambda: layers(True), lambda: layers(False))


def solution(mesh):
    in_specs = (
        P(("rep", "seq"), None),
        P(("rep", "seq"), None),
        P("rep", None),
        P("rep", None),
        P(),
        P(),
        P("seq", None, None),
        P("seq", None, None),
        P("seq", None, None),
        P("seq", None, None),
        P("seq", None, None),
    )
    out_specs = (
        P(("rep", "seq"), None),
        P(("rep", "seq"), None),
        P(("rep", "seq"), None, None),
        P("seq", None, None),
        P("seq", None, None),
        P("seq", None, None),
        P("seq", None, None),
        P(),
        P(),
    )
    return jax.shard_map(shards, mesh=mesh, in_specs=in_specs, out_specs=out_specs, check_vma=False)
```
